256 devices in a mesh: lon: 16 (over y_lo, x, core), lat: 16 (over y_hi, z).
Axes of the slice: x: 4, y: 4 (y_hi: 2, y_lo: 2; y = y_hi * 2 + y_lo), z: 8, core: 2. Of those that a mesh axis runs over, the one named last changes fastest.
Arguments:
- fields: bfloat16 [4, 96, 384, 192], P(None, 'lat', 'lon'), may hold values from -36 to 36
- gain_attn: float32 [192], replicated, may hold values from 0.1 to 1.9
- w_qkv: bfloat16 [192, 576], replicated, may hold values from -0.4375 to 0.4375
- bias: bfloat16 [16, 6, 144, 144], P('lat'), may hold values from -6 to 300
- w_proj: bfloat16 [192, 192], replicated, may hold values from -0.4375 to 0.4375
- gain_mlp: float32 [192], replicated, may hold values from 0.1 to 1.9
- w_up: bfloat16 [192, 768], replicated, may hold values from -0.4375 to 0.4375
- w_down: bfloat16 [768, 192], replicated, may hold values from -0.21875 to 0.21875
- cotangent: bfloat16 [4, 96, 384, 192], P(None, 'lat', 'lon'), may hold values from -6 to 6
Outputs:
- output: bfloat16 [4, 96, 384, 192], P(None, 'lat', 'lon')
- grad_fields: bfloat16 [4, 96, 384, 192], P(None, 'lat', 'lon')
- grad_qkv: float32 [192, 576], replicated
- grad_proj: float32 [192, 192], replicated
- grad_up: float32 [192, 768], replicated
- grad_down: float32 [768, 192], replicated
- grad_gain_attn: float32 [192], replicated
- grad_gain_mlp: float32 [192], replicated
The draws below stay inside these ranges and needn't reach their ends.
All inputs are finite; a program needn't handle non-finite values.
Results may differ from the reference program's by a relative error of at most 0.019.
Values may be sent and summed in bfloat16 or wider, within the bound.
A program may use at most 64 MiB of HBM per device.

```python
import math
import jax
import jax.numpy as jnp
from jax import lax

C = 192
HEADS = 6
FF = 768
WLEV = 2
WLAT = 6
WLON = 12
WTOK = 144
LEV = 4
NLAT = 96
NLON = 384
NLATWIN = 16
TOKENS = 147456


def draw_fields(key, part):
    key = jax.random.fold_in(key, 5)
    noise_key, row_key, col_key = jax.random.split(key, 3)
    field_shape = (LEV, NLAT, NLON, C)
    row_scale = 0.3 * jnp.exp(jax.random.uniform(row_key, (LEV, NLAT, NLON, 1), jnp.float32, 0.0, math.log(10.0)))
    col_scale = 0.3 * jnp.exp(jax.random.uniform(col_key, (C,), jnp.float32, 0.0, math.log(10.0)))
    noise = jnp.clip(jax.random.normal(noise_key, field_shape, jnp.float32), -4.0, 4.0)
    return (noise * row_scale * col_scale).astype(jnp.bfloat16)


def draw_bias(key, part):
    key = jax.random.fold_in(key, 11)
    bias_shape = (NLATWIN, HEADS, WTOK, WTOK)
    return jnp.clip(jax.random.normal(key, bias_shape, jnp.float32), -6.0, 6.0).astype(jnp.bfloat16)


def level_of(key, shape, cuts, low, largest):
    factor_of = 1.0
    for position, shards_of in cuts:
        steps = jax.random.uniform(jax.random.fold_in(jax.random.fold_in(key, 6), position), (shards_of,), jnp.float32, low / len(cuts), largest / len(cuts))
        factor_of = factor_of * jnp.repeat(jnp.exp(steps), shape[position] // shards_of).reshape((-1,) + (1,) * (len(shape) - 1 - position))
    return factor_of


def gaussian(own_key, shape, scale, bound, shards=(), kind=jnp.bfloat16):
    factor_of = level_of(own_key, shape, shards, -0.22, 0.18) if shards else 1.0
    entries = jax.random.normal(own_key, shape, jnp.float32) * scale * factor_of
    return jnp.minimum(jnp.maximum(entries, -bound), bound).astype(kind)


def setup_inputs(seed: int = 0) -> dict:
    keys = jax.random.split(jax.random.key(seed), 10)
    fields = draw_fields(jax.random.fold_in(keys[9], 71), 0)
    gain_attn = jnp.clip(1.0 + 0.18 * jax.random.normal(keys[1], (C,), jnp.float32), 0.1, 1.9)
    w_qkv = gaussian(keys[2], (C, 3 * C), C ** -0.5, 0.4375)
    bias = draw_bias(jax.random.fold_in(keys[9], 71), 0)
    w_proj = gaussian(keys[4], (C, C), C ** -0.5, 0.4375)
    gain_mlp = jnp.clip(1.0 + 0.18 * jax.random.normal(keys[5], (C,), jnp.float32), 0.1, 1.9)
    w_up = gaussian(keys[6], (C, FF), C ** -0.5, 0.4375)
    w_down = gaussian(keys[7], (FF, C), FF ** -0.5, 0.21875)
    cotangent = gaussian(keys[8], (LEV, NLAT, NLON, C), 1.0, 6.0, ((1, 16), (2, 16)))
    return dict(fields=fields, gain_attn=gain_attn, w_qkv=w_qkv, bias=bias, w_proj=w_proj, gain_mlp=gain_mlp, w_up=w_up, w_down=w_down, cotangent=cotangent)


NORM_EPS = 1e-05

def norm_rows(values, gain):
    center = values - lax.optimization_barrier(jnp.mean(values, axis=-1, keepdims=True))
    spread = lax.optimization_barrier(jnp.mean(center * center, axis=-1, keepdims=True))
    return center * lax.rsqrt(spread + NORM_EPS) * gain

def gelu_exact(values):
    return jax.nn.gelu(values, approximate=False)

def contract(left, right):
    return lax.dot_general(left, right, (((0,), (0,)), ((), ())), preferred_element_type=jnp.float32)

def split_windows(field_grid):
    levels, lat_rows, lon_cols, features = field_grid.shape
    tile_grid = field_grid.reshape(levels // WLEV, WLEV, lat_rows // WLAT, WLAT, lon_cols // WLON, WLON, features)
    tile_grid = tile_grid.transpose(2, 0, 4, 1, 3, 5, 6)
    return tile_grid.reshape(lat_rows // WLAT, levels // WLEV * (lon_cols // WLON), WLEV * WLAT * WLON, features)

def join_windows(tile_grid, levels, lon_cols):
    band_count = tile_grid.shape[0]
    features = tile_grid.shape[-1]
    field_grid = tile_grid.reshape(band_count, levels // WLEV, lon_cols // WLON, WLEV, WLAT, WLON, features)
    return field_grid.transpose(1, 3, 0, 4, 2, 5, 6).reshape(levels, band_count * WLAT, lon_cols, features)

def band_mask(is_last):
    lat_pos = jnp.arange(WTOK) // WLON % WLAT
    upper_half = lat_pos < WLAT // 2
    return jnp.logical_or(upper_half[:, None] == upper_half[None, :], jnp.logical_not(is_last))

def window_probs(windows, w_qkv, bias_band, is_last):
    window_count = windows.shape[0]
    features = windows.shape[-1]
    head_count = bias_band.shape[0]
    head_size = features // head_count
    qkv = jnp.dot(windows.reshape(-1, features), w_qkv, preferred_element_type=jnp.float32).astype(jnp.bfloat16)
    qkv = qkv.reshape(window_count, WTOK, 3, head_count, head_size)
    queries, key_rows, values = (qkv[:, :, 0], qkv[:, :, 1], qkv[:, :, 2])
    scores = jnp.einsum('nihd,njhd->nhij', queries.astype(jnp.float32), key_rows.astype(jnp.float32))
    scores = scores * head_size ** (-0.5) + bias_band.astype(jnp.float32)[None]
    scores = jnp.where(band_mask(is_last)[None, None], scores, -1e+30)
    row_max = lax.optimization_barrier(jnp.max(scores, axis=-1, keepdims=True))
    exponent = jnp.exp(scores - row_max)
    probs = exponent / lax.optimization_barrier(jnp.sum(exponent, axis=-1, keepdims=True))
    return (queries, key_rows, values, probs)

def attend(windows, w_qkv, bias_band, is_last):
    queries, key_rows, values, probs = window_probs(windows, w_qkv, bias_band, is_last)
    weights = lax.optimization_barrier(probs.astype(jnp.bfloat16)).astype(jnp.float32)
    mixed = jnp.einsum('nhij,njhd->nihd', weights, values.astype(jnp.float32)).astype(jnp.bfloat16)
    return mixed.reshape(windows.shape)

def attend_back(windows, upstream, w_qkv, bias_band, is_last):
    queries, key_rows, values, probs = window_probs(windows, w_qkv, bias_band, is_last)
    window_count, tokens, head_count, head_size = queries.shape
    grad_out = upstream.reshape(window_count, tokens, head_count, head_size).astype(jnp.float32)
    weights = lax.optimization_barrier(probs.astype(jnp.bfloat16)).astype(jnp.float32)
    grad_values = jnp.einsum('nhij,nihd->njhd', weights, grad_out).astype(jnp.bfloat16)
    grad_probs = jnp.einsum('nihd,njhd->nhij', grad_out, values.astype(jnp.float32))
    inner = lax.optimization_barrier(jnp.sum(probs * grad_probs, axis=-1, keepdims=True))
    grad_scores = (probs * (grad_probs - inner) * head_size ** (-0.5)).astype(jnp.bfloat16)
    grad_scores = lax.optimization_barrier(grad_scores).astype(jnp.float32)
    grad_query = jnp.einsum('nhij,njhd->nihd', grad_scores, key_rows.astype(jnp.float32)).astype(jnp.bfloat16)
    grad_key = jnp.einsum('nhij,nihd->njhd', grad_scores, queries.astype(jnp.float32)).astype(jnp.bfloat16)
    stacked = jnp.stack([grad_query, grad_key, grad_values], axis=2)
    return stacked.reshape(window_count, tokens, 3 * head_count * head_size)

def reference(fields, gain_attn, w_qkv, bias, w_proj, gain_mlp, w_up, w_down, cotangent):
    levels, lat_rows, lon_cols, features = fields.shape
    factor = float(TOKENS) ** (-0.5)
    half_lat = WLAT // 2
    half_lon = WLON // 2
    flat_fields = fields.reshape(-1, features)
    normed = norm_rows(flat_fields.astype(jnp.float32), gain_attn).astype(jnp.bfloat16).reshape(fields.shape)
    rolled = jnp.roll(normed, (-half_lat, -half_lon), axis=(1, 2))
    windows = split_windows(rolled)
    band_count = windows.shape[0]
    band_ids = jnp.arange(band_count, dtype=jnp.int32)
    mixed = lax.map(lambda inputs: attend(inputs[0], w_qkv, inputs[1], inputs[2] == band_count - 1), (windows, bias, band_ids))
    attn_out = jnp.roll(join_windows(mixed, levels, lon_cols), (half_lat, half_lon), axis=(1, 2))
    flat_attn = attn_out.reshape(-1, features)
    hidden_state = (flat_fields.astype(jnp.float32) + jnp.dot(flat_attn, w_proj, preferred_element_type=jnp.float32)).astype(jnp.bfloat16)
    normed_mlp = norm_rows(hidden_state.astype(jnp.float32), gain_mlp).astype(jnp.bfloat16)
    pre_act = jnp.dot(normed_mlp, w_up, preferred_element_type=jnp.float32)
    active = gelu_exact(pre_act).astype(jnp.bfloat16)
    output = (hidden_state.astype(jnp.float32) + jnp.dot(active, w_down, preferred_element_type=jnp.float32)).astype(jnp.bfloat16)
    flat_grad = cotangent.reshape(-1, features)
    grad_down = contract(active, flat_grad)
    grad_active = lax.dot_general(flat_grad, w_down, (((1,), (1,)), ((), ())), preferred_element_type=jnp.float32)
    grad_pre = jax.vjp(gelu_exact, pre_act)[1](grad_active)[0].astype(jnp.bfloat16)
    grad_up = contract(normed_mlp, grad_pre)
    grad_normed = lax.dot_general(grad_pre, w_up, (((1,), (1,)), ((), ())), preferred_element_type=jnp.float32)
    back_mlp = jax.vjp(norm_rows, hidden_state.astype(jnp.float32), gain_mlp)[1]
    grad_h_norm, grad_gain_mlp = back_mlp(grad_normed)
    grad_hidden = (flat_grad.astype(jnp.float32) + grad_h_norm).astype(jnp.bfloat16)
    grad_proj = contract(flat_attn, grad_hidden)
    grad_attn = lax.dot_general(grad_hidden, w_proj, (((1,), (1,)), ((), ())), preferred_element_type=jnp.float32)
    grad_attn = grad_attn.astype(jnp.bfloat16).reshape(fields.shape)
    grad_windows = split_windows(jnp.roll(grad_attn, (-half_lat, -half_lon), axis=(1, 2)))
    grad_qkv_windows = lax.map(lambda inputs: attend_back(inputs[0], inputs[1], w_qkv, inputs[2], inputs[3] == band_count - 1), (windows, grad_windows, bias, band_ids))
    flat_qkv_grad = grad_qkv_windows.reshape(-1, 3 * features)
    grad_qkv = contract(windows.reshape(-1, features), flat_qkv_grad)
    grad_rolled = lax.dot_general(flat_qkv_grad, w_qkv, (((1,), (1,)), ((), ())), preferred_element_type=jnp.float32)
    grad_rolled = grad_rolled.astype(jnp.bfloat16).reshape(windows.shape)
    grad_unrolled = jnp.roll(join_windows(grad_rolled, levels, lon_cols), (half_lat, half_lon), axis=(1, 2))
    back_attn = jax.vjp(norm_rows, flat_fields.astype(jnp.float32), gain_attn)[1]
    grad_x_norm, grad_gain_attn = back_attn(grad_unrolled.reshape(-1, features).astype(jnp.float32))
    grad_fields = (grad_hidden.astype(jnp.float32) + grad_x_norm).astype(jnp.bfloat16).reshape(fields.shape)
    return (output.reshape(fields.shape), grad_fields, grad_qkv * factor, grad_proj * factor, grad_up * factor, grad_down * factor, grad_gain_attn * factor, grad_gain_mlp * factor)
```

```python
import functools

import jax
import jax.numpy as jnp
import numpy as np
from jax import lax
from jax.experimental import pallas as pl
from jax.experimental.pallas import tpu as pltpu
from jax.sharding import PartitionSpec as P

WLAT = 6
WLON = 12
WTOK = 144
HEADS = 6
HEAD = 32
LEV = 4
C = 192
FF = 768
TOK = 576
NORM_EPS = 1e-05
MASKED = -1e30

PIECES = ((0, 64), (64, 64), (128, 32), (160, 32))

FLAT = 4096
GAIN_ROW = 3456

F32 = jnp.float32
BF16 = jnp.bfloat16
MESH = pl.DeviceIdType.MESH
VMEM = pl.BlockSpec(memory_space=pltpu.VMEM)


def piece_row(row, col):
    if row >= 3 and col >= 6:
        return (row - 3) * 18 + col - 6
    if col >= 6:
        return 64 + row * 18 + col - 6
    if row >= 3:
        return 128 + (row - 3) * 6 + col
    return 160 + row * 6 + col


def one_hot_tables():
    pack = np.zeros((192, 144), np.float32)
    place = np.zeros((144, 192), np.float32)
    for row in range(6):
        for col in range(24):
            pack[piece_row(row, col), row * 24 + col] = 1.0
            at = (col // WLON) * 72 + row * WLON + col % WLON
            place[at, piece_row((row + 3) % 6, (col + 6) % 24)] = 1.0
    return pack, place


def nn(left, right):
    return lax.dot_general(left, right, (((1,), (0,)), ((), ())), preferred_element_type=F32)


def nt(left, right):
    return lax.dot_general(left, right, (((1,), (1,)), ((), ())), preferred_element_type=F32)


def tn(left, right):
    return lax.dot_general(left, right, (((0,), (0,)), ((), ())), preferred_element_type=F32)


def row_mean(values):
    return jnp.sum(values, axis=-1, keepdims=True) * (1.0 / C)


def normalize(values):
    center = values - row_mean(values)
    inv = lax.rsqrt(row_mean(center * center) + NORM_EPS)
    return center * inv, inv


def norm_back(unit, inv, gain, upstream):
    scaled = upstream * gain
    grad = inv * (scaled - row_mean(scaled) - unit * row_mean(scaled * unit))
    return grad, jnp.sum(upstream * unit, axis=0, keepdims=True)


def head_masks():
    head_of = lax.broadcasted_iota(jnp.int32, (1, C), 1) // HEAD
    return [jnp.where(head_of == h, 1.0, 0.0).astype(BF16) for h in range(HEADS)]


def block_kernel(
    x_ref, ct_ref, bias_ref, ga_ref, wqkv_ref, wproj_ref, gm_ref, wup_ref, wdown_ref,
    out_ref, gx_ref, flat_ref,
    bias32, probs, normed_s, qkv_s, mixed_s, hid_grad_s, nm_s, act_s, gpre_s, gqkv_s, gattn_s,
):
    scale = HEAD ** (-0.5)
    masks = head_masks()
    is_last = lax.axis_index("lat") == lax.axis_size("lat") - 1
    row_half = (lax.broadcasted_iota(jnp.int32, (WTOK, WTOK), 0) // WLON) % WLAT < WLAT // 2
    col_half = (lax.broadcasted_iota(jnp.int32, (WTOK, WTOK), 1) // WLON) % WLAT < WLAT // 2
    cut = jnp.logical_and(row_half != col_half, is_last)
    penalty = jnp.where(cut, MASKED, 0.0)
    for h in range(HEADS):
        rows = slice(h * WTOK, (h + 1) * WTOK)
        bias32[rows, :] = bias_ref[rows, :].astype(F32) + penalty

    ga = ga_ref[...]
    gm = gm_ref[...]
    grad_gain_mlp = jnp.zeros((1, C), F32)
    for n in range(4):
        rows = slice(n * WTOK, (n + 1) * WTOK)
        x = x_ref[rows, :].astype(F32)
        unit, _ = normalize(x)
        normed = (unit * ga).astype(BF16)
        normed_s[rows, :] = normed
        qkv = nn(normed, wqkv_ref[...]).astype(BF16)
        qkv_s[rows, :] = qkv
        q = qkv[:, :C]
        k = qkv[:, C:2 * C]
        v = qkv[:, 2 * C:]
        mixed = jnp.zeros((WTOK, C), F32)
        for h in range(HEADS):
            s = nt(q * masks[h], k) * scale + bias32[h * WTOK:(h + 1) * WTOK, :]
            e = jnp.exp(s - jnp.max(s, axis=-1, keepdims=True))
            p = e * (1.0 / jnp.sum(e, axis=-1, keepdims=True))
            probs[n * HEADS + h] = p
            mixed = mixed + nn(p.astype(BF16), v * masks[h])
        mixed = mixed.astype(BF16)
        mixed_s[rows, :] = mixed
        hidden = (x + nn(mixed, wproj_ref[...])).astype(BF16).astype(F32)
        unit, inv = normalize(hidden)
        nm = (unit * gm).astype(BF16)
        nm_s[rows, :] = nm
        ct = ct_ref[rows, :]
        down = jnp.zeros((WTOK, C), F32)
        grad_nm = jnp.zeros((WTOK, C), F32)
        for f in range(3):
            cols = slice(f * 256, (f + 1) * 256)
            z = nn(nm, wup_ref[:, cols])
            phi = 0.5 * (1.0 + lax.erf(z * (0.5 ** 0.5)))
            act = (z * phi).astype(BF16)
            act_s[rows, cols] = act
            slope = phi + z * (jnp.exp(-0.5 * z * z) * ((2 * np.pi) ** -0.5))
            gpre = (nn(ct, wdown_ref[:, cols]) * slope).astype(BF16)
            gpre_s[rows, cols] = gpre
            down = down + nt(act, wdown_ref[:, cols])
            grad_nm = grad_nm + nt(gpre, wup_ref[:, cols])
        out_ref[rows, :] = (hidden + down).astype(BF16)
        grad_h, gain_term = norm_back(unit, inv, gm, grad_nm)
        grad_gain_mlp = grad_gain_mlp + gain_term
        grad_hidden = (ct.astype(F32) + grad_h).astype(BF16)
        hid_grad_s[rows, :] = grad_hidden
        gattn_s[rows, :] = nt(grad_hidden, wproj_ref[...]).astype(BF16)

    def store_blocks(base, values):
        for t in range(values.shape[1] // 128):
            flat_ref[base + t * C:base + (t + 1) * C, :] = values[:, t * 128:(t + 1) * 128].astype(BF16)

    store_blocks(6 * C, tn(nm_s[...], gpre_s[...]))
    store_blocks(12 * C, tn(ct_ref[...], act_s[...]))

    grad_gain_attn = jnp.zeros((1, C), F32)
    for n in range(4):
        rows = slice(n * WTOK, (n + 1) * WTOK)
        qkv = qkv_s[rows, :]
        q = qkv[:, :C]
        k = qkv[:, C:2 * C]
        v = qkv[:, 2 * C:]
        up = gattn_s[rows, :]
        gq = jnp.zeros((WTOK, C), F32)
        gk = jnp.zeros((WTOK, C), F32)
        gv = jnp.zeros((WTOK, C), F32)
        for h in range(HEADS):
            p = probs[n * HEADS + h]
            up_h = up * masks[h]
            gp = nt(up_h, v)
            inner = jnp.sum(p * gp, axis=-1, keepdims=True)
            gs = (p * (gp - inner) * scale).astype(BF16)
            gv = gv + tn(p.astype(BF16), up_h)
            gq = gq + nn(gs, k * masks[h])
            gk = gk + tn(gs, q * masks[h])
        gqkv = jnp.concatenate([gq, gk, gv], axis=1).astype(BF16)
        gqkv_s[rows, :] = gqkv
        grad_rolled = nt(gqkv, wqkv_ref[...]).astype(BF16).astype(F32)
        unit, inv = normalize(x_ref[rows, :].astype(F32))
        grad_x, gain_term = norm_back(unit, inv, ga, grad_rolled)
        grad_gain_attn = grad_gain_attn + gain_term
        gx_ref[rows, :] = (hid_grad_s[rows, :].astype(F32) + grad_x).astype(BF16)

    grad_qkv = tn(normed_s[...], gqkv_s[...])
    grad_proj = tn(mixed_s[...], hid_grad_s[...])
    store_blocks(0, jnp.concatenate([grad_qkv, grad_proj], axis=1))
    row = lax.broadcasted_iota(jnp.int32, (16, 128), 0)
    pad = jnp.zeros((1, 64), F32)
    gains = jnp.zeros((16, 128), F32)
    for g, value in enumerate((grad_gain_attn, grad_gain_mlp)):
        tail = jnp.concatenate([value[:, 128:], pad], axis=1)
        gains = jnp.where(row == 2 * g, value[:, :128], gains)
        gains = jnp.where(row == 2 * g + 1, tail, gains)
    flat_ref[GAIN_ROW:GAIN_ROW + 16, :] = gains.astype(BF16)
    flat_ref[GAIN_ROW + 16:, :] = jnp.zeros((FLAT - GAIN_ROW - 16, 128), BF16)


def block_call(x, ct, bias, gain_attn, w_qkv, w_proj, gain_mlp, w_up, w_down):
    shape = jax.ShapeDtypeStruct
    return pl.pallas_call(
        block_kernel,
        out_shape=(
            shape((TOK, C), BF16),
            shape((TOK, C), BF16),
            shape((FLAT, 128), BF16),
        ),
        in_specs=[VMEM] * 9,
        out_specs=(VMEM,) * 3,
        scratch_shapes=[
            pltpu.VMEM((HEADS * WTOK, WTOK), F32),
            pltpu.VMEM((4 * HEADS, WTOK, WTOK), F32),
            pltpu.VMEM((TOK, C), BF16),
            pltpu.VMEM((TOK, 3 * C), BF16),
            pltpu.VMEM((TOK, C), BF16),
            pltpu.VMEM((TOK, C), BF16),
            pltpu.VMEM((TOK, C), BF16),
            pltpu.VMEM((TOK, FF), BF16),
            pltpu.VMEM((TOK, FF), BF16),
            pltpu.VMEM((TOK, 3 * C), BF16),
            pltpu.VMEM((TOK, C), BF16),
        ],
        compiler_params=pltpu.CompilerParams(vmem_limit_bytes=48 * 2**20),
        name="window_block",
    )(x, ct, bias, gain_attn, w_qkv, w_proj, gain_mlp, w_up, w_down)


def remote(src, dst, send_sem, recv_sem, lon, lat):
    return pltpu.make_async_remote_copy(
        src_ref=src, dst_ref=dst, send_sem=send_sem, recv_sem=recv_sem,
        device_id=(lon, lat), device_id_type=MESH,
    )


def ring(index, step, size):
    return lax.rem(index + step + size, size)


def greet(devices):
    barrier = pltpu.get_barrier_semaphore()
    for device in devices:
        pl.semaphore_signal(barrier, inc=1, device_id=device, device_id_type=MESH)
    pl.semaphore_wait(barrier, len(devices))


def halo_neighbours(lon, lat):
    out = []
    for step in (1, -1):
        out.append((ring(lon, step, 16), lat))
        out.append((lon, ring(lat, step, 16)))
        out.append((ring(lon, step, 16), ring(lat, step, 16)))
    return out


def halo_copies(packed, landed, send_sem, recv_sem, step):
    lon, lat = lax.axis_index("lon"), lax.axis_index("lat")
    far_lon, far_lat = ring(lon, step, 16), ring(lat, step, 16)
    targets = ((lon, far_lat), (far_lon, lat), (far_lon, far_lat))
    copies = []
    for i, (start, size) in enumerate(PIECES[1:]):
        copies.append(remote(
            packed.at[:, pl.ds(start, size), :], landed.at[:, pl.ds(start - 64, size), :],
            send_sem.at[i], recv_sem.at[i], *targets[i],
        ))
    return copies


def halo_in_kernel(
    x_ref, ct_ref, pack_ref, place_ref, xw_ref, ctw_ref, packed, landed, send_sem, recv_sem
):
    lon, lat = lax.axis_index("lon"), lax.axis_index("lat")
    greet(halo_neighbours(lon, lat))
    copies = []
    for a, ref in enumerate((x_ref, ct_ref)):
        for level in range(LEV):
            rows = slice(level * WTOK, (level + 1) * WTOK)
            packed[a, level] = nn(pack_ref[...], ref[rows, :]).astype(BF16)
        mine = halo_copies(packed.at[a], landed.at[a], send_sem.at[a], recv_sem.at[a], -1)
        for copy in mine:
            copy.start()
        copies.append(mine)
    for a, ref in enumerate((xw_ref, ctw_ref)):
        for copy in copies[a]:
            copy.wait()
        for pair in range(LEV // 2):
            grids = []
            for level in (2 * pair, 2 * pair + 1):
                grids.append(
                    nn(place_ref[:, :64], packed[a, level, :64, :])
                    + nn(place_ref[:, 64:], landed[a, level])
                )
            for w in range(2):
                tokens = jnp.concatenate([grid[w * 72:(w + 1) * 72] for grid in grids], axis=0)
                start = (pair * 2 + w) * WTOK
                ref[start:start + WTOK, :] = tokens.astype(BF16)


def halo_in(x, ct, pack, place):
    shape = jax.ShapeDtypeStruct((TOK, C), BF16)
    return pl.pallas_call(
        halo_in_kernel,
        out_shape=(shape, shape),
        in_specs=[VMEM] * 4,
        out_specs=(VMEM, VMEM),
        scratch_shapes=[
            pltpu.VMEM((2, LEV, 192, C), BF16),
            pltpu.VMEM((2, LEV, 128, C), BF16),
            pltpu.SemaphoreType.DMA((2, 3)),
            pltpu.SemaphoreType.DMA((2, 3)),
        ],
        compiler_params=pltpu.CompilerParams(
            collective_id=0, has_side_effects=True, vmem_limit_bytes=24 * 2**20
        ),
        name="halo_in",
    )(x, ct, pack, place)


def pack_back(ref, place_ref, packed):
    for pair in range(LEV // 2):
        windows = []
        for w in range(2):
            start = (pair * 2 + w) * WTOK
            windows.append(ref[start:start + WTOK, :].astype(F32))
        for half in range(2):
            grid = jnp.concatenate([w[half * 72:(half + 1) * 72] for w in windows], axis=0)
            packed[2 * pair + half] = tn(place_ref[...], grid.astype(BF16)).astype(BF16)


def unpack_back(packed, landed, pack_ref, ref):
    for level in range(LEV):
        grid = tn(pack_ref[:64, :], packed[level, :64, :]) + tn(pack_ref[64:, :], landed[level])
        ref[level * WTOK:(level + 1) * WTOK, :] = grid.astype(BF16)


def reduce_kernel(
    out_ref, gx_ref, flat_ref, pack_ref, place_ref,
    out_grid, gx_grid, qkv_ref, proj_ref, up_ref, down_ref, gain_ref,
    packed, landed, halo_send, halo_recv,
    core_in, lon_out, lon_in, lat_out, lat_in, mine_out, full,
    core_send, core_recv, lon_send, lon_recv, lat_send, lat_recv,
    back_send, back_recv, lonb_send, lonb_recv, coreb_send, coreb_recv,
):
    lon, lat = lax.axis_index("lon"), lax.axis_index("lat")
    core, group = lax.rem(lon, 2), lon // 2
    partner = lon + 1 - 2 * core
    half = core * 2048
    devices = halo_neighbours(lon, lat) + [(partner, lat)]
    devices += [(ring(group, k, 8) * 2 + core, lat) for k in range(1, 8)]
    devices += [(lon, ring(lat, k, 16)) for k in range(1, 16)]
    greet(devices)

    def chunk(start, size):
        return pl.ds(pl.multiple_of(start, 16), size)

    started = []

    def start(copy):
        copy.start()
        started.append(copy)
        return copy

    core_copies = []
    for k in range(8):
        rows = chunk(2048 - half + ring(group, k + 1, 8) * 256, 256)
        core_copies.append(start(remote(
            flat_ref.at[rows], core_in.at[k], core_send.at[k], core_recv.at[k], partner, lat
        )))
    halos = []
    for a, ref in enumerate((out_ref, gx_ref)):
        pack_back(ref, place_ref, packed.at[a])
        mine = halo_copies(packed.at[a], landed.at[a], halo_send.at[a], halo_recv.at[a], 1)
        halos.append([start(copy) for copy in mine])
    lon_copies = []
    total = None
    for k in range(8):
        core_copies[k].wait_recv()
        peer = ring(group, k + 1, 8)
        summed = flat_ref[chunk(half + peer * 256, 256), :].astype(F32) + core_in[k].astype(F32)
        if k < 7:
            lon_out[k] = summed.astype(BF16)
            lon_copies.append(start(remote(
                lon_out.at[k], lon_in.at[k], lon_send.at[k], lon_recv.at[k], peer * 2 + core, lat
            )))
        else:
            total = summed
    for k in range(7):
        lon_copies[k].wait_recv()
        total = total + lon_in[k].astype(F32)
    lat_out[...] = total.astype(BF16)
    lat_copies = []
    for k in range(15):
        peer = ring(lat, k + 1, 16)
        lat_copies.append(start(remote(
            lat_out.at[chunk(peer * 16, 16)], lat_in.at[k], lat_send.at[k], lat_recv.at[k], lon, peer
        )))
    total = lat_out[chunk(lat * 16, 16), :].astype(F32)
    for k in range(15):
        lat_copies[k].wait_recv()
        total = total + lat_in[k].astype(F32)
    mine_out[...] = total.astype(BF16)
    base = half + group * 256
    own = chunk(base + lat * 16, 16)
    full[own, :] = mine_out[...]
    back = []
    for k in range(15):
        back.append(start(remote(
            mine_out, full.at[own], back_send.at[k], back_recv.at[k], lon, ring(lat, k + 1, 16)
        )))
    for a, ref in enumerate((out_grid, gx_grid)):
        for copy in halos[a]:
            copy.wait_recv()
        unpack_back(packed.at[a], landed.at[a], pack_ref, ref)
    for copy in back:
        copy.wait_recv()
    rows = chunk(base, 256)
    lon_back = []
    for k in range(7):
        peer = ring(group, k + 1, 8)
        lon_back.append(start(remote(
            full.at[rows], full.at[rows], lonb_send.at[k], lonb_recv.at[k], peer * 2 + core, lat
        )))
    core_back = []
    for k in range(8):
        if k > 0:
            lon_back[k - 1].wait_recv()
        rows = chunk(half + ring(group, -k, 8) * 256, 256)
        core_back.append(start(remote(
            full.at[rows], full.at[rows], coreb_send.at[k], coreb_recv.at[k], partner, lat
        )))
    for copy in core_back:
        copy.wait_recv()
    for copy in started:
        copy.wait_send()

    factor = 1.0 / 384.0

    def block(t):
        return full[t * C:(t + 1) * C, :].astype(F32) * factor

    both = jnp.concatenate([block(t) for t in range(6)], axis=1)
    qkv_ref[...] = both[:, :3 * C]
    proj_ref[...] = both[:, 3 * C:]
    for t in range(6):
        up_ref[:, t * 128:(t + 1) * 128] = block(6 + t)
        down_ref[:, t * 128:(t + 1) * 128] = block(12 + t)
    gains = full[GAIN_ROW:GAIN_ROW + 16, :].astype(F32) * factor
    for g in range(2):
        gain_ref[g:g + 1, :] = jnp.concatenate(
            [gains[2 * g:2 * g + 1], gains[2 * g + 1:2 * g + 2, :64]], axis=1
        )


def reduce_call(out, gx, flat, pack, place):
    shape = jax.ShapeDtypeStruct
    sem = pltpu.SemaphoreType.DMA
    return pl.pallas_call(
        reduce_kernel,
        out_shape=(
            shape((TOK, C), BF16),
            shape((TOK, C), BF16),
            shape((C, 3 * C), F32),
            shape((C, C), F32),
            shape((C, FF), F32),
            shape((C, FF), F32),
            shape((2, C), F32),
        ),
        in_specs=[VMEM] * 5,
        out_specs=(VMEM,) * 7,
        scratch_shapes=[
            pltpu.VMEM((2, LEV, 192, C), BF16),
            pltpu.VMEM((2, LEV, 128, C), BF16),
            sem((2, 3)), sem((2, 3)),
            pltpu.VMEM((8, 256, 128), BF16),
            pltpu.VMEM((7, 256, 128), BF16),
            pltpu.VMEM((7, 256, 128), BF16),
            pltpu.VMEM((256, 128), BF16),
            pltpu.VMEM((15, 16, 128), BF16),
            pltpu.VMEM((16, 128), BF16),
            pltpu.VMEM((FLAT, 128), BF16),
            sem((8,)), sem((8,)), sem((7,)), sem((7,)), sem((15,)), sem((15,)),
            sem((15,)), sem((15,)), sem((7,)), sem((7,)), sem((8,)), sem((8,)),
        ],
        compiler_params=pltpu.CompilerParams(
            collective_id=1, has_side_effects=True, vmem_limit_bytes=32 * 2**20
        ),
        name="reduce_back",
    )(out, gx, flat, pack, place)


def body(fields, gain_attn, w_qkv, bias, w_proj, gain_mlp, w_up, w_down, cotangent):
    pack, place = (jnp.asarray(table, BF16) for table in one_hot_tables())
    x, ct = halo_in(fields.reshape(TOK, C), cotangent.reshape(TOK, C), pack, place)
    out, gx, flat = block_call(
        x, ct, bias.reshape(HEADS * WTOK, WTOK), gain_attn.reshape(1, C), w_qkv, w_proj,
        gain_mlp.reshape(1, C), w_up, w_down.T,
    )
    out, gx, qkv, proj, up, down, gains = reduce_call(out, gx, flat, pack, place)
    return (
        out.reshape(fields.shape), gx.reshape(fields.shape), qkv, proj, up, down.T, gains[0], gains[1]
    )


def solution(mesh):
    grid = P(None, "lat", "lon", None)
    in_specs = (grid, P(), P(), P("lat", None, None, None), P(), P(), P(), P(), grid)
    out_specs = (grid, grid, P(), P(), P(), P(), P(), P())
    return jax.shard_map(body, mesh=mesh, in_specs=in_specs, out_specs=out_specs, check_vma=False)
```

```python
import jax
import jax.numpy as jnp
from jax import lax
from jax.experimental import pallas as pl
from jax.experimental.pallas import tpu as pltpu
from jax.sharding import PartitionSpec as P

WLAT = 6
WLON = 12
WTOK = 144
HEADS = 6
HEAD = 32
LEV = 4
C = 192
FF = 768
TOK = 576
NORM_EPS = 1e-05
MASKED = -1e30
FACTOR = 1.0 / 384.0

PIECES = ((0, 64), (64, 64), (128, 32), (160, 32))

CHUNK = (80, 48)
ROWS = (32 * 80, 32 * 48)
GAIN_ROW = 6 * C
PLANE = [(dy, dx) for dy in range(4) for dx in range(4) if (dy, dx) != (0, 0)]

F32 = jnp.float32
BF16 = jnp.bfloat16
MESH = pl.DeviceIdType.MESH
VMEM = pl.BlockSpec(memory_space=pltpu.VMEM)
ANY = pl.BlockSpec(memory_space=pl.ANY)


def nn(left, right):
    return lax.dot_general(left, right, (((1,), (0,)), ((), ())), preferred_element_type=F32)


def nt(left, right):
    return lax.dot_general(left, right, (((1,), (1,)), ((), ())), preferred_element_type=F32)


def tn(left, right):
    return lax.dot_general(left, right, (((0,), (0,)), ((), ())), preferred_element_type=F32)


def row_mean(values):
    return jnp.sum(values, axis=-1, keepdims=True) * (1.0 / C)


def normalize(values):
    center = values - row_mean(values)
    inv = lax.rsqrt(row_mean(center * center) + NORM_EPS)
    return center * inv, inv


def norm_back(unit, inv, gain, upstream):
    scaled = upstream * gain
    grad = inv * (scaled - row_mean(scaled) - unit * row_mean(scaled * unit))
    return grad, jnp.sum(upstream * unit, axis=0, keepdims=True)


def head_masks():
    head_of = lax.broadcasted_iota(jnp.int32, (1, C), 1) // HEAD
    return [jnp.where(head_of == h, 1.0, 0.0).astype(BF16) for h in range(HEADS)]


def piece_row(row, col):
    stay_row = row >= 3
    stay_col = col >= 6
    left = jnp.where(stay_row, 128 + (row - 3) * 6 + col, 160 + row * 6 + col)
    right = jnp.where(stay_row, (row - 3) * 18 + col - 6, 64 + row * 18 + col - 6)
    return jnp.where(stay_col, right, left)


def pack_rows(token):
    return piece_row(token // 24, token % 24)


def place_rows(token):
    window = token // 72
    row = (token % 72) // WLON
    col = token % WLON + window * WLON
    return piece_row((row + 3) % 6, (col + 6) % 24)


def table(rows_of):
    token = lax.broadcasted_iota(jnp.int32, (1, WTOK), 1)
    piece = lax.broadcasted_iota(jnp.int32, (192, WTOK), 0)
    return jnp.where(piece == rows_of(token), 1.0, 0.0).astype(BF16)


def table_t(rows_of):
    token = lax.broadcasted_iota(jnp.int32, (WTOK, 1), 0)
    piece = lax.broadcasted_iota(jnp.int32, (WTOK, 192), 1)
    return jnp.where(piece == rows_of(token), 1.0, 0.0).astype(BF16)


def remote(src, dst, send_sem, recv_sem, device):
    return pltpu.make_async_remote_copy(
        src_ref=src, dst_ref=dst, send_sem=send_sem, recv_sem=recv_sem,
        device_id=device, device_id_type=MESH,
    )


def ring(index, step, size):
    return lax.rem(index + step + size, size)


def chunk(start, size):
    return pl.ds(pl.multiple_of(start, 16), size)


class Place:
    def __init__(self):
        self.lon, self.lat = lax.axis_index("lon"), lax.axis_index("lat")
        self.core = lax.rem(self.lon, 2)
        self.x = lax.rem(self.lon // 2, 4)
        self.y = self.lat // 8 * 2 + self.lon // 8
        self.z = lax.rem(self.lat, 8)

    def device(self, y, x, z, core):
        return ((lax.rem(y, 2) * 4 + x) * 2 + core, y // 2 * 8 + z)

    def other_core(self):
        return self.device(self.y, self.x, self.z, 1 - self.core)

    def plane_spot(self, dy, dx):
        return ring(self.y, dy, 4), ring(self.x, dx, 4)

    def plane_peer(self, dy, dx):
        y, x = self.plane_spot(dy, dx)
        return self.device(y, x, self.z, self.core)

    def z_peer(self, dz):
        return self.device(self.y, self.x, ring(self.z, dz, 8), self.core)

    def halo_targets(self, step):
        lon, lat = ring(self.lon, step, 16), ring(self.lat, step, 16)
        return (self.lon, lat), (lon, self.lat), (lon, lat)

    def everyone(self):
        devices = list(self.halo_targets(1)) + list(self.halo_targets(-1)) + [self.other_core()]
        devices += [self.plane_peer(dy, dx) for dy, dx in PLANE]
        return devices + [self.z_peer(dz) for dz in range(1, 8)]


class Halo:
    def __init__(self, spot, packed, landed, send_sem, recv_sem, step):
        targets = spot.halo_targets(step)
        self.packed, self.landed = packed, landed
        self.copies = [
            remote(
                packed.at[:, pl.ds(start, size), :], landed.at[:, pl.ds(start - 64, size), :],
                send_sem.at[i], recv_sem.at[i], targets[i],
            )
            for i, (start, size) in enumerate(PIECES[1:])
        ]

    def start(self):
        for copy in self.copies:
            copy.start()

    def wait(self):
        for copy in self.copies:
            copy.wait()

    def pack_grid(self, ref, pack_ref):
        for level in range(LEV):
            rows = slice(level * WTOK, (level + 1) * WTOK)
            self.packed[level] = nn(pack_ref[...], ref[rows, :]).astype(BF16)

    def unpack_windows(self, place_t_ref, ref):
        for pair in range(LEV // 2):
            grids = []
            for level in (2 * pair, 2 * pair + 1):
                grids.append(
                    nn(place_t_ref[:, :64], self.packed[level, :64, :])
                    + nn(place_t_ref[:, 64:], self.landed[level])
                )
            for w in range(2):
                tokens = jnp.concatenate([grid[w * 72:(w + 1) * 72] for grid in grids], axis=0)
                start = (pair * 2 + w) * WTOK
                ref[start:start + WTOK, :] = tokens.astype(BF16)

    def pack_windows(self, ref, place_ref, pair):
        windows = []
        for w in range(2):
            start = (pair * 2 + w) * WTOK
            windows.append(ref[start:start + WTOK, :].astype(F32))
        for half in range(2):
            grid = jnp.concatenate([w[half * 72:(half + 1) * 72] for w in windows], axis=0)
            self.packed[2 * pair + half] = nn(place_ref[...], grid.astype(BF16)).astype(BF16)

    def unpack_grid(self, pack_t_ref, ref):
        for level in range(LEV):
            grid = nn(pack_t_ref[:, :64], self.packed[level, :64, :])
            grid = grid + nn(pack_t_ref[:, 64:], self.landed[level])
            ref[level * WTOK:(level + 1) * WTOK, :] = grid.astype(BF16)


class Sum:
    def __init__(self, spot, size, flat, full, bufs, sems):
        self.spot, self.size, self.flat, self.full = spot, size, flat, full
        self.core_in, self.plane_out, self.plane_in, self.z_buf = bufs
        (self.core_s, self.core_r, self.plane_s, self.plane_r, self.z_s, self.z_r,
         self.back_s, self.back_r, self.last_s, self.last_r) = sems
        self.sent = []
        self.half = spot.core * (16 * size)
        self.own = (spot.y * 4 + spot.x) * size

    def launch(self, copy):
        copy.start()
        self.sent.append(copy)
        return copy

    def rows(self, dy, dx):
        y, x = self.spot.plane_spot(dy, dx)
        return (y * 4 + x) * self.size

    def to_core(self):
        other = 16 * self.size - self.half
        self.core_copy = self.launch(remote(
            self.flat.at[chunk(other, 16 * self.size)], self.core_in,
            self.core_s, self.core_r, self.spot.other_core(),
        ))

    def to_plane(self):
        self.core_copy.wait_recv()
        mine = self.flat[chunk(self.half, 16 * self.size), :].astype(F32)
        self.plane_out[...] = (mine + self.core_in[...].astype(F32)).astype(BF16)
        self.plane_copies = [
            self.launch(remote(
                self.plane_out.at[chunk(self.rows(dy, dx), self.size)], self.plane_in.at[k],
                self.plane_s.at[k], self.plane_r.at[k], self.spot.plane_peer(dy, dx),
            ))
            for k, (dy, dx) in enumerate(PLANE)
        ]

    def to_z(self):
        total = self.plane_out[chunk(self.own, self.size), :].astype(F32)
        for k, copy in enumerate(self.plane_copies):
            copy.wait_recv()
            total = total + self.plane_in[k].astype(F32)
        self.z_buf[self.spot.z] = total.astype(BF16)
        self.z_copies = [
            self.launch(remote(
                self.z_buf.at[self.spot.z], self.z_buf.at[self.spot.z],
                self.z_s.at[dz - 1], self.z_r.at[dz - 1], self.spot.z_peer(dz),
            ))
            for dz in range(1, 8)
        ]

    def back_to_plane(self):
        for copy in self.z_copies:
            copy.wait_recv()
        total = self.z_buf[0].astype(F32)
        for z in range(1, 8):
            total = total + self.z_buf[z].astype(F32)
        own = chunk(self.half + self.own, self.size)
        self.full[own, :] = total.astype(BF16)
        self.back_copies = [
            self.launch(remote(
                self.full.at[own], self.full.at[own],
                self.back_s.at[k], self.back_r.at[k], self.spot.plane_peer(dy, dx),
            ))
            for k, (dy, dx) in enumerate(PLANE)
        ]

    def back_to_core(self):
        self.last_copies = []
        for k in range(16):
            dy, dx = (0, 0)
            if k > 0:
                self.back_copies[k - 1].wait_recv()
                dy, dx = PLANE[k - 1]
            rows = chunk(self.half + self.rows(-dy, -dx), self.size)
            self.last_copies.append(self.launch(remote(
                self.full.at[rows], self.full.at[rows],
                self.last_s.at[k], self.last_r.at[k], self.spot.other_core(),
            )))

    def finish(self):
        for copy in self.last_copies:
            copy.wait_recv()

    def drain(self):
        for copy in self.sent:
            copy.wait_send()


def block_kernel(
    x_hbm, ct_hbm, bias_hbm, ga_hbm, wqkv_hbm, wproj_hbm, gm_hbm, wup_hbm, wdown_hbm,
    out_grid, gx_grid, full0, full1,
    x_in, ct_in, bias_in, ga_in, wqkv_in, wproj_in, gm_in, wup_in, wdown_in, load_sem,
    pack, pack_t, place, place_t,
    x_ref, ct_ref, out_ref, gx_ref, bias32, probs,
    normed_s, qkv_s, mixed_s, hid_s, hid_grad_s, nm_s, act_s, gpre_s, gqkv_s, gattn_s,
    packed, landed, halo_send, halo_recv, flat0, flat1,
    core_in0, plane_out0, plane_in0, z_buf0, core_in1, plane_out1, plane_in1, z_buf1,
    *sems,
):
    spot = Place()
    loads = []
    for i, (src, dst) in enumerate((
        (x_hbm, x_in), (ct_hbm, ct_in), (bias_hbm, bias_in), (ga_hbm, ga_in), (wqkv_hbm, wqkv_in),
        (wproj_hbm, wproj_in), (gm_hbm, gm_in), (wup_hbm, wup_in), (wdown_hbm, wdown_in),
    )):
        loads.append(pltpu.make_async_copy(src, dst, load_sem.at[i]))
        loads[-1].start()
    barrier = pltpu.get_barrier_semaphore()
    devices = spot.everyone()
    for device in devices:
        pl.semaphore_signal(barrier, inc=1, device_id=device, device_id_type=MESH)
    halos = [
        Halo(spot, packed.at[a], landed.at[a], halo_send.at[a], halo_recv.at[a], step)
        for a, step in enumerate((-1, -1, 1, 1))
    ]
    x_halo, ct_halo, out_halo, gx_halo = halos
    sums = [
        Sum(spot, CHUNK[0], flat0, full0, (core_in0, plane_out0, plane_in0, z_buf0), sems[:10]),
        Sum(spot, CHUNK[1], flat1, full1, (core_in1, plane_out1, plane_in1, z_buf1), sems[10:]),
    ]
    mlp_sum, attn_sum = sums

    pack[...] = table(pack_rows)
    loads[0].wait()
    x_halo.pack_grid(x_in, pack)
    pl.semaphore_wait(barrier, len(devices))
    x_halo.start()
    pack_t[...] = table_t(pack_rows)
    place[...] = table(place_rows)
    place_t[...] = table_t(place_rows)
    loads[1].wait()
    ct_halo.pack_grid(ct_in, pack)
    loads[2].wait()
    is_last = spot.lat == lax.axis_size("lat") - 1
    row_half = (lax.broadcasted_iota(jnp.int32, (WTOK, 1), 0) // WLON) % WLAT < WLAT // 2
    col_half = (lax.broadcasted_iota(jnp.int32, (1, WTOK), 1) // WLON) % WLAT < WLAT // 2
    cut = jnp.logical_and(row_half != col_half, is_last)
    penalty = jnp.where(cut, MASKED, 0.0)
    for h in range(HEADS):
        rows = slice(h * WTOK, (h + 1) * WTOK)
        bias32[rows, :] = bias_in[rows, :].astype(F32) + penalty
    for load in loads[3:]:
        load.wait()
    x_halo.wait()
    ct_halo.start()
    x_halo.unpack_windows(place_t, x_ref)

    scale = HEAD ** (-0.5)
    masks = head_masks()
    ga = ga_in[...]
    gm = gm_in[...]
    for n in range(4):
        rows = slice(n * WTOK, (n + 1) * WTOK)
        x = x_ref[rows, :].astype(F32)
        unit, _ = normalize(x)
        normed = (unit * ga).astype(BF16)
        normed_s[rows, :] = normed
        qkv = nn(normed, wqkv_in[...]).astype(BF16)
        qkv_s[rows, :] = qkv
        q = qkv[:, :C]
        k = qkv[:, C:2 * C]
        v = qkv[:, 2 * C:]
        mixed = jnp.zeros((WTOK, C), F32)
        for h in range(HEADS):
            s = nt(q * masks[h], k) * scale + bias32[h * WTOK:(h + 1) * WTOK, :]
            e = jnp.exp(s - jnp.max(s, axis=-1, keepdims=True))
            p = e * (1.0 / jnp.sum(e, axis=-1, keepdims=True))
            probs[n * HEADS + h] = p
            mixed = mixed + nn(p.astype(BF16), v * masks[h])
        mixed = mixed.astype(BF16)
        mixed_s[rows, :] = mixed
        hid_s[rows, :] = (x + nn(mixed, wproj_in[...])).astype(BF16)

    ct_halo.wait()
    ct_halo.unpack_windows(place_t, ct_ref)
    grad_gain_mlp = jnp.zeros((1, C), F32)
    for n in range(4):
        rows = slice(n * WTOK, (n + 1) * WTOK)
        hidden = hid_s[rows, :].astype(F32)
        unit, inv = normalize(hidden)
        nm = (unit * gm).astype(BF16)
        nm_s[rows, :] = nm
        ct = ct_ref[rows, :]
        down = jnp.zeros((WTOK, C), F32)
        grad_nm = jnp.zeros((WTOK, C), F32)
        for f in range(3):
            cols = slice(f * 256, (f + 1) * 256)
            z = nn(nm, wup_in[:, cols])
            phi = 0.5 * (1.0 + lax.erf(z * (0.5 ** 0.5)))
            act = (z * phi).astype(BF16)
            act_s[rows, cols] = act
            slope = phi + z * (jnp.exp(-0.5 * z * z) * 0.3989422804014327)
            gpre = (nn(ct, wdown_in[:, cols]) * slope).astype(BF16)
            gpre_s[rows, cols] = gpre
            down = down + nt(act, wdown_in[:, cols])
            grad_nm = grad_nm + nt(gpre, wup_in[:, cols])
        out_ref[rows, :] = (hidden + down).astype(BF16)
        grad_h, gain_term = norm_back(unit, inv, gm, grad_nm)
        grad_gain_mlp = grad_gain_mlp + gain_term
        grad_hidden = (ct.astype(F32) + grad_h).astype(BF16)
        hid_grad_s[rows, :] = grad_hidden
        gattn_s[rows, :] = nt(grad_hidden, wproj_in[...]).astype(BF16)

    def store_blocks(flat, base, values):
        for t in range(6):
            flat[base + t * C:base + (t + 1) * C, :] = values[:, t * 128:(t + 1) * 128].astype(BF16)

    store_blocks(flat0, 0, tn(nm_s[...], gpre_s[...]))
    store_blocks(flat0, 6 * C, tn(ct_ref[...], act_s[...]))
    flat0[12 * C:, :] = jnp.zeros((ROWS[0] - 12 * C, 128), BF16)
    mlp_sum.to_core()
    for pair in range(2):
        out_halo.pack_windows(out_ref, place, pair)
    out_halo.start()

    grad_gain_attn = jnp.zeros((1, C), F32)
    for n in range(4):
        rows = slice(n * WTOK, (n + 1) * WTOK)
        qkv = qkv_s[rows, :]
        q = qkv[:, :C]
        k = qkv[:, C:2 * C]
        v = qkv[:, 2 * C:]
        up = gattn_s[rows, :]
        gq = jnp.zeros((WTOK, C), F32)
        gk = jnp.zeros((WTOK, C), F32)
        gv = jnp.zeros((WTOK, C), F32)
        for h in range(HEADS):
            p = probs[n * HEADS + h]
            up_h = up * masks[h]
            gp = nt(up_h, v)
            inner = jnp.sum(p * gp, axis=-1, keepdims=True)
            gs = (p * (gp - inner) * scale).astype(BF16)
            gv = gv + tn(p.astype(BF16), up_h)
            gq = gq + nn(gs, k * masks[h])
            gk = gk + tn(gs, q * masks[h])
        gqkv = jnp.concatenate([gq, gk, gv], axis=1).astype(BF16)
        gqkv_s[rows, :] = gqkv
        grad_rolled = nt(gqkv, wqkv_in[...]).astype(BF16).astype(F32)
        unit, inv = normalize(x_ref[rows, :].astype(F32))
        grad_x, gain_term = norm_back(unit, inv, ga, grad_rolled)
        grad_gain_attn = grad_gain_attn + gain_term
        gx_ref[rows, :] = (hid_grad_s[rows, :].astype(F32) + grad_x).astype(BF16)
        if n == 0:
            mlp_sum.to_plane()
    grad_qkv = tn(normed_s[...], gqkv_s[...])
    grad_proj = tn(mixed_s[...], hid_grad_s[...])
    store_blocks(flat1, 0, jnp.concatenate([grad_qkv, grad_proj], axis=1))
    row = lax.broadcasted_iota(jnp.int32, (16, 128), 0)
    pad = jnp.zeros((1, 64), F32)
    gains = jnp.zeros((16, 128), F32)
    for g, value in enumerate((grad_gain_attn, grad_gain_mlp)):
        tail = jnp.concatenate([value[:, 128:], pad], axis=1)
        gains = jnp.where(row == 2 * g, value[:, :128], gains)
        gains = jnp.where(row == 2 * g + 1, tail, gains)
    flat1[GAIN_ROW:GAIN_ROW + 16, :] = gains.astype(BF16)
    flat1[GAIN_ROW + 16:, :] = jnp.zeros((ROWS[1] - GAIN_ROW - 16, 128), BF16)
    attn_sum.to_core()
    mlp_sum.to_z()
    attn_sum.to_plane()
    for pair in range(2):
        gx_halo.pack_windows(gx_ref, place, pair)
    gx_halo.start()
    mlp_sum.back_to_plane()
    attn_sum.to_z()
    out_halo.wait()
    out_halo.unpack_grid(pack_t, out_grid)
    mlp_sum.back_to_core()
    attn_sum.back_to_plane()
    gx_halo.wait()
    gx_halo.unpack_grid(pack_t, gx_grid)
    attn_sum.back_to_core()
    mlp_sum.finish()
    attn_sum.finish()
    mlp_sum.drain()
    attn_sum.drain()


def sum_bufs(size):
    return [
        pltpu.VMEM((16 * size, 128), BF16),
        pltpu.VMEM((16 * size, 128), BF16),
        pltpu.VMEM((15, size, 128), BF16),
        pltpu.VMEM((8, size, 128), BF16),
    ]


def sum_sems():
    sem = pltpu.SemaphoreType.DMA
    one = pltpu.SemaphoreType.DMA
    counts = (15, 15, 7, 7, 15, 15, 16, 16)
    return [one, one] + [sem((count,)) for count in counts]


def block_call(x, ct, bias, gain_attn, w_qkv, w_proj, gain_mlp, w_up, w_down):
    shape = jax.ShapeDtypeStruct
    args = (x, ct, bias, gain_attn, w_qkv, w_proj, gain_mlp, w_up, w_down)
    sem = pltpu.SemaphoreType.DMA
    return pl.pallas_call(
        block_kernel,
        out_shape=(
            shape((TOK, C), BF16),
            shape((TOK, C), BF16),
            shape((ROWS[0], 128), BF16),
            shape((ROWS[1], 128), BF16),
        ),
        in_specs=[ANY] * 9,
        out_specs=(VMEM,) * 4,
        scratch_shapes=[
            *[pltpu.VMEM(arg.shape, arg.dtype) for arg in args], sem((9,)),
            pltpu.VMEM((192, WTOK), BF16),
            pltpu.VMEM((WTOK, 192), BF16),
            pltpu.VMEM((192, WTOK), BF16),
            pltpu.VMEM((WTOK, 192), BF16),
            pltpu.VMEM((TOK, C), BF16),
            pltpu.VMEM((TOK, C), BF16),
            pltpu.VMEM((TOK, C), BF16),
            pltpu.VMEM((TOK, C), BF16),
            pltpu.VMEM((HEADS * WTOK, WTOK), F32),
            pltpu.VMEM((4 * HEADS, WTOK, WTOK), F32),
            pltpu.VMEM((TOK, C), BF16),
            pltpu.VMEM((TOK, 3 * C), BF16),
            pltpu.VMEM((TOK, C), BF16),
            pltpu.VMEM((TOK, C), BF16),
            pltpu.VMEM((TOK, C), BF16),
            pltpu.VMEM((TOK, C), BF16),
            pltpu.VMEM((TOK, FF), BF16),
            pltpu.VMEM((TOK, FF), BF16),
            pltpu.VMEM((TOK, 3 * C), BF16),
            pltpu.VMEM((TOK, C), BF16),
            pltpu.VMEM((4, LEV, 192, C), BF16),
            pltpu.VMEM((4, LEV, 128, C), BF16),
            sem((4, 3)), sem((4, 3)),
            pltpu.VMEM((ROWS[0], 128), BF16),
            pltpu.VMEM((ROWS[1], 128), BF16),
            *sum_bufs(CHUNK[0]), *sum_bufs(CHUNK[1]),
            *sum_sems(), *sum_sems(),
        ],
        compiler_params=pltpu.CompilerParams(
            collective_id=0, has_side_effects=True, vmem_limit_bytes=56 * 2**20
        ),
        name="block",
    )(*args)


def finish_kernel(
    out_in, gx_in, full0, full1, out_ref, gx_ref, qkv_ref, proj_ref, up_ref, down_ref, gain_ref
):
    def block(full, t):
        return full[t * C:(t + 1) * C, :].astype(F32) * FACTOR

    out_ref[...] = out_in[...]
    gx_ref[...] = gx_in[...]
    both = jnp.concatenate([block(full1, t) for t in range(6)], axis=1)
    qkv_ref[...] = both[:, :3 * C]
    proj_ref[...] = both[:, 3 * C:]
    for t in range(6):
        up_ref[:, t * 128:(t + 1) * 128] = block(full0, t)
        down_ref[:, t * 128:(t + 1) * 128] = block(full0, 6 + t)
    gains = full1[GAIN_ROW:GAIN_ROW + 16, :].astype(F32) * FACTOR
    for g in range(2):
        gain_ref[g:g + 1, :] = jnp.concatenate(
            [gains[2 * g:2 * g + 1], gains[2 * g + 1:2 * g + 2, :64]], axis=1
        )


def finish_call(out, gx, full0, full1):
    shape = jax.ShapeDtypeStruct
    return pl.pallas_call(
        finish_kernel,
        out_shape=(
            shape((TOK, C), BF16),
            shape((TOK, C), BF16),
            shape((C, 3 * C), F32),
            shape((C, C), F32),
            shape((C, FF), F32),
            shape((C, FF), F32),
            shape((2, C), F32),
        ),
        in_specs=[VMEM] * 4,
        out_specs=(VMEM,) * 7,
        compiler_params=pltpu.CompilerParams(vmem_limit_bytes=32 * 2**20),
        name="finish",
    )(out, gx, full0, full1)


def body(fields, gain_attn, w_qkv, bias, w_proj, gain_mlp, w_up, w_down, cotangent):
    out, gx, full0, full1 = block_call(
        fields.reshape(TOK, C), cotangent.reshape(TOK, C), bias.reshape(HEADS * WTOK, WTOK),
        gain_attn.reshape(1, C), w_qkv, w_proj, gain_mlp.reshape(1, C), w_up, w_down.T,
    )
    out, gx, qkv, proj, up, down, gains = finish_call(out, gx, full0, full1)
    return (
        out.reshape(fields.shape), gx.reshape(fields.shape), qkv, proj, up, down.T, gains[0], gains[1]
    )


def solution(mesh):
    grid = P(None, "lat", "lon", None)
    in_specs = (grid, P(), P(), P("lat", None, None, None), P(), P(), P(), P(), grid)
    out_specs = (grid, grid, P(), P(), P(), P(), P(), P())
    return jax.shard_map(body, mesh=mesh, in_specs=in_specs, out_specs=out_specs, check_vma=False)
```

```python
import jax
import jax.numpy as jnp
from jax import lax
from jax.experimental import pallas as pl
from jax.experimental.pallas import tpu as pltpu
from jax.sharding import PartitionSpec as P

WLAT = 6
WLON = 12
WTOK = 144
HEADS = 6
HEAD = 32
C = 192
FF = 768
TOK = 576
NORM_EPS = 1e-05
MASKED = -1e30
FACTOR = 1.0 / 384.0

STAY = 112
PACKED = 320
PIECES = ((112, 112), (224, 48), (272, 48))
PAIR = 288

CHUNK = (80, 32)
ROWS = (32 * 80, 32 * 32)
GAIN_ROW = 5 * C
PLANE = [(dy, dx) for dy in range(4) for dx in range(4) if (dy, dx) != (0, 0)]

F32 = jnp.float32
BF16 = jnp.bfloat16
MESH = pl.DeviceIdType.MESH
VMEM = pl.BlockSpec(memory_space=pltpu.VMEM)
HBM = pl.BlockSpec(memory_space=pltpu.HBM)


def nn(left, right):
    return lax.dot_general(left, right, (((1,), (0,)), ((), ())), preferred_element_type=F32)


def nt(left, right):
    return lax.dot_general(left, right, (((1,), (1,)), ((), ())), preferred_element_type=F32)


def tn(left, right):
    return lax.dot_general(left, right, (((0,), (0,)), ((), ())), preferred_element_type=F32)


def row_mean(values):
    return jnp.sum(values, axis=-1, keepdims=True) * (1.0 / C)


def normalize(values):
    center = values - row_mean(values)
    inv = lax.rsqrt(row_mean(center * center) + NORM_EPS)
    return center * inv, inv


def norm_back(unit, inv, gain, upstream):
    scaled = upstream * gain
    grad = inv * (scaled - row_mean(scaled) - unit * row_mean(scaled * unit))
    return grad, jnp.sum(upstream * unit, axis=0, keepdims=True)


def head_masks():
    head_of = lax.broadcasted_iota(jnp.int32, (1, C), 1) // HEAD
    return [jnp.where(head_of == h, 1.0, 0.0).astype(BF16) for h in range(HEADS)]


def piece_row(level, row, col):
    stay_row = row >= 3
    low = jnp.where(stay_row, row - 3, row)
    wide = level * 54 + low * 18 + col - 6
    thin = level * 18 + low * 6 + col
    right = jnp.where(stay_row, wide, wide + PIECES[0][0])
    left = jnp.where(stay_row, thin + PIECES[1][0], thin + PIECES[2][0])
    return jnp.where(col >= 6, right, left)


def pack_rows(token):
    return piece_row(token // 144, token % 144 // 24, token % 24)


def place_rows(token):
    col = token % WLON + token // 144 * WLON
    return piece_row(token % 144 // 72, (token % 72 // WLON + 3) % 6, (col + 6) % 24)


def table(rows_of):
    token = lax.broadcasted_iota(jnp.int32, (1, PAIR), 1)
    piece = lax.broadcasted_iota(jnp.int32, (PACKED, PAIR), 0)
    return jnp.where(piece == rows_of(token), 1.0, 0.0).astype(BF16)


def table_t(rows_of):
    token = lax.broadcasted_iota(jnp.int32, (PAIR, 1), 0)
    piece = lax.broadcasted_iota(jnp.int32, (PAIR, PACKED), 1)
    return jnp.where(piece == rows_of(token), 1.0, 0.0).astype(BF16)


def remote(src, dst, send_sem, recv_sem, device):
    return pltpu.make_async_remote_copy(
        src_ref=src, dst_ref=dst, send_sem=send_sem, recv_sem=recv_sem,
        device_id=device, device_id_type=MESH,
    )


def ring(index, step, size):
    return lax.rem(index + step + size, size)


def chunk(start, size):
    return pl.ds(pl.multiple_of(start, 16), size)


class Place:
    def __init__(self):
        self.lon, self.lat = lax.axis_index("lon"), lax.axis_index("lat")
        self.core = lax.rem(self.lon, 2)
        self.x = lax.rem(self.lon // 2, 4)
        self.y = self.lat // 8 * 2 + self.lon // 8
        self.z = lax.rem(self.lat, 8)

    def device(self, y, x, z, core):
        return ((lax.rem(y, 2) * 4 + x) * 2 + core, y // 2 * 8 + z)

    def other_core(self):
        return self.device(self.y, self.x, self.z, 1 - self.core)

    def plane_spot(self, dy, dx):
        return ring(self.y, dy, 4), ring(self.x, dx, 4)

    def plane_peer(self, dy, dx):
        y, x = self.plane_spot(dy, dx)
        return self.device(y, x, self.z, self.core)

    def z_peer(self, dz):
        return self.device(self.y, self.x, ring(self.z, dz, 8), self.core)

    def halo_targets(self, step):
        lon, lat = ring(self.lon, step, 16), ring(self.lat, step, 16)
        return (self.lon, lat), (lon, self.lat), (lon, lat)

    def everyone(self):
        devices = list(self.halo_targets(1)) + list(self.halo_targets(-1)) + [self.other_core()]
        devices += [self.plane_peer(dy, dx) for dy, dx in PLANE]
        return devices + [self.z_peer(dz) for dz in range(1, 8)]


class Halo:
    def __init__(self, spot, packed, landed, send_sem, recv_sem, step):
        targets = spot.halo_targets(step)
        self.packed, self.landed = packed, landed
        self.copies = [
            remote(
                packed.at[pl.ds(start, size), :], landed.at[pl.ds(start - STAY, size), :],
                send_sem.at[i], recv_sem.at[i], targets[i],
            )
            for i, (start, size) in enumerate(PIECES)
        ]

    def start(self):
        for copy in self.copies:
            copy.start()

    def wait(self):
        for copy in self.copies:
            copy.wait()

    def pack(self, ref, table_ref):
        pairs = [ref[i * PAIR:(i + 1) * PAIR, :].astype(F32) for i in range(2)]
        both = jnp.concatenate(pairs, axis=1).astype(BF16)
        self.packed[...] = nn(table_ref[...], both).astype(BF16)

    def unpack(self, table_ref, ref):
        both = nn(table_ref[:, :STAY], self.packed[:STAY, :]) + nn(table_ref[:, STAY:], self.landed[...])
        for i in range(2):
            ref[i * PAIR:(i + 1) * PAIR, :] = both[:, i * C:(i + 1) * C].astype(BF16)


class Sum:
    def __init__(self, spot, size, flat, full, bufs, sems):
        self.spot, self.size, self.flat, self.full = spot, size, flat, full
        self.core_in, self.plane_out, self.plane_in, self.z_buf = bufs
        (self.core_s, self.core_r, self.plane_s, self.plane_r, self.z_s, self.z_r,
         self.back_s, self.back_r, self.last_s, self.last_r) = sems
        self.sent = []
        self.half = spot.core * (16 * size)
        self.own = (spot.y * 4 + spot.x) * size

    def launch(self, copy):
        copy.start()
        self.sent.append(copy)
        return copy

    def rows(self, dy, dx):
        y, x = self.spot.plane_spot(dy, dx)
        return (y * 4 + x) * self.size

    def to_core(self):
        other = 16 * self.size - self.half
        self.core_copy = self.launch(remote(
            self.flat.at[chunk(other, 16 * self.size)], self.core_in,
            self.core_s, self.core_r, self.spot.other_core(),
        ))

    def to_plane(self):
        self.core_copy.wait_recv()
        mine = self.flat[chunk(self.half, 16 * self.size), :].astype(F32)
        self.plane_out[...] = (mine + self.core_in[...].astype(F32)).astype(BF16)
        self.plane_copies = [
            self.launch(remote(
                self.plane_out.at[chunk(self.rows(dy, dx), self.size)], self.plane_in.at[k],
                self.plane_s.at[k], self.plane_r.at[k], self.spot.plane_peer(dy, dx),
            ))
            for k, (dy, dx) in enumerate(PLANE)
        ]

    def to_z(self):
        total = self.plane_out[chunk(self.own, self.size), :].astype(F32)
        for k, copy in enumerate(self.plane_copies):
            copy.wait_recv()
            total = total + self.plane_in[k].astype(F32)
        self.z_buf[self.spot.z] = total.astype(BF16)
        self.z_copies = [
            self.launch(remote(
                self.z_buf.at[self.spot.z], self.z_buf.at[self.spot.z],
                self.z_s.at[dz - 1], self.z_r.at[dz - 1], self.spot.z_peer(dz),
            ))
            for dz in range(1, 8)
        ]

    def back_to_plane(self):
        for copy in self.z_copies:
            copy.wait_recv()
        total = self.z_buf[0].astype(F32)
        for z in range(1, 8):
            total = total + self.z_buf[z].astype(F32)
        own = chunk(self.half + self.own, self.size)
        self.full[own, :] = total.astype(BF16)
        self.back_copies = [
            self.launch(remote(
                self.full.at[own], self.full.at[own],
                self.back_s.at[k], self.back_r.at[k], self.spot.plane_peer(dy, dx),
            ))
            for k, (dy, dx) in enumerate(PLANE)
        ]

    def back_to_core(self):
        self.last_copies = []
        for k in range(16):
            dy, dx = (0, 0)
            if k > 0:
                self.back_copies[k - 1].wait_recv()
                dy, dx = PLANE[k - 1]
            rows = chunk(self.half + self.rows(-dy, -dx), self.size)
            self.last_copies.append(self.launch(remote(
                self.full.at[rows], self.full.at[rows],
                self.last_s.at[k], self.last_r.at[k], self.spot.other_core(),
            )))

    def finish(self):
        for copy in self.last_copies:
            copy.wait_recv()

    def drain(self):
        for copy in self.sent:
            copy.wait_send()


def block_kernel(
    x_hbm, ct_hbm, bias_hbm, ga_hbm, wqkv_hbm, wproj_hbm, gm_hbm, wup_hbm, wdown_hbm,
    out_grid, gx_grid, full0, full1,
    x_in, ct_in, bias_in, ga_in, wqkv_in, wproj_in, gm_in, wup_in, wdown_in, load_sem,
    pack, pack_t, place, place_t,
    x_ref, ct_ref, out_ref, gx_ref, bias32, probs,
    normed_s, qkv_s, mixed_s, hid_s, hid_grad_s, nm_s, act_s, gpre_s, gqkv_s, gattn_s,
    packed, landed, halo_send, halo_recv, flat0, flat1,
    core_in0, plane_out0, plane_in0, z_buf0, core_in1, plane_out1, plane_in1, z_buf1,
    *sems,
):
    spot = Place()
    loads = []
    for i, (src, dst) in enumerate((
        (x_hbm, x_in), (ct_hbm, ct_in), (bias_hbm, bias_in), (ga_hbm, ga_in), (wqkv_hbm, wqkv_in),
        (wproj_hbm, wproj_in), (gm_hbm, gm_in), (wup_hbm, wup_in), (wdown_hbm, wdown_in),
    )):
        loads.append(pltpu.make_async_copy(src, dst, load_sem.at[i]))
        loads[-1].start()
    barrier = pltpu.get_barrier_semaphore()
    devices = spot.everyone()
    for device in devices:
        pl.semaphore_signal(barrier, inc=1, device_id=device, device_id_type=MESH)
    halos = [
        Halo(spot, packed.at[a], landed.at[a], halo_send.at[a], halo_recv.at[a], step)
        for a, step in enumerate((-1, -1, 1, 1))
    ]
    x_halo, ct_halo, out_halo, gx_halo = halos
    sums = [
        Sum(spot, CHUNK[0], flat0, full0, (core_in0, plane_out0, plane_in0, z_buf0), sems[:10]),
        Sum(spot, CHUNK[1], flat1, full1, (core_in1, plane_out1, plane_in1, z_buf1), sems[10:]),
    ]
    mlp_sum, attn_sum = sums

    pack[...] = table(pack_rows)
    loads[0].wait()
    x_halo.pack(x_in, pack)
    pl.semaphore_wait(barrier, len(devices))
    x_halo.start()
    pack_t[...] = table_t(pack_rows)
    place[...] = table(place_rows)
    place_t[...] = table_t(place_rows)
    loads[1].wait()
    ct_halo.pack(ct_in, pack)
    ct_halo.start()
    loads[2].wait()
    is_last = spot.lat == lax.axis_size("lat") - 1
    row_half = (lax.broadcasted_iota(jnp.int32, (WTOK, 1), 0) // WLON) % WLAT < WLAT // 2
    col_half = (lax.broadcasted_iota(jnp.int32, (1, WTOK), 1) // WLON) % WLAT < WLAT // 2
    cut = jnp.logical_and(row_half != col_half, is_last)
    penalty = jnp.where(cut, MASKED, 0.0)
    for h in range(HEADS):
        rows = slice(h * WTOK, (h + 1) * WTOK)
        bias32[rows, :] = bias_in[rows, :].astype(F32) + penalty
    for load in loads[3:]:
        load.wait()
    x_halo.wait()
    x_halo.unpack(place_t, x_ref)

    scale = HEAD ** (-0.5)
    masks = head_masks()
    ga = ga_in[...]
    gm = gm_in[...]
    for n in range(4):
        rows = slice(n * WTOK, (n + 1) * WTOK)
        x = x_ref[rows, :].astype(F32)
        unit, _ = normalize(x)
        normed = (unit * ga).astype(BF16)
        normed_s[rows, :] = normed
        qkv = nn(normed, wqkv_in[...]).astype(BF16)
        qkv_s[rows, :] = qkv
        q = qkv[:, :C]
        k = qkv[:, C:2 * C]
        v = qkv[:, 2 * C:]
        mixed = jnp.zeros((WTOK, C), F32)
        for h in range(HEADS):
            s = nt(q * masks[h], k) * scale + bias32[h * WTOK:(h + 1) * WTOK, :]
            e = jnp.exp(s - jnp.max(s, axis=-1, keepdims=True))
            p = e * (1.0 / jnp.sum(e, axis=-1, keepdims=True))
            probs[n * HEADS + h] = p
            mixed = mixed + nn(p.astype(BF16), v * masks[h])
        mixed = mixed.astype(BF16)
        mixed_s[rows, :] = mixed
        hid_s[rows, :] = (x + nn(mixed, wproj_in[...])).astype(BF16)

    ct_halo.wait()
    ct_halo.unpack(place_t, ct_ref)
    grad_gain_mlp = jnp.zeros((1, C), F32)
    for n in range(4):
        rows = slice(n * WTOK, (n + 1) * WTOK)
        hidden = hid_s[rows, :].astype(F32)
        unit, inv = normalize(hidden)
        nm = (unit * gm).astype(BF16)
        nm_s[rows, :] = nm
        ct = ct_ref[rows, :]
        down = jnp.zeros((WTOK, C), F32)
        grad_nm = jnp.zeros((WTOK, C), F32)
        for f in range(3):
            cols = slice(f * 256, (f + 1) * 256)
            z = nn(nm, wup_in[:, cols])
            phi = 0.5 * (1.0 + lax.erf(z * (0.5 ** 0.5)))
            act = (z * phi).astype(BF16)
            act_s[rows, cols] = act
            slope = phi + z * (jnp.exp(-0.5 * z * z) * 0.3989422804014327)
            gpre = (nn(ct, wdown_in[:, cols]) * slope).astype(BF16)
            gpre_s[rows, cols] = gpre
            down = down + nt(act, wdown_in[:, cols])
            grad_nm = grad_nm + nt(gpre, wup_in[:, cols])
        out_ref[rows, :] = (hidden + down).astype(BF16)
        grad_h, gain_term = norm_back(unit, inv, gm, grad_nm)
        grad_gain_mlp = grad_gain_mlp + gain_term
        grad_hidden = (ct.astype(F32) + grad_h).astype(BF16)
        hid_grad_s[rows, :] = grad_hidden
        gattn_s[rows, :] = nt(grad_hidden, wproj_in[...]).astype(BF16)

    def store_blocks(flat, base, values):
        for t in range(values.shape[1] // 128):
            flat[base + t * C:base + (t + 1) * C, :] = values[:, t * 128:(t + 1) * 128].astype(BF16)

    store_blocks(flat0, 0, tn(nm_s[...], gpre_s[...]))
    store_blocks(flat0, 6 * C, tn(ct_ref[...], act_s[...]))
    grad_proj = tn(mixed_s[...], hid_grad_s[...])
    store_blocks(flat0, 12 * C, grad_proj)
    flat0[13 * C:, :] = jnp.zeros((ROWS[0] - 13 * C, 128), BF16)
    mlp_sum.to_core()
    out_halo.pack(out_ref, place)
    mlp_sum.to_plane()

    grad_gain_attn = jnp.zeros((1, C), F32)
    for n in range(4):
        rows = slice(n * WTOK, (n + 1) * WTOK)
        qkv = qkv_s[rows, :]
        q = qkv[:, :C]
        k = qkv[:, C:2 * C]
        v = qkv[:, 2 * C:]
        up = gattn_s[rows, :]
        gq = jnp.zeros((WTOK, C), F32)
        gk = jnp.zeros((WTOK, C), F32)
        gv = jnp.zeros((WTOK, C), F32)
        for h in range(HEADS):
            p = probs[n * HEADS + h]
            up_h = up * masks[h]
            gp = nt(up_h, v)
            inner = jnp.sum(p * gp, axis=-1, keepdims=True)
            gs = (p * (gp - inner) * scale).astype(BF16)
            gv = gv + tn(p.astype(BF16), up_h)
            gq = gq + nn(gs, k * masks[h])
            gk = gk + tn(gs, q * masks[h])
        gqkv = jnp.concatenate([gq, gk, gv], axis=1).astype(BF16)
        gqkv_s[rows, :] = gqkv
        grad_rolled = nt(gqkv, wqkv_in[...]).astype(BF16).astype(F32)
        unit, inv = normalize(x_ref[rows, :].astype(F32))
        grad_x, gain_term = norm_back(unit, inv, ga, grad_rolled)
        grad_gain_attn = grad_gain_attn + gain_term
        gx_ref[rows, :] = (hid_grad_s[rows, :].astype(F32) + grad_x).astype(BF16)
        if n == 1:
            out_halo.start()
    mlp_sum.to_z()
    grad_qkv = tn(normed_s[...], gqkv_s[...])
    store_blocks(flat1, 0, grad_qkv)
    mixed_tile = jnp.concatenate([grad_qkv[:, 512:], grad_proj[:, 128:]], axis=1)
    store_blocks(flat1, 4 * C, mixed_tile)
    row = lax.broadcasted_iota(jnp.int32, (16, 128), 0)
    pad = jnp.zeros((1, 64), F32)
    gains = jnp.zeros((16, 128), F32)
    for g, value in enumerate((grad_gain_attn, grad_gain_mlp)):
        tail = jnp.concatenate([value[:, 128:], pad], axis=1)
        gains = jnp.where(row == 2 * g, value[:, :128], gains)
        gains = jnp.where(row == 2 * g + 1, tail, gains)
    flat1[GAIN_ROW:GAIN_ROW + 16, :] = gains.astype(BF16)
    flat1[GAIN_ROW + 16:, :] = jnp.zeros((ROWS[1] - GAIN_ROW - 16, 128), BF16)
    attn_sum.to_core()
    gx_halo.pack(gx_ref, place)
    attn_sum.to_plane()
    gx_halo.start()
    mlp_sum.back_to_plane()
    out_halo.wait()
    out_halo.unpack(pack_t, out_grid)
    attn_sum.to_z()
    gx_halo.wait()
    gx_halo.unpack(pack_t, gx_grid)
    mlp_sum.back_to_core()
    attn_sum.back_to_plane()
    mlp_sum.finish()
    attn_sum.back_to_core()
    attn_sum.finish()
    mlp_sum.drain()
    attn_sum.drain()


def sum_bufs(size):
    return [
        pltpu.VMEM((16 * size, 128), BF16),
        pltpu.VMEM((16 * size, 128), BF16),
        pltpu.VMEM((15, size, 128), BF16),
        pltpu.VMEM((8, size, 128), BF16),
    ]


def sum_sems():
    sem = pltpu.SemaphoreType.DMA
    one = pltpu.SemaphoreType.DMA
    counts = (15, 15, 7, 7, 15, 15, 16, 16)
    return [one, one] + [sem((count,)) for count in counts]


def block_call(x, ct, bias, gain_attn, w_qkv, w_proj, gain_mlp, w_up, w_down):
    shape = jax.ShapeDtypeStruct
    args = (x, ct, bias, gain_attn, w_qkv, w_proj, gain_mlp, w_up, w_down)
    sem = pltpu.SemaphoreType.DMA
    return pl.pallas_call(
        block_kernel,
        out_shape=(
            shape((TOK, C), BF16),
            shape((TOK, C), BF16),
            shape((ROWS[0], 128), BF16),
            shape((ROWS[1], 128), BF16),
        ),
        in_specs=[HBM] * 9,
        out_specs=(VMEM,) * 4,
        scratch_shapes=[
            *[pltpu.VMEM(arg.shape, arg.dtype) for arg in args], sem((9,)),
            pltpu.VMEM((PACKED, PAIR), BF16),
            pltpu.VMEM((PAIR, PACKED), BF16),
            pltpu.VMEM((PACKED, PAIR), BF16),
            pltpu.VMEM((PAIR, PACKED), BF16),
            pltpu.VMEM((TOK, C), BF16),
            pltpu.VMEM((TOK, C), BF16),
            pltpu.VMEM((TOK, C), BF16),
            pltpu.VMEM((TOK, C), BF16),
            pltpu.VMEM((HEADS * WTOK, WTOK), F32),
            pltpu.VMEM((4 * HEADS, WTOK, WTOK), F32),
            pltpu.VMEM((TOK, C), BF16),
            pltpu.VMEM((TOK, 3 * C), BF16),
            pltpu.VMEM((TOK, C), BF16),
            pltpu.VMEM((TOK, C), BF16),
            pltpu.VMEM((TOK, C), BF16),
            pltpu.VMEM((TOK, C), BF16),
            pltpu.VMEM((TOK, FF), BF16),
            pltpu.VMEM((TOK, FF), BF16),
            pltpu.VMEM((TOK, 3 * C), BF16),
            pltpu.VMEM((TOK, C), BF16),
            pltpu.VMEM((4, PACKED, 2 * C), BF16),
            pltpu.VMEM((4, PACKED - STAY, 2 * C), BF16),
            sem((4, 3)), sem((4, 3)),
            pltpu.VMEM((ROWS[0], 128), BF16),
            pltpu.VMEM((ROWS[1], 128), BF16),
            *sum_bufs(CHUNK[0]), *sum_bufs(CHUNK[1]),
            *sum_sems(), *sum_sems(),
        ],
        compiler_params=pltpu.CompilerParams(
            collective_id=0, has_side_effects=True, vmem_limit_bytes=56 * 2**20
        ),
        name="block",
    )(*args)


def finish_kernel(
    out_hbm, gx_hbm, full0_hbm, full1_hbm,
    out_ref, gx_ref, qkv_ref, proj_ref, up_ref, down_ref, ga_ref, gm_ref,
    full0, full1, sem,
):
    copies = []
    for i, (src, dst) in enumerate((
        (full1_hbm, full1), (full0_hbm, full0), (out_hbm, out_ref), (gx_hbm, gx_ref),
    )):
        copies.append(pltpu.make_async_copy(src, dst, sem.at[i]))
        copies[-1].start()

    def block(full, t):
        return full[t * C:(t + 1) * C, :].astype(F32) * FACTOR

    copies[0].wait()
    copies[1].wait()
    for t in range(4):
        qkv_ref[:, t * 128:(t + 1) * 128] = block(full1, t)
    mixed_tile = block(full1, 4)
    qkv_ref[:, 512:] = mixed_tile[:, :64]
    proj_ref[:, :128] = block(full0, 12)
    proj_ref[:, 128:] = mixed_tile[:, 64:]
    for t in range(6):
        up_ref[:, t * 128:(t + 1) * 128] = block(full0, t)
        down_ref[:, t * 128:(t + 1) * 128] = block(full0, 6 + t)
    gains = full1[GAIN_ROW:GAIN_ROW + 16, :].astype(F32) * FACTOR
    for g, ref in enumerate((ga_ref, gm_ref)):
        ref[...] = jnp.concatenate(
            [gains[2 * g:2 * g + 1], gains[2 * g + 1:2 * g + 2, :64]], axis=1
        )
    copies[2].wait()
    copies[3].wait()


def finish_call(out, gx, full0, full1):
    shape = jax.ShapeDtypeStruct
    return pl.pallas_call(
        finish_kernel,
        out_shape=(
            shape((TOK, C), BF16),
            shape((TOK, C), BF16),
            shape((C, 3 * C), F32),
            shape((C, C), F32),
            shape((C, FF), F32),
            shape((C, FF), F32),
            shape((1, C), F32),
            shape((1, C), F32),
        ),
        in_specs=[HBM] * 4,
        out_specs=(HBM, HBM) + (VMEM,) * 6,
        scratch_shapes=[
            pltpu.VMEM((ROWS[0], 128), BF16),
            pltpu.VMEM((ROWS[1], 128), BF16),
            pltpu.SemaphoreType.DMA((4,)),
        ],
        compiler_params=pltpu.CompilerParams(vmem_limit_bytes=56 * 2**20),
        name="finish",
    )(out, gx, full0, full1)


def body(fields, gain_attn, w_qkv, bias, w_proj, gain_mlp, w_up, w_down, cotangent):
    out, gx, full0, full1 = block_call(
        fields.reshape(TOK, C), cotangent.reshape(TOK, C), bias.reshape(HEADS * WTOK, WTOK),
        gain_attn.reshape(1, C), w_qkv, w_proj, gain_mlp.reshape(1, C), w_up, w_down.T,
    )
    out, gx, qkv, proj, up, down, ga, gm = finish_call(out, gx, full0, full1)
    return (
        out.reshape(fields.shape), gx.reshape(fields.shape), qkv, proj, up, down.T,
        ga.reshape(C), gm.reshape(C),
    )


def solution(mesh):
    grid = P(None, "lat", "lon", None)
    in_specs = (grid, P(), P(), P("lat", None, None, None), P(), P(), P(), P(), grid)
    out_specs = (grid, grid, P(), P(), P(), P(), P(), P())
    return jax.shard_map(body, mesh=mesh, in_specs=in_specs, out_specs=out_specs, check_vma=False)
```

```python
import jax
import jax.numpy as jnp
from jax import lax
from jax.experimental import pallas as pl
from jax.experimental.pallas import tpu as pltpu
from jax.sharding import PartitionSpec as P

WLAT = 6
WLON = 12
WTOK = 144
HEADS = 6
HEAD = 32
C = 192
FF = 768
TOK = 576
NORM_EPS = 1e-05
MASKED = -1e30
FACTOR = 1.0 / 384.0

STAY = 112
PACKED = 320
PIECES = ((112, 112), (224, 48), (272, 48))
PAIR = 288

CHUNK = (80, 32)
ROWS = (32 * 80, 32 * 32)
PLANE = [(dy, dx) for dy in range(4) for dx in range(4) if (dy, dx) != (0, 0)]

F32 = jnp.float32
BF16 = jnp.bfloat16
MESH = pl.DeviceIdType.MESH
VMEM = pl.BlockSpec(memory_space=pltpu.VMEM)
HBM = pl.BlockSpec(memory_space=pltpu.HBM)


def nn(left, right):
    return lax.dot_general(left, right, (((1,), (0,)), ((), ())), preferred_element_type=F32)


def nt(left, right):
    return lax.dot_general(left, right, (((1,), (1,)), ((), ())), preferred_element_type=F32)


def tn(left, right):
    return lax.dot_general(left, right, (((0,), (0,)), ((), ())), preferred_element_type=F32)


def row_mean(values):
    return jnp.sum(values, axis=-1, keepdims=True) * (1.0 / C)


def normalize(values):
    center = values - row_mean(values)
    inv = lax.rsqrt(row_mean(center * center) + NORM_EPS)
    return center * inv, inv


def norm_back(unit, inv, gain, upstream):
    scaled = upstream * gain
    grad = inv * (scaled - row_mean(scaled) - unit * row_mean(scaled * unit))
    return grad


def head_masks():
    head_of = lax.broadcasted_iota(jnp.int32, (1, C), 1) // HEAD
    return [jnp.where(head_of == h, 1.0, 0.0).astype(BF16) for h in range(HEADS)]


def piece_row(level, row, col):
    stay_row = row >= 3
    low = jnp.where(stay_row, row - 3, row)
    wide = level * 54 + low * 18 + col - 6
    thin = level * 18 + low * 6 + col
    right = jnp.where(stay_row, wide, wide + PIECES[0][0])
    left = jnp.where(stay_row, thin + PIECES[1][0], thin + PIECES[2][0])
    return jnp.where(col >= 6, right, left)


def pack_rows(token):
    return piece_row(token // 144, token % 144 // 24, token % 24)


def place_rows(token):
    col = token % WLON + token // 144 * WLON
    return piece_row(token % 144 // 72, (token % 72 // WLON + 3) % 6, (col + 6) % 24)


def table(rows_of):
    token = lax.broadcasted_iota(jnp.int32, (1, PAIR), 1)
    piece = lax.broadcasted_iota(jnp.int32, (PACKED, PAIR), 0)
    return jnp.where(piece == rows_of(token), 1.0, 0.0).astype(BF16)


def table_t(rows_of):
    token = lax.broadcasted_iota(jnp.int32, (PAIR, 1), 0)
    piece = lax.broadcasted_iota(jnp.int32, (PAIR, PACKED), 1)
    return jnp.where(piece == rows_of(token), 1.0, 0.0).astype(BF16)


def remote(src, dst, send_sem, recv_sem, device):
    return pltpu.make_async_remote_copy(
        src_ref=src, dst_ref=dst, send_sem=send_sem, recv_sem=recv_sem,
        device_id=device, device_id_type=MESH,
    )


def ring(index, step, size):
    return lax.rem(index + step + size, size)


def chunk(start, size):
    return pl.ds(pl.multiple_of(start, 16), size)


class Place:
    def __init__(self):
        self.lon, self.lat = lax.axis_index("lon"), lax.axis_index("lat")
        self.core = lax.rem(self.lon, 2)
        self.x = lax.rem(self.lon // 2, 4)
        self.y = self.lat // 8 * 2 + self.lon // 8
        self.z = lax.rem(self.lat, 8)

    def device(self, y, x, z, core):
        return ((lax.rem(y, 2) * 4 + x) * 2 + core, y // 2 * 8 + z)

    def other_core(self):
        return self.device(self.y, self.x, self.z, 1 - self.core)

    def plane_spot(self, dy, dx):
        return ring(self.y, dy, 4), ring(self.x, dx, 4)

    def plane_peer(self, dy, dx):
        y, x = self.plane_spot(dy, dx)
        return self.device(y, x, self.z, self.core)

    def z_peer(self, dz):
        return self.device(self.y, self.x, ring(self.z, dz, 8), self.core)

    def halo_targets(self, step):
        lon, lat = ring(self.lon, step, 16), ring(self.lat, step, 16)
        return (self.lon, lat), (lon, self.lat), (lon, lat)

    def everyone(self):
        devices = list(self.halo_targets(1)) + list(self.halo_targets(-1)) + [self.other_core()]
        devices += [self.plane_peer(dy, dx) for dy, dx in PLANE]
        return devices + [self.z_peer(dz) for dz in range(1, 8)]


class Halo:
    def __init__(self, spot, packed, landed, send_sem, recv_sem, step):
        targets = spot.halo_targets(step)
        self.packed, self.landed = packed, landed
        self.copies = [
            remote(
                packed.at[pl.ds(start, size), :], landed.at[pl.ds(start - STAY, size), :],
                send_sem.at[i], recv_sem.at[i], targets[i],
            )
            for i, (start, size) in enumerate(PIECES)
        ]

    def start(self):
        for copy in self.copies:
            copy.start()

    def wait(self):
        for copy in self.copies:
            copy.wait()

    def pack(self, ref, table_ref):
        pairs = [ref[i * PAIR:(i + 1) * PAIR, :].astype(F32) for i in range(2)]
        both = jnp.concatenate(pairs, axis=1).astype(BF16)
        self.packed[...] = nn(table_ref[...], both).astype(BF16)

    def unpack(self, table_ref, ref):
        both = nn(table_ref[:, :STAY], self.packed[:STAY, :]) + nn(table_ref[:, STAY:], self.landed[...])
        for i in range(2):
            ref[i * PAIR:(i + 1) * PAIR, :] = both[:, i * C:(i + 1) * C].astype(BF16)


class Sum:
    def __init__(self, spot, size, flat, full, bufs, sems):
        self.spot, self.size, self.flat, self.full = spot, size, flat, full
        self.core_in, self.plane_out, self.plane_in, self.z_buf = bufs
        (self.core_s, self.core_r, self.plane_s, self.plane_r, self.z_s, self.z_r,
         self.back_s, self.back_r, self.last_s, self.last_r) = sems
        self.sent = []
        self.half = spot.core * (16 * size)
        self.own = (spot.y * 4 + spot.x) * size

    def launch(self, copy):
        copy.start()
        self.sent.append(copy)
        return copy

    def rows(self, dy, dx):
        y, x = self.spot.plane_spot(dy, dx)
        return (y * 4 + x) * self.size

    def to_core(self):
        other = 16 * self.size - self.half
        self.core_copy = self.launch(remote(
            self.flat.at[chunk(other, 16 * self.size)], self.core_in,
            self.core_s, self.core_r, self.spot.other_core(),
        ))

    def to_plane(self):
        self.core_copy.wait_recv()
        mine = self.flat[chunk(self.half, 16 * self.size), :].astype(F32)
        self.plane_out[...] = (mine + self.core_in[...].astype(F32)).astype(BF16)
        self.plane_copies = [
            self.launch(remote(
                self.plane_out.at[chunk(self.rows(dy, dx), self.size)], self.plane_in.at[k],
                self.plane_s.at[k], self.plane_r.at[k], self.spot.plane_peer(dy, dx),
            ))
            for k, (dy, dx) in enumerate(PLANE)
        ]

    def to_z(self):
        total = self.plane_out[chunk(self.own, self.size), :].astype(F32)
        for k, copy in enumerate(self.plane_copies):
            copy.wait_recv()
            total = total + self.plane_in[k].astype(F32)
        self.z_buf[self.spot.z] = total.astype(BF16)
        self.z_copies = [
            self.launch(remote(
                self.z_buf.at[self.spot.z], self.z_buf.at[self.spot.z],
                self.z_s.at[dz - 1], self.z_r.at[dz - 1], self.spot.z_peer(dz),
            ))
            for dz in range(1, 8)
        ]

    def back_to_plane(self):
        for copy in self.z_copies:
            copy.wait_recv()
        total = self.z_buf[0].astype(F32)
        for z in range(1, 8):
            total = total + self.z_buf[z].astype(F32)
        own = chunk(self.half + self.own, self.size)
        self.full[own, :] = total.astype(BF16)
        self.back_copies = [
            self.launch(remote(
                self.full.at[own], self.full.at[own],
                self.back_s.at[k], self.back_r.at[k], self.spot.plane_peer(dy, dx),
            ))
            for k, (dy, dx) in enumerate(PLANE)
        ]

    def back_to_core(self):
        self.last_copies = []
        for k in range(16):
            dy, dx = (0, 0)
            if k > 0:
                self.back_copies[k - 1].wait_recv()
                dy, dx = PLANE[k - 1]
            rows = chunk(self.half + self.rows(-dy, -dx), self.size)
            self.last_copies.append(self.launch(remote(
                self.full.at[rows], self.full.at[rows],
                self.last_s.at[k], self.last_r.at[k], self.spot.other_core(),
            )))

    def finish(self):
        for copy in self.last_copies:
            copy.wait_recv()

    def drain(self):
        for copy in self.sent:
            copy.wait_send()


def block_kernel(
    x_hbm, ct_hbm, bias_hbm, ga_hbm, wqkv_hbm, wproj_hbm, gm_hbm, wup_hbm, wdown_hbm,
    out_grid, gx_grid, full0, full1,
    x_in, ct_in, bias_in, ga_in, wqkv_in, wproj_in, gm_in, wup_in, wdown_in, load_sem,
    pack, pack_t, place, place_t,
    x_ref, ct_ref, out_ref, gx_ref, bias32, probs,
    normed_s, qkv_s, mixed_s, hid_s, hid_grad_s, nm_s, act_s, gpre_s, gqkv_s, gattn_s,
    packed, landed, halo_send, halo_recv, flat0, flat1,
    core_in0, plane_out0, plane_in0, z_buf0, core_in1, plane_out1, plane_in1, z_buf1,
    *sems,
):
    spot = Place()
    loads = []
    for i, (src, dst) in enumerate((
        (x_hbm, x_in), (ct_hbm, ct_in), (bias_hbm, bias_in), (ga_hbm, ga_in), (wqkv_hbm, wqkv_in),
        (wproj_hbm, wproj_in), (gm_hbm, gm_in), (wup_hbm, wup_in), (wdown_hbm, wdown_in),
    )):
        loads.append(pltpu.make_async_copy(src, dst, load_sem.at[i]))
        loads[-1].start()
    barrier = pltpu.get_barrier_semaphore()
    devices = spot.everyone()
    for device in devices:
        pl.semaphore_signal(barrier, inc=1, device_id=device, device_id_type=MESH)
    halos = [
        Halo(spot, packed.at[a], landed.at[a], halo_send.at[a], halo_recv.at[a], step)
        for a, step in enumerate((-1, -1, 1, 1))
    ]
    x_halo, ct_halo, out_halo, gx_halo = halos
    sums = [
        Sum(spot, CHUNK[0], flat0, full0, (core_in0, plane_out0, plane_in0, z_buf0), sems[:10]),
        Sum(spot, CHUNK[1], flat1, full1, (core_in1, plane_out1, plane_in1, z_buf1), sems[10:]),
    ]
    mlp_sum, attn_sum = sums

    pack[...] = table(pack_rows)
    loads[0].wait()
    x_halo.pack(x_in, pack)
    pl.semaphore_wait(barrier, len(devices))
    x_halo.start()
    pack_t[...] = table_t(pack_rows)
    flat0[13 * C:, :] = jnp.zeros((ROWS[0] - 13 * C, 128), BF16)
    flat1[5 * C:, :] = jnp.zeros((ROWS[1] - 5 * C, 128), BF16)
    place[...] = table(place_rows)
    place_t[...] = table_t(place_rows)
    loads[1].wait()
    ct_halo.pack(ct_in, pack)
    ct_halo.start()
    loads[2].wait()
    is_last = spot.lat == lax.axis_size("lat") - 1
    row_half = (lax.broadcasted_iota(jnp.int32, (WTOK, 1), 0) // WLON) % WLAT < WLAT // 2
    col_half = (lax.broadcasted_iota(jnp.int32, (1, WTOK), 1) // WLON) % WLAT < WLAT // 2
    cut = jnp.logical_and(row_half != col_half, is_last)
    penalty = jnp.where(cut, MASKED, 0.0)
    for h in range(HEADS):
        rows = slice(h * WTOK, (h + 1) * WTOK)
        bias32[rows, :] = bias_in[rows, :].astype(F32).T + penalty
    for load in loads[3:]:
        load.wait()
    x_halo.wait()
    x_halo.unpack(place_t, x_ref)

    scale = HEAD ** (-0.5)
    masks = head_masks()
    ga = ga_in[...]
    gm = gm_in[...]

    def forward():
        x = x_ref[...].astype(F32)
        unit, _ = normalize(x)
        normed_s[...] = (unit * ga).astype(BF16)
        qkv_s[...] = nn(normed_s[...], wqkv_in[...]).astype(BF16)
        for n in range(4):
            rows = slice(n * WTOK, (n + 1) * WTOK)
            q, k, v = split_heads(rows)
            km = jnp.concatenate([k * masks[h] for h in range(HEADS)], axis=0)
            vm = jnp.concatenate([v * masks[h] for h in range(HEADS)], axis=0)
            s = (nt(km, q) * scale + bias32[...]).reshape(HEADS, WTOK, WTOK)
            e = jnp.exp(s - jnp.max(s, axis=1, keepdims=True))
            p = e * (1.0 / jnp.sum(e, axis=1, keepdims=True))
            probs[n * HEADS:(n + 1) * HEADS] = p
            mixed = tn(p.astype(BF16).reshape(HEADS * WTOK, WTOK), vm)
            mixed_s[rows, :] = mixed.astype(BF16)

    def split_heads(rows):
        qkv = qkv_s[rows, :]
        return qkv[:, :C], qkv[:, C:2 * C], qkv[:, 2 * C:]

    def mlp():
        hidden = (x_ref[...].astype(F32) + nn(mixed_s[...], wproj_in[...])).astype(BF16)
        hid_s[...] = hidden
        unit, inv = normalize(hidden.astype(F32))
        nm_s[...] = (unit * gm).astype(BF16)
        grad_nm = jnp.zeros((TOK, C), F32)
        for f in range(3):
            cols = slice(f * 256, (f + 1) * 256)
            z = nn(nm_s[...], wup_in[:, cols])
            phi = 0.5 * (1.0 + lax.erf(z * (0.5 ** 0.5)))
            act_s[:, cols] = (z * phi).astype(BF16)
            slope = phi + z * (jnp.exp(-0.5 * z * z) * 0.3989422804014327)
            gpre = (nn(ct_ref[...], wdown_in[:, cols]) * slope).astype(BF16)
            gpre_s[:, cols] = gpre
            grad_nm = grad_nm + nt(gpre, wup_in[:, cols])
        grad_hidden = (ct_ref[...].astype(F32) + norm_back(unit, inv, gm, grad_nm)).astype(BF16)
        hid_grad_s[...] = grad_hidden
        gattn_s[...] = nt(grad_hidden, wproj_in[...]).astype(BF16)

    def attention_back(n):
        rows = slice(n * WTOK, (n + 1) * WTOK)
        q, k, v = split_heads(rows)
        up = gattn_s[rows, :]
        km = jnp.concatenate([k * masks[h] for h in range(HEADS)], axis=0)
        vm = jnp.concatenate([v * masks[h] for h in range(HEADS)], axis=0)
        p = probs[n * HEADS:(n + 1) * HEADS]
        gp = nt(vm, up).reshape(HEADS, WTOK, WTOK)
        inner = jnp.sum(p * gp, axis=1, keepdims=True)
        gs = (p * (gp - inner) * scale).astype(BF16).reshape(HEADS * WTOK, WTOK)
        gv_all = nn(p.astype(BF16).reshape(HEADS * WTOK, WTOK), up)
        gk_all = nn(gs, q)
        gq = tn(gs, km)
        gk = jnp.zeros((WTOK, C), F32)
        gv = jnp.zeros((WTOK, C), F32)
        for h in range(HEADS):
            gk = jnp.where(masks[h] > 0, gk_all[h * WTOK:(h + 1) * WTOK], gk)
            gv = jnp.where(masks[h] > 0, gv_all[h * WTOK:(h + 1) * WTOK], gv)
        gqkv_s[rows, :] = jnp.concatenate([gq, gk, gv], axis=1).astype(BF16)

    def output():
        out_ref[...] = (hid_s[...].astype(F32) + nt(act_s[...], wdown_in[...])).astype(BF16)

    def input_grad():
        grad_rolled = nt(gqkv_s[...], wqkv_in[...]).astype(BF16).astype(F32)
        unit, inv = normalize(x_ref[...].astype(F32))
        grad_x = norm_back(unit, inv, ga, grad_rolled)
        gx_ref[...] = (hid_grad_s[...].astype(F32) + grad_x).astype(BF16)

    def store_blocks(flat, base, values):
        for t in range(values.shape[1] // 128):
            flat[base + t * C:base + (t + 1) * C, :] = values[:, t * 128:(t + 1) * 128].astype(BF16)

    forward()
    ct_halo.wait()
    ct_halo.unpack(place_t, ct_ref)
    mlp()
    store_blocks(flat0, 0, tn(nm_s[...], gpre_s[...]))
    store_blocks(flat0, 6 * C, tn(ct_ref[...], act_s[...]))
    grad_proj = tn(mixed_s[...], hid_grad_s[...])
    store_blocks(flat0, 12 * C, grad_proj)
    mlp_sum.to_core()
    attention_back(0)
    attention_back(1)
    mlp_sum.to_plane()
    attention_back(2)
    attention_back(3)
    grad_qkv = tn(normed_s[...], gqkv_s[...])
    store_blocks(flat1, 0, grad_qkv)
    store_blocks(flat1, 4 * C, jnp.concatenate([grad_qkv[:, 512:], grad_proj[:, 128:]], axis=1))
    attn_sum.to_core()
    output()
    out_halo.pack(out_ref, place)
    attn_sum.to_plane()
    out_halo.start()
    input_grad()
    gx_halo.pack(gx_ref, place)
    gx_halo.start()
    mlp_sum.to_z()
    attn_sum.to_z()
    out_halo.wait()
    out_halo.unpack(pack_t, out_grid)
    mlp_sum.back_to_plane()
    attn_sum.back_to_plane()
    gx_halo.wait()
    gx_halo.unpack(pack_t, gx_grid)
    mlp_sum.back_to_core()
    attn_sum.back_to_core()
    mlp_sum.finish()
    attn_sum.finish()
    mlp_sum.drain()
    attn_sum.drain()


def sum_bufs(size):
    return [
        pltpu.VMEM((16 * size, 128), BF16),
        pltpu.VMEM((16 * size, 128), BF16),
        pltpu.VMEM((15, size, 128), BF16),
        pltpu.VMEM((8, size, 128), BF16),
    ]


def sum_sems():
    sem = pltpu.SemaphoreType.DMA
    one = pltpu.SemaphoreType.DMA
    counts = (15, 15, 7, 7, 15, 15, 16, 16)
    return [one, one] + [sem((count,)) for count in counts]


def block_call(x, ct, bias, gain_attn, w_qkv, w_proj, gain_mlp, w_up, w_down):
    shape = jax.ShapeDtypeStruct
    args = (x, ct, bias, gain_attn, w_qkv, w_proj, gain_mlp, w_up, w_down)
    sem = pltpu.SemaphoreType.DMA
    return pl.pallas_call(
        block_kernel,
        out_shape=(
            shape((TOK, C), BF16),
            shape((TOK, C), BF16),
            shape((ROWS[0], 128), BF16),
            shape((ROWS[1], 128), BF16),
        ),
        in_specs=[HBM] * 9,
        out_specs=(VMEM,) * 4,
        scratch_shapes=[
            *[pltpu.VMEM(arg.shape, arg.dtype) for arg in args], sem((9,)),
            pltpu.VMEM((PACKED, PAIR), BF16),
            pltpu.VMEM((PAIR, PACKED), BF16),
            pltpu.VMEM((PACKED, PAIR), BF16),
            pltpu.VMEM((PAIR, PACKED), BF16),
            pltpu.VMEM((TOK, C), BF16),
            pltpu.VMEM((TOK, C), BF16),
            pltpu.VMEM((TOK, C), BF16),
            pltpu.VMEM((TOK, C), BF16),
            pltpu.VMEM((HEADS * WTOK, WTOK), F32),
            pltpu.VMEM((4 * HEADS, WTOK, WTOK), F32),
            pltpu.VMEM((TOK, C), BF16),
            pltpu.VMEM((TOK, 3 * C), BF16),
            pltpu.VMEM((TOK, C), BF16),
            pltpu.VMEM((TOK, C), BF16),
            pltpu.VMEM((TOK, C), BF16),
            pltpu.VMEM((TOK, C), BF16),
            pltpu.VMEM((TOK, FF), BF16),
            pltpu.VMEM((TOK, FF), BF16),
            pltpu.VMEM((TOK, 3 * C), BF16),
            pltpu.VMEM((TOK, C), BF16),
            pltpu.VMEM((4, PACKED, 2 * C), BF16),
            pltpu.VMEM((4, PACKED - STAY, 2 * C), BF16),
            sem((4, 3)), sem((4, 3)),
            pltpu.VMEM((ROWS[0], 128), BF16),
            pltpu.VMEM((ROWS[1], 128), BF16),
            *sum_bufs(CHUNK[0]), *sum_bufs(CHUNK[1]),
            *sum_sems(), *sum_sems(),
        ],
        compiler_params=pltpu.CompilerParams(
            collective_id=0, has_side_effects=True, vmem_limit_bytes=56 * 2**20
        ),
        name="block",
    )(*args)


def finish_kernel(
    out_hbm, gx_hbm, full0_hbm, full1_hbm, wqkv_hbm, wup_hbm, gain_a_hbm, gain_m_hbm,
    out_ref, gx_ref, qkv_ref, proj_ref, up_ref, down_ref, ga_ref, gm_ref,
    full0, full1, wqkv, wup, gain_a, gain_m, sem,
):
    copies = []
    for i, (src, dst) in enumerate((
        (full1_hbm, full1), (full0_hbm, full0), (wqkv_hbm, wqkv), (wup_hbm, wup),
        (gain_a_hbm, gain_a), (gain_m_hbm, gain_m), (out_hbm, out_ref), (gx_hbm, gx_ref),
    )):
        copies.append(pltpu.make_async_copy(src, dst, sem.at[i]))
        copies[-1].start()

    def block(full, t):
        return full[t * C:(t + 1) * C, :].astype(F32) * FACTOR

    copies[0].wait()
    copies[1].wait()
    for t in range(4):
        qkv_ref[:, t * 128:(t + 1) * 128] = block(full1, t)
    mixed_tile = block(full1, 4)
    qkv_ref[:, 512:] = mixed_tile[:, :64]
    proj_ref[:, :128] = block(full0, 12)
    proj_ref[:, 128:] = mixed_tile[:, 64:]
    for t in range(6):
        up_ref[:, t * 128:(t + 1) * 128] = block(full0, t)
        down_ref[:, t * 128:(t + 1) * 128] = block(full0, 6 + t)
    for copy in copies[2:]:
        copy.wait()
    for weight, grad, gain, ref in ((wqkv, qkv_ref, gain_a, ga_ref), (wup, up_ref, gain_m, gm_ref)):
        product = weight[...].astype(F32) * grad[...]
        total = lax.dot_general(
            jnp.ones((8, product.shape[1]), F32), product, (((1,), (1,)), ((), ())),
            precision=lax.Precision.HIGHEST, preferred_element_type=F32,
        )
        ref[...] = total[:1] / gain[...]


def finish_call(out, gx, full0, full1, w_qkv, w_up, gain_attn, gain_mlp):
    shape = jax.ShapeDtypeStruct
    return pl.pallas_call(
        finish_kernel,
        out_shape=(
            shape((TOK, C), BF16),
            shape((TOK, C), BF16),
            shape((C, 3 * C), F32),
            shape((C, C), F32),
            shape((C, FF), F32),
            shape((C, FF), F32),
            shape((1, C), F32),
            shape((1, C), F32),
        ),
        in_specs=[HBM] * 8,
        out_specs=(VMEM,) * 8,
        scratch_shapes=[
            pltpu.VMEM((ROWS[0], 128), BF16),
            pltpu.VMEM((ROWS[1], 128), BF16),
            pltpu.VMEM((C, 3 * C), BF16),
            pltpu.VMEM((C, FF), BF16),
            pltpu.VMEM((1, C), F32),
            pltpu.VMEM((1, C), F32),
            pltpu.SemaphoreType.DMA((8,)),
        ],
        compiler_params=pltpu.CompilerParams(vmem_limit_bytes=56 * 2**20),
        name="finish",
    )(out, gx, full0, full1, w_qkv, w_up, gain_attn, gain_mlp)


def body(fields, gain_attn, w_qkv, bias, w_proj, gain_mlp, w_up, w_down, cotangent):
    out, gx, full0, full1 = block_call(
        fields.reshape(TOK, C), cotangent.reshape(TOK, C), bias.reshape(HEADS * WTOK, WTOK),
        gain_attn.reshape(1, C), w_qkv, w_proj, gain_mlp.reshape(1, C), w_up, w_down.T,
    )
    out, gx, qkv, proj, up, down, ga, gm = finish_call(
        out, gx, full0, full1, w_qkv, w_up, gain_attn.reshape(1, C), gain_mlp.reshape(1, C),
    )
    return (
        out.reshape(fields.shape), gx.reshape(fields.shape), qkv, proj, up, down.T,
        ga.reshape(C), gm.reshape(C),
    )


def solution(mesh):
    grid = P(None, "lat", "lon", None)
    in_specs = (grid, P(), P(), P("lat", None, None, None), P(), P(), P(), P(), grid)
    out_specs = (grid, grid, P(), P(), P(), P(), P(), P())
    return jax.shard_map(body, mesh=mesh, in_specs=in_specs, out_specs=out_specs, check_vma=False)
```

```python
import jax
import jax.numpy as jnp
from jax import lax
from jax.experimental import pallas as pl
from jax.experimental.pallas import tpu as pltpu
from jax.sharding import PartitionSpec as P

WLAT = 6
WLON = 12
WTOK = 144
HEADS = 6
HEAD = 32
C = 192
FF = 768
TOK = 576
NORM_EPS = 1e-05
MASKED = -1e30
FACTOR = 1.0 / 384.0

STAY = 112
PACKED = 320
PIECES = ((112, 112), (224, 48), (272, 48))
PAIR = 288

ROWS = (1536, 1024, 1024)

F32 = jnp.float32
BF16 = jnp.bfloat16
MESH = pl.DeviceIdType.MESH
VMEM = pl.BlockSpec(memory_space=pltpu.VMEM)
HBM = pl.BlockSpec(memory_space=pltpu.HBM)


def nn(left, right):
    return lax.dot_general(left, right, (((1,), (0,)), ((), ())), preferred_element_type=F32)


def nt(left, right):
    return lax.dot_general(left, right, (((1,), (1,)), ((), ())), preferred_element_type=F32)


def tn(left, right):
    return lax.dot_general(left, right, (((0,), (0,)), ((), ())), preferred_element_type=F32)


def row_mean(values):
    return jnp.sum(values, axis=-1, keepdims=True) * (1.0 / C)


def normalize(values):
    center = values - row_mean(values)
    inv = lax.rsqrt(row_mean(center * center) + NORM_EPS)
    return center * inv, inv


def norm_back(unit, inv, gain, upstream):
    scaled = upstream * gain
    grad = inv * (scaled - row_mean(scaled) - unit * row_mean(scaled * unit))
    return grad


def head_masks():
    head_of = lax.broadcasted_iota(jnp.int32, (1, C), 1) // HEAD
    return [jnp.where(head_of == h, 1.0, 0.0).astype(BF16) for h in range(HEADS)]


def piece_row(level, row, col):
    stay_row = row >= 3
    low = jnp.where(stay_row, row - 3, row)
    wide = level * 54 + low * 18 + col - 6
    thin = level * 18 + low * 6 + col
    right = jnp.where(stay_row, wide, wide + PIECES[0][0])
    left = jnp.where(stay_row, thin + PIECES[1][0], thin + PIECES[2][0])
    return jnp.where(col >= 6, right, left)


def pack_rows(token):
    return piece_row(token // 144, token % 144 // 24, token % 24)


def place_rows(token):
    col = token % WLON + token // 144 * WLON
    return piece_row(token % 144 // 72, (token % 72 // WLON + 3) % 6, (col + 6) % 24)


def table(rows_of):
    token = lax.broadcasted_iota(jnp.int32, (1, PAIR), 1)
    piece = lax.broadcasted_iota(jnp.int32, (PACKED, PAIR), 0)
    return jnp.where(piece == rows_of(token), 1.0, 0.0).astype(BF16)


def table_t(rows_of):
    token = lax.broadcasted_iota(jnp.int32, (PAIR, 1), 0)
    piece = lax.broadcasted_iota(jnp.int32, (PAIR, PACKED), 1)
    return jnp.where(piece == rows_of(token), 1.0, 0.0).astype(BF16)


def remote(src, dst, send_sem, recv_sem, device):
    return pltpu.make_async_remote_copy(
        src_ref=src, dst_ref=dst, send_sem=send_sem, recv_sem=recv_sem,
        device_id=device, device_id_type=MESH,
    )


def ring(index, step, size):
    return lax.rem(index + step + size, size)


def chunk(start, size):
    return pl.ds(pl.multiple_of(start, 16), size)


def near(steps, size):
    return sorted(steps, key=lambda step: sum(min(d, n - d) for d, n in zip(step, size)))


PLANE = near([(dy, dx) for dy in range(4) for dx in range(4) if (dy, dx) != (0, 0)], (4, 4))
RING = [dz for dz, in near([(dz,) for dz in range(1, 8)], (8,))]


class Place:
    def __init__(self):
        self.lon, self.lat = lax.axis_index("lon"), lax.axis_index("lat")
        self.core = lax.rem(self.lon, 2)
        self.x = lax.rem(self.lon // 2, 4)
        self.y = self.lat // 8 * 2 + self.lon // 8
        self.z = lax.rem(self.lat, 8)

    def device(self, y, x, z, core):
        return ((lax.rem(y, 2) * 4 + x) * 2 + core, y // 2 * 8 + z)

    def other_core(self):
        return self.device(self.y, self.x, self.z, 1 - self.core)

    def plane_spot(self, dy, dx):
        return ring(self.y, dy, 4), ring(self.x, dx, 4)

    def plane_peer(self, dy, dx):
        y, x = self.plane_spot(dy, dx)
        return self.device(y, x, self.z, self.core)

    def z_peer(self, dz):
        return self.device(self.y, self.x, ring(self.z, dz, 8), self.core)

    def halo_targets(self, step):
        lon, lat = ring(self.lon, step, 16), ring(self.lat, step, 16)
        return (self.lon, lat), (lon, self.lat), (lon, lat)

    def everyone(self):
        devices = list(self.halo_targets(1)) + list(self.halo_targets(-1)) + [self.other_core()]
        devices += [self.plane_peer(dy, dx) for dy, dx in PLANE]
        return devices + [self.z_peer(dz) for dz in range(1, 8)]


class Halo:
    def __init__(self, spot, packed, landed, send_sem, recv_sem, step):
        targets = spot.halo_targets(step)
        self.packed, self.landed = packed, landed
        self.copies = [
            remote(
                packed.at[pl.ds(start, size), :], landed.at[pl.ds(start - STAY, size), :],
                send_sem.at[i], recv_sem.at[i], targets[i],
            )
            for i, (start, size) in enumerate(PIECES)
        ]

    def start(self):
        for copy in self.copies:
            copy.start()

    def wait(self):
        for copy in self.copies:
            copy.wait()

    def pack(self, ref, table_ref):
        pairs = [ref[i * PAIR:(i + 1) * PAIR, :].astype(F32) for i in range(2)]
        both = jnp.concatenate(pairs, axis=1).astype(BF16)
        self.packed[...] = nn(table_ref[...], both).astype(BF16)

    def unpack(self, table_ref, ref):
        both = nn(table_ref[:, :STAY], self.packed[:STAY, :]) + nn(table_ref[:, STAY:], self.landed[...])
        for i in range(2):
            ref[i * PAIR:(i + 1) * PAIR, :] = both[:, i * C:(i + 1) * C].astype(BF16)


class Sum:
    def __init__(self, spot, flat, full, scratch):
        self.spot, self.flat, self.full = spot, flat, full
        (self.core_in, self.out, self.first_in, self.second_in, core, first_s, first_r,
         second_s, second_r, back_s, back_r, last_s, last_r) = scratch
        self.core_sems = core.at[0], core.at[1]
        self.first_sems, self.second_sems = (first_s, first_r), (second_s, second_r)
        self.back_sems, self.last_sems = (back_s, back_r), (last_s, last_r)
        self.size = self.first_in.shape[1]
        self.sent = []
        self.count = self.first_in.shape[0] + 1
        self.half = spot.core * (self.count * self.size)
        self.own = self.first_index(self.first_steps[-1], True) * self.size

    def launch(self, src, dst, sems, device, index=None):
        send_sem, recv_sem = sems if index is None else (sems[0].at[index], sems[1].at[index])
        copy = remote(src, dst, send_sem, recv_sem, device)
        copy.start()
        self.sent.append(copy)
        return copy

    def far_first(self, steps, make):
        copies = [make(k, steps[k]) for k in reversed(range(len(steps)))]
        return copies[::-1]

    def to_core(self):
        other = self.count * self.size - self.half
        self.core_copy = self.launch(
            self.flat.at[chunk(other, self.count * self.size)], self.core_in,
            self.core_sems, self.spot.other_core(),
        )

    def to_first(self):
        self.core_copy.wait_recv()
        mine = self.flat[chunk(self.half, self.count * self.size), :].astype(F32)
        self.out[...] = (mine + self.core_in[...].astype(F32)).astype(BF16)
        self.first_copies = self.far_first(self.first_steps, lambda k, step: self.launch(
            self.out.at[chunk(self.first_index(step) * self.size, self.size)],
            self.first_in.at[k], self.first_sems, self.first_peer(step), k,
        ))

    def to_second(self):
        total = self.out[chunk(self.own, self.size), :].astype(F32)
        for k, copy in enumerate(self.first_copies):
            copy.wait_recv()
            total = total + self.first_in[k].astype(F32)
        mine = self.second_in.at[self.second_here()]
        mine[...] = total.astype(BF16)
        self.second_copies = self.far_first(self.second_steps, lambda k, step: self.launch(
            mine, mine, self.second_sems, self.second_peer(step), k,
        ))

    def back_to_first(self):
        for copy in self.second_copies:
            copy.wait_recv()
        total = self.second_in[0].astype(F32)
        for i in range(1, len(self.second_steps) + 1):
            total = total + self.second_in[i].astype(F32)
        own = self.full.at[chunk(self.half + self.own, self.size)]
        own[...] = total.astype(BF16)
        self.back_copies = self.far_first(self.first_steps, lambda k, step: self.launch(
            own, own, self.back_sems, self.first_peer(step), k,
        ))

    def back_to_core(self):
        self.last_copies = []
        for k in range(self.count):
            start = self.own
            if k > 0:
                self.back_copies[k - 1].wait_recv()
                start = self.first_index(self.first_steps[k - 1], False, -1) * self.size
            rows = self.full.at[chunk(self.half + start, self.size)]
            self.last_copies.append(
                self.launch(rows, rows, self.last_sems, self.spot.other_core(), k)
            )

    def finish(self):
        for copy in self.last_copies:
            copy.wait_recv()

    def drain(self):
        for copy in self.sent:
            copy.wait_send()


class PlaneSum(Sum):
    first_steps, second_steps = PLANE, RING

    def first_index(self, step, here=False, sign=1):
        y, x = (self.spot.y, self.spot.x) if here else self.spot.plane_spot(sign * step[0], sign * step[1])
        return y * 4 + x

    def first_peer(self, step):
        return self.spot.plane_peer(*step)

    def second_here(self):
        return self.spot.z

    def second_peer(self, step):
        return self.spot.z_peer(step)


class RingSum(Sum):
    first_steps, second_steps = RING, PLANE

    def first_index(self, step, here=False, sign=1):
        return self.spot.z if here else ring(self.spot.z, sign * step, 8)

    def first_peer(self, step):
        return self.spot.z_peer(step)

    def second_here(self):
        return self.spot.y * 4 + self.spot.x

    def second_peer(self, step):
        return self.spot.plane_peer(*step)


def sum_scratch(kind, size):
    first, second = len(kind.first_steps), len(kind.second_steps)
    sem = pltpu.SemaphoreType.DMA
    return [
        pltpu.VMEM(((first + 1) * size, 128), BF16),
        pltpu.VMEM(((first + 1) * size, 128), BF16),
        pltpu.VMEM((first, size, 128), BF16),
        pltpu.VMEM((second + 1, size, 128), BF16),
        sem((2,)), sem((first,)), sem((first,)), sem((second,)), sem((second,)),
        sem((first,)), sem((first,)), sem((first + 1,)), sem((first + 1,)),
    ]


PARTS = ((PlaneSum, 48), (RingSum, 64), (PlaneSum, 32))


def block_kernel(
    x_hbm, ct_hbm, bias_hbm, ga_hbm, wqkv_hbm, wproj_hbm, gm_hbm, wup_hbm, wdown_hbm,
    out_grid, gx_grid, full0, full1, full2,
    x_in, ct_in, bias_in, ga_in, wqkv_in, wproj_in, gm_in, wup_in, wdown_in, load_sem,
    pack, pack_t, place, place_t,
    x_ref, ct_ref, out_ref, gx_ref, bias32, probs,
    normed_s, qkv_s, mixed_s, hid_s, hid_grad_s, nm_s, act_s, gpre_s, gqkv_s, gattn_s,
    packed, landed, halo_send, halo_recv, flat0, flat1, flat2, *sum_refs,
):
    spot = Place()
    loads = []
    for i, (src, dst) in enumerate((
        (x_hbm, x_in), (ct_hbm, ct_in), (bias_hbm, bias_in), (ga_hbm, ga_in), (wqkv_hbm, wqkv_in),
        (wproj_hbm, wproj_in), (gm_hbm, gm_in), (wup_hbm, wup_in), (wdown_hbm, wdown_in),
    )):
        loads.append(pltpu.make_async_copy(src, dst, load_sem.at[i]))
        loads[-1].start()
    barrier = pltpu.get_barrier_semaphore()
    devices = spot.everyone()
    for device in devices:
        pl.semaphore_signal(barrier, inc=1, device_id=device, device_id_type=MESH)
    halos = [
        Halo(spot, packed.at[a], landed.at[a], halo_send.at[a], halo_recv.at[a], step)
        for a, step in enumerate((-1, -1, 1, 1))
    ]
    x_halo, ct_halo, out_halo, gx_halo = halos
    sums = []
    for i, (kind, _) in enumerate(PARTS):
        flat, full = ((flat0, full0), (flat1, full1), (flat2, full2))[i]
        count = len(sum_refs) // len(PARTS)
        sums.append(kind(spot, flat, full, sum_refs[i * count:(i + 1) * count]))
    early, late = sums[:2], sums[2]

    pack[...] = table(pack_rows)
    loads[0].wait()
    x_halo.pack(x_in, pack)
    pl.semaphore_wait(barrier, len(devices))
    x_halo.start()
    pack_t[...] = table_t(pack_rows)
    flat1[5 * C:, :] = jnp.zeros((ROWS[1] - 5 * C, 128), BF16)
    flat2[5 * C:, :] = jnp.zeros((ROWS[2] - 5 * C, 128), BF16)
    place[...] = table(place_rows)
    place_t[...] = table_t(place_rows)
    loads[1].wait()
    ct_halo.pack(ct_in, pack)
    ct_halo.start()
    loads[2].wait()
    is_last = spot.lat == lax.axis_size("lat") - 1
    row_half = (lax.broadcasted_iota(jnp.int32, (WTOK, 1), 0) // WLON) % WLAT < WLAT // 2
    col_half = (lax.broadcasted_iota(jnp.int32, (1, WTOK), 1) // WLON) % WLAT < WLAT // 2
    cut = jnp.logical_and(row_half != col_half, is_last)
    penalty = jnp.where(cut, MASKED, 0.0)
    for h in range(HEADS):
        rows = slice(h * WTOK, (h + 1) * WTOK)
        bias32[rows, :] = bias_in[rows, :].astype(F32).T + penalty
    for load in loads[3:]:
        load.wait()
    x_halo.wait()
    x_halo.unpack(place_t, x_ref)

    scale = HEAD ** (-0.5)
    masks = head_masks()
    ga = ga_in[...]
    gm = gm_in[...]

    def forward():
        x = x_ref[...].astype(F32)
        unit, _ = normalize(x)
        normed_s[...] = (unit * ga).astype(BF16)
        qkv_s[...] = nn(normed_s[...], wqkv_in[...]).astype(BF16)
        for n in range(4):
            rows = slice(n * WTOK, (n + 1) * WTOK)
            q, k, v = split_heads(rows)
            km = jnp.concatenate([k * masks[h] for h in range(HEADS)], axis=0)
            vm = jnp.concatenate([v * masks[h] for h in range(HEADS)], axis=0)
            s = (nt(km, q) * scale + bias32[...]).reshape(HEADS, WTOK, WTOK)
            e = jnp.exp(s - jnp.max(s, axis=1, keepdims=True))
            p = e * (1.0 / jnp.sum(e, axis=1, keepdims=True))
            probs[n * HEADS:(n + 1) * HEADS] = p
            mixed = tn(p.astype(BF16).reshape(HEADS * WTOK, WTOK), vm)
            mixed_s[rows, :] = mixed.astype(BF16)

    def split_heads(rows):
        qkv = qkv_s[rows, :]
        return qkv[:, :C], qkv[:, C:2 * C], qkv[:, 2 * C:]

    def mlp():
        hidden = (x_ref[...].astype(F32) + nn(mixed_s[...], wproj_in[...])).astype(BF16)
        hid_s[...] = hidden
        unit, inv = normalize(hidden.astype(F32))
        nm_s[...] = (unit * gm).astype(BF16)
        grad_nm = jnp.zeros((TOK, C), F32)
        for f in range(3):
            cols = slice(f * 256, (f + 1) * 256)
            z = nn(nm_s[...], wup_in[:, cols])
            phi = 0.5 * (1.0 + lax.erf(z * (0.5 ** 0.5)))
            act_s[:, cols] = (z * phi).astype(BF16)
            slope = phi + z * (jnp.exp(-0.5 * z * z) * 0.3989422804014327)
            gpre = (nn(ct_ref[...], wdown_in[:, cols]) * slope).astype(BF16)
            gpre_s[:, cols] = gpre
            grad_nm = grad_nm + nt(gpre, wup_in[:, cols])
        grad_hidden = (ct_ref[...].astype(F32) + norm_back(unit, inv, gm, grad_nm)).astype(BF16)
        hid_grad_s[...] = grad_hidden
        gattn_s[...] = nt(grad_hidden, wproj_in[...]).astype(BF16)

    def attention_back(n):
        rows = slice(n * WTOK, (n + 1) * WTOK)
        q, k, v = split_heads(rows)
        up = gattn_s[rows, :]
        km = jnp.concatenate([k * masks[h] for h in range(HEADS)], axis=0)
        vm = jnp.concatenate([v * masks[h] for h in range(HEADS)], axis=0)
        p = probs[n * HEADS:(n + 1) * HEADS]
        gp = nt(vm, up).reshape(HEADS, WTOK, WTOK)
        inner = jnp.sum(p * gp, axis=1, keepdims=True)
        gs = (p * (gp - inner) * scale).astype(BF16).reshape(HEADS * WTOK, WTOK)
        gv_all = nn(p.astype(BF16).reshape(HEADS * WTOK, WTOK), up)
        gk_all = nn(gs, q)
        gq = tn(gs, km)
        gk = jnp.zeros((WTOK, C), F32)
        gv = jnp.zeros((WTOK, C), F32)
        for h in range(HEADS):
            gk = jnp.where(masks[h] > 0, gk_all[h * WTOK:(h + 1) * WTOK], gk)
            gv = jnp.where(masks[h] > 0, gv_all[h * WTOK:(h + 1) * WTOK], gv)
        gqkv_s[rows, :] = jnp.concatenate([gq, gk, gv], axis=1).astype(BF16)

    def output():
        out_ref[...] = (hid_s[...].astype(F32) + nt(act_s[...], wdown_in[...])).astype(BF16)

    def input_grad():
        grad_rolled = nt(gqkv_s[...], wqkv_in[...]).astype(BF16).astype(F32)
        unit, inv = normalize(x_ref[...].astype(F32))
        grad_x = norm_back(unit, inv, ga, grad_rolled)
        gx_ref[...] = (hid_grad_s[...].astype(F32) + grad_x).astype(BF16)

    def store_blocks(flat, base, values):
        for t in range(values.shape[1] // 128):
            flat[base + t * C:base + (t + 1) * C, :] = values[:, t * 128:(t + 1) * 128].astype(BF16)

    forward()
    ct_halo.wait()
    ct_halo.unpack(place_t, ct_ref)
    mlp()
    grad_up = tn(nm_s[...], gpre_s[...])
    grad_proj = tn(mixed_s[...], hid_grad_s[...])
    store_blocks(flat1, 0, grad_up[:, :640])
    store_blocks(flat0, 0, tn(ct_ref[...], act_s[...]))
    store_blocks(flat0, 6 * C, grad_proj)
    store_blocks(flat0, 7 * C, grad_up[:, 640:])
    for part in early:
        part.to_core()
    attention_back(0)
    attention_back(1)
    for part in early:
        part.to_first()
    attention_back(2)
    attention_back(3)
    grad_qkv = tn(normed_s[...], gqkv_s[...])
    store_blocks(flat2, 0, grad_qkv)
    store_blocks(flat2, 4 * C, jnp.concatenate([grad_qkv[:, 512:], grad_proj[:, 128:]], axis=1))
    late.to_core()
    output()
    out_halo.pack(out_ref, place)
    late.to_first()
    input_grad()
    gx_halo.pack(gx_ref, place)
    out_halo.start()
    gx_halo.start()
    for part in sums:
        part.to_second()
    out_halo.wait()
    out_halo.unpack(pack_t, out_grid)
    for part in sums:
        part.back_to_first()
    gx_halo.wait()
    gx_halo.unpack(pack_t, gx_grid)
    for part in sums:
        part.back_to_core()
    for part in sums:
        part.finish()
    for part in sums:
        part.drain()


def block_call(x, ct, bias, gain_attn, w_qkv, w_proj, gain_mlp, w_up, w_down):
    shape = jax.ShapeDtypeStruct
    args = (x, ct, bias, gain_attn, w_qkv, w_proj, gain_mlp, w_up, w_down)
    sem = pltpu.SemaphoreType.DMA
    return pl.pallas_call(
        block_kernel,
        out_shape=(
            shape((TOK, C), BF16),
            shape((TOK, C), BF16),
            *[shape((rows, 128), BF16) for rows in ROWS],
        ),
        in_specs=[HBM] * 9,
        out_specs=(VMEM,) * 5,
        scratch_shapes=[
            *[pltpu.VMEM(arg.shape, arg.dtype) for arg in args], sem((9,)),
            pltpu.VMEM((PACKED, PAIR), BF16),
            pltpu.VMEM((PAIR, PACKED), BF16),
            pltpu.VMEM((PACKED, PAIR), BF16),
            pltpu.VMEM((PAIR, PACKED), BF16),
            pltpu.VMEM((TOK, C), BF16),
            pltpu.VMEM((TOK, C), BF16),
            pltpu.VMEM((TOK, C), BF16),
            pltpu.VMEM((TOK, C), BF16),
            pltpu.VMEM((HEADS * WTOK, WTOK), F32),
            pltpu.VMEM((4 * HEADS, WTOK, WTOK), F32),
            pltpu.VMEM((TOK, C), BF16),
            pltpu.VMEM((TOK, 3 * C), BF16),
            pltpu.VMEM((TOK, C), BF16),
            pltpu.VMEM((TOK, C), BF16),
            pltpu.VMEM((TOK, C), BF16),
            pltpu.VMEM((TOK, C), BF16),
            pltpu.VMEM((TOK, FF), BF16),
            pltpu.VMEM((TOK, FF), BF16),
            pltpu.VMEM((TOK, 3 * C), BF16),
            pltpu.VMEM((TOK, C), BF16),
            pltpu.VMEM((4, PACKED, 2 * C), BF16),
            pltpu.VMEM((4, PACKED - STAY, 2 * C), BF16),
            sem((4, 3)), sem((4, 3)),
            *[pltpu.VMEM((rows, 128), BF16) for rows in ROWS],
            *[ref for kind, size in PARTS for ref in sum_scratch(kind, size)],
        ],
        compiler_params=pltpu.CompilerParams(
            collective_id=0, has_side_effects=True, vmem_limit_bytes=56 * 2**20
        ),
        name="block",
    )(*args)


def finish_kernel(
    out_hbm, gx_hbm, full0_hbm, full1_hbm, full2_hbm, wqkv_hbm, wup_hbm, gain_a_hbm, gain_m_hbm,
    out_ref, gx_ref, qkv_ref, proj_ref, up_ref, down_ref, ga_ref, gm_ref,
    full0, full1, full2, wqkv, wup, gain_a, gain_m, sem,
):
    copies = []
    for i, (src, dst) in enumerate((
        (full0_hbm, full0), (full1_hbm, full1), (full2_hbm, full2), (wqkv_hbm, wqkv), (wup_hbm, wup),
        (gain_a_hbm, gain_a), (gain_m_hbm, gain_m), (out_hbm, out_ref), (gx_hbm, gx_ref),
    )):
        copies.append(pltpu.make_async_copy(src, dst, sem.at[i]))
        copies[-1].start()

    def block(full, t):
        return full[t * C:(t + 1) * C, :].astype(F32) * FACTOR

    for copy in copies[:3]:
        copy.wait()
    for t in range(4):
        qkv_ref[:, t * 128:(t + 1) * 128] = block(full2, t)
    mixed_tile = block(full2, 4)
    qkv_ref[:, 512:] = mixed_tile[:, :64]
    proj_ref[:, :128] = block(full0, 6)
    proj_ref[:, 128:] = mixed_tile[:, 64:]
    for t in range(6):
        up_ref[:, t * 128:(t + 1) * 128] = block(full1, t) if t < 5 else block(full0, 7)
        down_ref[:, t * 128:(t + 1) * 128] = block(full0, t)
    for copy in copies[3:]:
        copy.wait()
    for weight, grad, gain, ref in ((wqkv, qkv_ref, gain_a, ga_ref), (wup, up_ref, gain_m, gm_ref)):
        product = weight[...].astype(F32) * grad[...]
        total = lax.dot_general(
            jnp.ones((8, product.shape[1]), F32), product, (((1,), (1,)), ((), ())),
            precision=lax.Precision.HIGHEST, preferred_element_type=F32,
        )
        ref[...] = total[:1] / gain[...]


def finish_call(out, gx, full, w_qkv, w_up, gain_attn, gain_mlp):
    shape = jax.ShapeDtypeStruct
    return pl.pallas_call(
        finish_kernel,
        out_shape=(
            shape((TOK, C), BF16),
            shape((TOK, C), BF16),
            shape((C, 3 * C), F32),
            shape((C, C), F32),
            shape((C, FF), F32),
            shape((C, FF), F32),
            shape((1, C), F32),
            shape((1, C), F32),
        ),
        in_specs=[HBM] * 9,
        out_specs=(VMEM,) * 8,
        scratch_shapes=[
            *[pltpu.VMEM((rows, 128), BF16) for rows in ROWS],
            pltpu.VMEM((C, 3 * C), BF16),
            pltpu.VMEM((C, FF), BF16),
            pltpu.VMEM((1, C), F32),
            pltpu.VMEM((1, C), F32),
            pltpu.SemaphoreType.DMA((9,)),
        ],
        compiler_params=pltpu.CompilerParams(vmem_limit_bytes=56 * 2**20),
        name="finish",
    )(out, gx, *full, w_qkv, w_up, gain_attn, gain_mlp)


def body(fields, gain_attn, w_qkv, bias, w_proj, gain_mlp, w_up, w_down, cotangent):
    out, gx, *full = block_call(
        fields.reshape(TOK, C), cotangent.reshape(TOK, C), bias.reshape(HEADS * WTOK, WTOK),
        gain_attn.reshape(1, C), w_qkv, w_proj, gain_mlp.reshape(1, C), w_up, w_down.T,
    )
    out, gx, qkv, proj, up, down, ga, gm = finish_call(
        out, gx, full, w_qkv, w_up, gain_attn.reshape(1, C), gain_mlp.reshape(1, C),
    )
    return (
        out.reshape(fields.shape), gx.reshape(fields.shape), qkv, proj, up, down.T,
        ga.reshape(C), gm.reshape(C),
    )


def solution(mesh):
    grid = P(None, "lat", "lon", None)
    in_specs = (grid, P(), P(), P("lat", None, None, None), P(), P(), P(), P(), grid)
    out_specs = (grid, grid, P(), P(), P(), P(), P(), P())
    return jax.shard_map(body, mesh=mesh, in_specs=in_specs, out_specs=out_specs, check_vma=False)
```

```python
import jax
import jax.numpy as jnp
from jax import lax
from jax.experimental import pallas as pl
from jax.experimental.pallas import tpu as pltpu
from jax.sharding import PartitionSpec as P

WLAT = 6
WLON = 12
WTOK = 144
HEADS = 6
HEAD = 32
C = 192
FF = 768
TOK = 576
NORM_EPS = 1e-05
MASKED = -1e30
FACTOR = 1.0 / 384.0

STAY = 112
PACKED = 320
PIECES = ((112, 112), (224, 48), (272, 48))
PAIR = 288

ROWS = (1536, 1024, 1024)

F32 = jnp.float32
BF16 = jnp.bfloat16
MESH = pl.DeviceIdType.MESH
VMEM = pl.BlockSpec(memory_space=pltpu.VMEM)
HBM = pl.BlockSpec(memory_space=pltpu.HBM)


def nn(left, right):
    return lax.dot_general(left, right, (((1,), (0,)), ((), ())), preferred_element_type=F32)


def nt(left, right):
    return lax.dot_general(left, right, (((1,), (1,)), ((), ())), preferred_element_type=F32)


def tn(left, right):
    return lax.dot_general(left, right, (((0,), (0,)), ((), ())), preferred_element_type=F32)


def row_mean(values):
    return jnp.sum(values, axis=-1, keepdims=True) * (1.0 / C)


def normalize(values):
    center = values - row_mean(values)
    inv = lax.rsqrt(row_mean(center * center) + NORM_EPS)
    return center * inv, inv


def norm_back(unit, inv, gain, upstream):
    scaled = upstream * gain
    grad = inv * (scaled - row_mean(scaled) - unit * row_mean(scaled * unit))
    return grad


def head_masks():
    head_of = lax.broadcasted_iota(jnp.int32, (1, C), 1) // HEAD
    return [jnp.where(head_of == h, 1.0, 0.0).astype(BF16) for h in range(HEADS)]


def piece_row(level, row, col):
    stay_row = row >= 3
    low = jnp.where(stay_row, row - 3, row)
    wide = level * 54 + low * 18 + col - 6
    thin = level * 18 + low * 6 + col
    right = jnp.where(stay_row, wide, wide + PIECES[0][0])
    left = jnp.where(stay_row, thin + PIECES[1][0], thin + PIECES[2][0])
    return jnp.where(col >= 6, right, left)


def pack_rows(token):
    return piece_row(token // 144, token % 144 // 24, token % 24)


def place_rows(token):
    col = token % WLON + token // 144 * WLON
    return piece_row(token % 144 // 72, (token % 72 // WLON + 3) % 6, (col + 6) % 24)


def table(rows_of):
    token = lax.broadcasted_iota(jnp.int32, (1, PAIR), 1)
    piece = lax.broadcasted_iota(jnp.int32, (PACKED, PAIR), 0)
    return jnp.where(piece == rows_of(token), 1.0, 0.0).astype(BF16)


def table_t(rows_of):
    token = lax.broadcasted_iota(jnp.int32, (PAIR, 1), 0)
    piece = lax.broadcasted_iota(jnp.int32, (PAIR, PACKED), 1)
    return jnp.where(piece == rows_of(token), 1.0, 0.0).astype(BF16)


def remote(src, dst, send_sem, recv_sem, device):
    return pltpu.make_async_remote_copy(
        src_ref=src, dst_ref=dst, send_sem=send_sem, recv_sem=recv_sem,
        device_id=device, device_id_type=MESH,
    )


def ring(index, step, size):
    return lax.rem(index + step + size, size)


def chunk(start, size):
    return pl.ds(pl.multiple_of(start, 16), size)


def near(steps, size):
    return sorted(steps, key=lambda step: sum(min(d, n - d) for d, n in zip(step, size)))


PLANE = near([(dy, dx) for dy in range(4) for dx in range(4) if (dy, dx) != (0, 0)], (4, 4))
RING = [dz for dz, in near([(dz,) for dz in range(1, 8)], (8,))]


class Place:
    def __init__(self):
        self.lon, self.lat = lax.axis_index("lon"), lax.axis_index("lat")
        self.core = lax.rem(self.lon, 2)
        self.x = lax.rem(self.lon // 2, 4)
        self.y = self.lat // 8 * 2 + self.lon // 8
        self.z = lax.rem(self.lat, 8)

    def device(self, y, x, z, core):
        return ((lax.rem(y, 2) * 4 + x) * 2 + core, y // 2 * 8 + z)

    def other_core(self):
        return self.device(self.y, self.x, self.z, 1 - self.core)

    def plane_spot(self, dy, dx):
        return ring(self.y, dy, 4), ring(self.x, dx, 4)

    def plane_peer(self, dy, dx):
        y, x = self.plane_spot(dy, dx)
        return self.device(y, x, self.z, self.core)

    def z_peer(self, dz):
        return self.device(self.y, self.x, ring(self.z, dz, 8), self.core)

    def halo_targets(self, step):
        lon, lat = ring(self.lon, step, 16), ring(self.lat, step, 16)
        return (self.lon, lat), (lon, self.lat), (lon, lat)

    def everyone(self):
        devices = list(self.halo_targets(-1)) + list(self.halo_targets(1)) + [self.other_core()]
        devices += [self.plane_peer(dy, dx) for dy, dx in PLANE]
        return devices + [self.z_peer(dz) for dz in range(1, 8)]


class Halo:
    def __init__(self, spot, packed, landed, send_sem, recv_sem, step):
        targets = spot.halo_targets(step)
        self.packed, self.landed = packed, landed
        self.copies = [
            remote(
                packed.at[pl.ds(start, size), :], landed.at[pl.ds(start - STAY, size), :],
                send_sem.at[i], recv_sem.at[i], targets[i],
            )
            for i, (start, size) in enumerate(PIECES)
        ]

    def start(self):
        for copy in self.copies:
            copy.start()

    def wait(self):
        for copy in self.copies:
            copy.wait()

    def pack(self, ref, table_ref):
        pairs = [ref[i * PAIR:(i + 1) * PAIR, :].astype(F32) for i in range(2)]
        both = jnp.concatenate(pairs, axis=1).astype(BF16)
        self.packed[...] = nn(table_ref[...], both).astype(BF16)

    def unpack(self, table_ref, ref):
        both = nn(table_ref[:, :STAY], self.packed[:STAY, :]) + nn(table_ref[:, STAY:], self.landed[...])
        for i in range(2):
            ref[i * PAIR:(i + 1) * PAIR, :] = both[:, i * C:(i + 1) * C].astype(BF16)


class Sum:
    def __init__(self, spot, flat, full, scratch):
        self.spot, self.flat, self.full = spot, flat, full
        (self.core_in, self.out, self.first_in, self.second_in, core, first_s, first_r,
         second_s, second_r, back_s, back_r, last) = scratch
        self.core_sems = core.at[0], core.at[1]
        self.first_sems, self.second_sems = (first_s, first_r), (second_s, second_r)
        self.back_sems, self.last_sems = (back_s, back_r), (last.at[0], last.at[1])
        self.size = self.first_in.shape[1]
        self.sent = []
        self.count = self.first_in.shape[0] + 1
        self.half = spot.core * (self.count * self.size)
        self.own = self.first_here() * self.size

    def launch(self, src, dst, sems, device, index=None):
        send_sem, recv_sem = sems if index is None else (sems[0].at[index], sems[1].at[index])
        copy = remote(src, dst, send_sem, recv_sem, device)
        copy.start()
        self.sent.append(copy)
        return copy

    def far_first(self, steps, make):
        copies = [make(k, steps[k]) for k in reversed(range(len(steps)))]
        return copies[::-1]

    def to_core(self):
        other = self.count * self.size - self.half
        self.core_copy = self.launch(
            self.flat.at[chunk(other, self.count * self.size)], self.core_in,
            self.core_sems, self.spot.other_core(),
        )

    def to_first(self):
        self.core_copy.wait_recv()
        mine = self.flat[chunk(self.half, self.count * self.size), :].astype(F32)
        self.out[...] = (mine + self.core_in[...].astype(F32)).astype(BF16)
        self.first_copies = self.far_first(self.first_steps, lambda k, step: self.launch(
            self.out.at[chunk(self.first_index(step) * self.size, self.size)],
            self.first_in.at[k], self.first_sems, self.first_peer(step), k,
        ))

    def to_second(self):
        total = self.out[chunk(self.own, self.size), :].astype(F32)
        for k, copy in enumerate(self.first_copies):
            copy.wait_recv()
            total = total + self.first_in[k].astype(F32)
        mine = self.second_in.at[self.second_here()]
        mine[...] = total.astype(BF16)
        self.second_copies = self.far_first(self.second_steps, lambda k, step: self.launch(
            mine, mine, self.second_sems, self.second_peer(step), k,
        ))

    def back_to_first(self):
        for copy in self.second_copies:
            copy.wait_recv()
        total = self.second_in[0].astype(F32)
        for i in range(1, len(self.second_steps) + 1):
            total = total + self.second_in[i].astype(F32)
        own = self.full.at[chunk(self.half + self.own, self.size)]
        own[...] = total.astype(BF16)
        self.back_copies = self.far_first(self.first_steps, lambda k, step: self.launch(
            own, own, self.back_sems, self.first_peer(step), k,
        ))

    def back_to_core(self):
        for copy in self.back_copies:
            copy.wait_recv()
        rows = self.full.at[chunk(self.half, self.count * self.size)]
        self.last_copy = self.launch(rows, rows, self.last_sems, self.spot.other_core())

    def finish(self):
        self.last_copy.wait_recv()

    def drain(self):
        for copy in self.sent:
            copy.wait_send()


class PlaneSum(Sum):
    first_steps, second_steps = PLANE, RING

    def first_here(self):
        return self.spot.y * 4 + self.spot.x

    def first_index(self, step):
        y, x = self.spot.plane_spot(*step)
        return y * 4 + x

    def first_peer(self, step):
        return self.spot.plane_peer(*step)

    def second_here(self):
        return self.spot.z

    def second_peer(self, step):
        return self.spot.z_peer(step)


class RingSum(Sum):
    first_steps, second_steps = RING, PLANE

    def first_here(self):
        return self.spot.z

    def first_index(self, step):
        return ring(self.spot.z, step, 8)

    def first_peer(self, step):
        return self.spot.z_peer(step)

    def second_here(self):
        return self.spot.y * 4 + self.spot.x

    def second_peer(self, step):
        return self.spot.plane_peer(*step)


def sum_scratch(kind, size):
    first, second = len(kind.first_steps), len(kind.second_steps)
    sem = pltpu.SemaphoreType.DMA
    return [
        pltpu.VMEM(((first + 1) * size, 128), BF16),
        pltpu.VMEM(((first + 1) * size, 128), BF16),
        pltpu.VMEM((first, size, 128), BF16),
        pltpu.VMEM((second + 1, size, 128), BF16),
        sem((2,)), sem((first,)), sem((first,)), sem((second,)), sem((second,)),
        sem((first,)), sem((first,)), sem((2,)),
    ]


PARTS = ((PlaneSum, 48), (RingSum, 64), (PlaneSum, 32))


def block_kernel(
    x_hbm, ct_hbm, bias_hbm, ga_hbm, wqkv_hbm, wproj_hbm, gm_hbm, wup_hbm, wdown_hbm,
    out_grid, gx_grid, full0, full1, full2,
    x_in, ct_in, bias_in, ga_in, wqkv_in, wproj_in, gm_in, wup_in, wdown_in, load_sem,
    pack, pack_t, place, place_t,
    x_ref, ct_ref, out_ref, gx_ref, bias32, probs, weights, km_s, vm_s, q_s,
    normed_t, nm_t, mixed_t, ct_t, mixed_s, hid_s, hid_grad_s, nm_s, act_s, gpre_s, gqkv_s, gattn_s,
    packed, landed, halo_send, halo_recv, flat0, flat1, flat2, *sum_refs,
):
    spot = Place()
    barrier = pltpu.get_barrier_semaphore()
    devices = spot.everyone()
    for device in devices[:6]:
        pl.semaphore_signal(barrier, inc=1, device_id=device, device_id_type=MESH)
    loads = []
    for i, (src, dst) in enumerate((
        (x_hbm, x_in), (ct_hbm, ct_in), (bias_hbm, bias_in), (ga_hbm, ga_in), (wqkv_hbm, wqkv_in),
        (wproj_hbm, wproj_in), (gm_hbm, gm_in), (wup_hbm, wup_in), (wdown_hbm, wdown_in),
    )):
        loads.append(pltpu.make_async_copy(src, dst, load_sem.at[i]))
        loads[-1].start()
    for device in devices[6:]:
        pl.semaphore_signal(barrier, inc=1, device_id=device, device_id_type=MESH)
    halos = [
        Halo(spot, packed.at[a], landed.at[a], halo_send.at[a], halo_recv.at[a], step)
        for a, step in enumerate((-1, -1, 1, 1))
    ]
    x_halo, ct_halo, out_halo, gx_halo = halos
    sums = []
    for i, (kind, _) in enumerate(PARTS):
        flat, full = ((flat0, full0), (flat1, full1), (flat2, full2))[i]
        count = len(sum_refs) // len(PARTS)
        sums.append(kind(spot, flat, full, sum_refs[i * count:(i + 1) * count]))
    early, late = sums[:2], sums[2]

    pack[...] = table(pack_rows)
    loads[0].wait()
    x_halo.pack(x_in, pack)
    pl.semaphore_wait(barrier, len(devices))
    x_halo.start()
    pack_t[...] = table_t(pack_rows)
    flat1[5 * C:, :] = jnp.zeros((ROWS[1] - 5 * C, 128), BF16)
    flat2[5 * C:, :] = jnp.zeros((ROWS[2] - 5 * C, 128), BF16)
    place[...] = table(place_rows)
    place_t[...] = table_t(place_rows)
    loads[1].wait()
    ct_halo.pack(ct_in, pack)
    ct_halo.start()
    loads[2].wait()
    is_last = spot.lat == lax.axis_size("lat") - 1
    row_half = (lax.broadcasted_iota(jnp.int32, (WTOK, 1), 0) // WLON) % WLAT < WLAT // 2
    col_half = (lax.broadcasted_iota(jnp.int32, (1, WTOK), 1) // WLON) % WLAT < WLAT // 2
    cut = jnp.logical_and(row_half != col_half, is_last)
    penalty = jnp.where(cut, MASKED, 0.0)
    for h in range(HEADS):
        rows = slice(h * WTOK, (h + 1) * WTOK)
        bias32[rows, :] = bias_in[rows, :].astype(F32).T + penalty
    for load in loads[3:]:
        load.wait()
    x_halo.wait()
    x_halo.unpack(place_t, x_ref)

    scale = HEAD ** (-0.5)
    masks = head_masks()
    ga = ga_in[...]
    gm = gm_in[...]

    def forward():
        x = x_ref[...].astype(F32)
        unit, _ = normalize(x)
        normed = (unit * ga).astype(BF16)
        normed_t[...] = normed.T
        qkv = nn(normed, wqkv_in[...]).astype(BF16)
        q_s[...] = qkv[:, :C]
        k = qkv[:, C:2 * C]
        v = qkv[:, 2 * C:]
        for n in range(4):
            rows = slice(n * WTOK, (n + 1) * WTOK)
            km = jnp.concatenate([k[rows] * masks[h] for h in range(HEADS)], axis=0)
            vm = jnp.concatenate([v[rows] * masks[h] for h in range(HEADS)], axis=0)
            km_s[n] = km
            vm_s[n] = vm
            s = (nt(km, q_s[rows, :]) * scale + bias32[...]).reshape(HEADS, WTOK, WTOK)
            e = jnp.exp(s - jnp.max(s, axis=1, keepdims=True))
            p = e * (1.0 / jnp.sum(e, axis=1, keepdims=True))
            probs[n * HEADS:(n + 1) * HEADS] = p
            weights[n] = p.astype(BF16).reshape(HEADS * WTOK, WTOK)
            mixed_s[rows, :] = tn(weights[n], vm).astype(BF16)

    def mlp():
        hidden = (x_ref[...].astype(F32) + nn(mixed_s[...], wproj_in[...])).astype(BF16)
        hid_s[...] = hidden
        unit, inv = normalize(hidden.astype(F32))
        nm_s[...] = (unit * gm).astype(BF16)
        nm_t[...] = nm_s[...].T
        grad_nm = jnp.zeros((TOK, C), F32)
        for f in range(3):
            cols = slice(f * 256, (f + 1) * 256)
            z = nn(nm_s[...], wup_in[:, cols])
            phi = 0.5 * (1.0 + lax.erf(z * (0.5 ** 0.5)))
            act_s[:, cols] = (z * phi).astype(BF16)
            slope = phi + z * (jnp.exp(-0.5 * z * z) * 0.3989422804014327)
            gpre = (nn(ct_ref[...], wdown_in[:, cols]) * slope).astype(BF16)
            gpre_s[:, cols] = gpre
            grad_nm = grad_nm + nt(gpre, wup_in[:, cols])
        grad_hidden = (ct_ref[...].astype(F32) + norm_back(unit, inv, gm, grad_nm)).astype(BF16)
        hid_grad_s[...] = grad_hidden
        gattn_s[...] = nt(grad_hidden, wproj_in[...]).astype(BF16)

    def attention_back(n):
        rows = slice(n * WTOK, (n + 1) * WTOK)
        up = gattn_s[rows, :]
        p = probs[n * HEADS:(n + 1) * HEADS]
        gp = nt(vm_s[n], up).reshape(HEADS, WTOK, WTOK)
        inner = jnp.sum(p * gp, axis=1, keepdims=True)
        gs = (p * (gp - inner) * scale).astype(BF16).reshape(HEADS * WTOK, WTOK)
        gv_all = nn(weights[n], up)
        gk_all = nn(gs, q_s[rows, :])
        gq = tn(gs, km_s[n])
        gk = jnp.zeros((WTOK, C), F32)
        gv = jnp.zeros((WTOK, C), F32)
        for h in range(HEADS):
            gk = jnp.where(masks[h] > 0, gk_all[h * WTOK:(h + 1) * WTOK], gk)
            gv = jnp.where(masks[h] > 0, gv_all[h * WTOK:(h + 1) * WTOK], gv)
        gqkv_s[rows, :] = jnp.concatenate([gq, gk, gv], axis=1).astype(BF16)

    def output():
        out_ref[...] = (hid_s[...].astype(F32) + nt(act_s[...], wdown_in[...])).astype(BF16)

    def input_grad():
        grad_rolled = nt(gqkv_s[...], wqkv_in[...]).astype(BF16).astype(F32)
        unit, inv = normalize(x_ref[...].astype(F32))
        grad_x = norm_back(unit, inv, ga, grad_rolled)
        gx_ref[...] = (hid_grad_s[...].astype(F32) + grad_x).astype(BF16)

    def store_blocks(flat, base, values):
        for t in range(values.shape[1] // 128):
            flat[base + t * C:base + (t + 1) * C, :] = values[:, t * 128:(t + 1) * 128].astype(BF16)

    forward()
    mixed_t[...] = mixed_s[...].T
    ct_halo.wait()
    ct_halo.unpack(place_t, ct_ref)
    ct_t[...] = ct_ref[...].T
    mlp()
    grad_up = nn(nm_t[...], gpre_s[...])
    grad_proj = nn(mixed_t[...], hid_grad_s[...])
    store_blocks(flat1, 0, grad_up[:, :640])
    store_blocks(flat0, 0, nn(ct_t[...], act_s[...]))
    store_blocks(flat0, 6 * C, grad_proj)
    store_blocks(flat0, 7 * C, grad_up[:, 640:])
    for part in early:
        part.to_core()
    attention_back(0)
    attention_back(1)
    for part in early:
        part.to_first()
    attention_back(2)
    attention_back(3)
    grad_qkv = nn(normed_t[...], gqkv_s[...])
    store_blocks(flat2, 0, grad_qkv)
    store_blocks(flat2, 4 * C, jnp.concatenate([grad_qkv[:, 512:], grad_proj[:, 128:]], axis=1))
    late.to_core()
    late.to_first()
    output()
    out_halo.pack(out_ref, place)
    input_grad()
    gx_halo.pack(gx_ref, place)
    out_halo.start()
    gx_halo.start()
    for part in sums:
        part.to_second()
    out_halo.wait()
    out_halo.unpack(pack_t, out_grid)
    for part in sums:
        part.back_to_first()
    gx_halo.wait()
    gx_halo.unpack(pack_t, gx_grid)
    for part in sums:
        part.back_to_core()
    for part in sums:
        part.finish()
    for part in sums:
        part.drain()


def block_call(x, ct, bias, gain_attn, w_qkv, w_proj, gain_mlp, w_up, w_down):
    shape = jax.ShapeDtypeStruct
    args = (x, ct, bias, gain_attn, w_qkv, w_proj, gain_mlp, w_up, w_down)
    sem = pltpu.SemaphoreType.DMA
    return pl.pallas_call(
        block_kernel,
        out_shape=(
            shape((TOK, C), BF16),
            shape((TOK, C), BF16),
            *[shape((rows, 128), BF16) for rows in ROWS],
        ),
        in_specs=[HBM] * 9,
        out_specs=(VMEM,) * 5,
        scratch_shapes=[
            *[pltpu.VMEM(arg.shape, arg.dtype) for arg in args], sem((9,)),
            pltpu.VMEM((PACKED, PAIR), BF16),
            pltpu.VMEM((PAIR, PACKED), BF16),
            pltpu.VMEM((PACKED, PAIR), BF16),
            pltpu.VMEM((PAIR, PACKED), BF16),
            pltpu.VMEM((TOK, C), BF16),
            pltpu.VMEM((TOK, C), BF16),
            pltpu.VMEM((TOK, C), BF16),
            pltpu.VMEM((TOK, C), BF16),
            pltpu.VMEM((HEADS * WTOK, WTOK), F32),
            pltpu.VMEM((4 * HEADS, WTOK, WTOK), F32),
            pltpu.VMEM((4, HEADS * WTOK, WTOK), BF16),
            pltpu.VMEM((4, HEADS * WTOK, C), BF16),
            pltpu.VMEM((4, HEADS * WTOK, C), BF16),
            pltpu.VMEM((TOK, C), BF16),
            *[pltpu.VMEM((C, TOK), BF16)] * 4,
            pltpu.VMEM((TOK, C), BF16),
            pltpu.VMEM((TOK, C), BF16),
            pltpu.VMEM((TOK, C), BF16),
            pltpu.VMEM((TOK, C), BF16),
            pltpu.VMEM((TOK, FF), BF16),
            pltpu.VMEM((TOK, FF), BF16),
            pltpu.VMEM((TOK, 3 * C), BF16),
            pltpu.VMEM((TOK, C), BF16),
            pltpu.VMEM((4, PACKED, 2 * C), BF16),
            pltpu.VMEM((4, PACKED - STAY, 2 * C), BF16),
            sem((4, 3)), sem((4, 3)),
            *[pltpu.VMEM((rows, 128), BF16) for rows in ROWS],
            *[ref for kind, size in PARTS for ref in sum_scratch(kind, size)],
        ],
        compiler_params=pltpu.CompilerParams(
            collective_id=0, has_side_effects=True, vmem_limit_bytes=56 * 2**20
        ),
        name="block",
    )(*args)


def finish_kernel(
    out_in, gx_in, full0_hbm, full1_hbm, full2_hbm, wqkv_hbm, wup_hbm, gain_a_hbm, gain_m_hbm,
    out_hbm, gx_hbm, qkv_hbm, proj_hbm, up_hbm, down_hbm, ga_hbm, gm_hbm,
    full0, full1, full2, wqkv, wup, gain_a, gain_m,
    out_ref, gx_ref, qkv_ref, proj_ref, up_ref, down_ref, ga_ref, gm_ref, in_sem, out_sem,
):
    def read(i, src, dst):
        copy = pltpu.make_async_copy(src, dst, in_sem.at[i])
        copy.start()
        return copy

    written = []

    def write(i, src, dst):
        written.append(pltpu.make_async_copy(src, dst, out_sem.at[i]))
        written[-1].start()

    def block(full, t):
        return full[t * C:(t + 1) * C, :].astype(F32) * FACTOR

    copies = [
        read(i, src, dst) for i, (src, dst) in enumerate((
            (full0_hbm, full0), (full1_hbm, full1), (full2_hbm, full2), (out_in, out_ref),
            (gx_in, gx_ref), (wqkv_hbm, wqkv), (wup_hbm, wup), (gain_a_hbm, gain_a),
            (gain_m_hbm, gain_m),
        ))
    ]
    copies[0].wait()
    for t in range(6):
        down_ref[:, t * 128:(t + 1) * 128] = block(full0, t)
    write(0, down_ref, down_hbm)
    copies[1].wait()
    for t in range(6):
        up_ref[:, t * 128:(t + 1) * 128] = block(full1, t) if t < 5 else block(full0, 7)
    write(1, up_ref, up_hbm)
    copies[2].wait()
    for t in range(4):
        qkv_ref[:, t * 128:(t + 1) * 128] = block(full2, t)
    mixed_tile = block(full2, 4)
    qkv_ref[:, 512:] = mixed_tile[:, :64]
    write(2, qkv_ref, qkv_hbm)
    proj_ref[:, :128] = block(full0, 6)
    proj_ref[:, 128:] = mixed_tile[:, 64:]
    write(3, proj_ref, proj_hbm)
    copies[3].wait()
    write(4, out_ref, out_hbm)
    copies[4].wait()
    write(5, gx_ref, gx_hbm)
    for copy in copies[5:]:
        copy.wait()
    for weight, grad, gain, ref in ((wqkv, qkv_ref, gain_a, ga_ref), (wup, up_ref, gain_m, gm_ref)):
        product = weight[...].astype(F32) * grad[...]
        total = lax.dot_general(
            jnp.ones((8, product.shape[1]), F32), product, (((1,), (1,)), ((), ())),
            precision=lax.Precision.HIGHEST, preferred_element_type=F32,
        )
        ref[...] = total[:1] / gain[...]
    write(6, ga_ref, ga_hbm)
    write(7, gm_ref, gm_hbm)
    for copy in written:
        copy.wait()


def finish_call(out, gx, full, w_qkv, w_up, gain_attn, gain_mlp):
    shape = jax.ShapeDtypeStruct
    results = (
        shape((TOK, C), BF16),
        shape((TOK, C), BF16),
        shape((C, 3 * C), F32),
        shape((C, C), F32),
        shape((C, FF), F32),
        shape((C, FF), F32),
        shape((1, C), F32),
        shape((1, C), F32),
    )
    return pl.pallas_call(
        finish_kernel,
        out_shape=results,
        in_specs=[HBM] * 9,
        out_specs=(HBM,) * 8,
        scratch_shapes=[
            *[pltpu.VMEM((rows, 128), BF16) for rows in ROWS],
            pltpu.VMEM((C, 3 * C), BF16),
            pltpu.VMEM((C, FF), BF16),
            pltpu.VMEM((1, C), F32),
            pltpu.VMEM((1, C), F32),
            *[pltpu.VMEM(result.shape, result.dtype) for result in results],
            pltpu.SemaphoreType.DMA((9,)),
            pltpu.SemaphoreType.DMA((8,)),
        ],
        compiler_params=pltpu.CompilerParams(vmem_limit_bytes=56 * 2**20),
        name="finish",
    )(out, gx, *full, w_qkv, w_up, gain_attn, gain_mlp)


def body(fields, gain_attn, w_qkv, bias, w_proj, gain_mlp, w_up, w_down, cotangent):
    out, gx, *full = block_call(
        fields.reshape(TOK, C), cotangent.reshape(TOK, C), bias.reshape(HEADS * WTOK, WTOK),
        gain_attn.reshape(1, C), w_qkv, w_proj, gain_mlp.reshape(1, C), w_up, w_down.T,
    )
    out, gx, qkv, proj, up, down, ga, gm = finish_call(
        out, gx, full, w_qkv, w_up, gain_attn.reshape(1, C), gain_mlp.reshape(1, C),
    )
    return (
        out.reshape(fields.shape), gx.reshape(fields.shape), qkv, proj, up, down.T,
        ga.reshape(C), gm.reshape(C),
    )


def solution(mesh):
    grid = P(None, "lat", "lon", None)
    in_specs = (grid, P(), P(), P("lat", None, None, None), P(), P(), P(), P(), grid)
    out_specs = (grid, grid, P(), P(), P(), P(), P(), P())
    return jax.shard_map(body, mesh=mesh, in_specs=in_specs, out_specs=out_specs, check_vma=False)
```

```python
import jax
import jax.numpy as jnp
from jax import lax
from jax.experimental import pallas as pl
from jax.experimental.pallas import tpu as pltpu
from jax.sharding import PartitionSpec as P

WLAT = 6
WLON = 12
WTOK = 144
HEADS = 6
HEAD = 32
C = 192
FF = 768
TOK = 576
NORM_EPS = 1e-05
MASKED = -1e30
FACTOR = 1.0 / 384.0

STAY = 112
PACKED = 320
PIECES = ((112, 112), (224, 48), (272, 48))
PAIR = 288

ROWS = (1536, 1024, 1024)

F32 = jnp.float32
BF16 = jnp.bfloat16
MESH = pl.DeviceIdType.MESH
VMEM = pl.BlockSpec(memory_space=pltpu.VMEM)
HBM = pl.BlockSpec(memory_space=pltpu.HBM)


def nn(left, right):
    return lax.dot_general(left, right, (((1,), (0,)), ((), ())), preferred_element_type=F32)


def nt(left, right):
    return lax.dot_general(left, right, (((1,), (1,)), ((), ())), preferred_element_type=F32)


def tn(left, right):
    return lax.dot_general(left, right, (((0,), (0,)), ((), ())), preferred_element_type=F32)


def row_mean(values):
    return jnp.sum(values, axis=-1, keepdims=True) * (1.0 / C)


def normalize(values):
    center = values - row_mean(values)
    inv = lax.rsqrt(row_mean(center * center) + NORM_EPS)
    return center * inv, inv


def norm_back(unit, inv, gain, upstream):
    scaled = upstream * gain
    grad = inv * (scaled - row_mean(scaled) - unit * row_mean(scaled * unit))
    return grad


def head_masks():
    head_of = lax.broadcasted_iota(jnp.int32, (1, C), 1) // HEAD
    return [jnp.where(head_of == h, 1.0, 0.0).astype(BF16) for h in range(HEADS)]


def piece_row(level, row, col):
    stay_row = row >= 3
    low = jnp.where(stay_row, row - 3, row)
    wide = level * 54 + low * 18 + col - 6
    thin = level * 18 + low * 6 + col
    right = jnp.where(stay_row, wide, wide + PIECES[0][0])
    left = jnp.where(stay_row, thin + PIECES[1][0], thin + PIECES[2][0])
    return jnp.where(col >= 6, right, left)


def pack_rows(token):
    return piece_row(token // 144, token % 144 // 24, token % 24)


def place_rows(token):
    col = token % WLON + token // 144 * WLON
    return piece_row(token % 144 // 72, (token % 72 // WLON + 3) % 6, (col + 6) % 24)


def table(rows_of):
    token = lax.broadcasted_iota(jnp.int32, (1, PAIR), 1)
    piece = lax.broadcasted_iota(jnp.int32, (PACKED, PAIR), 0)
    return jnp.where(piece == rows_of(token), 1.0, 0.0).astype(BF16)


def table_t(rows_of):
    token = lax.broadcasted_iota(jnp.int32, (PAIR, 1), 0)
    piece = lax.broadcasted_iota(jnp.int32, (PAIR, PACKED), 1)
    return jnp.where(piece == rows_of(token), 1.0, 0.0).astype(BF16)


def remote(src, dst, send_sem, recv_sem, device):
    return pltpu.make_async_remote_copy(
        src_ref=src, dst_ref=dst, send_sem=send_sem, recv_sem=recv_sem,
        device_id=device, device_id_type=MESH,
    )


def ring(index, step, size):
    return lax.rem(index + step + size, size)


def chunk(start, size):
    return pl.ds(pl.multiple_of(start, 16), size)


def near(steps, size):
    return sorted(steps, key=lambda step: sum(min(d, n - d) for d, n in zip(step, size)))


PLANE = near([(dy, dx) for dy in range(4) for dx in range(4) if (dy, dx) != (0, 0)], (4, 4))
RING = [dz for dz, in near([(dz,) for dz in range(1, 8)], (8,))]


class Place:
    def __init__(self):
        self.lon, self.lat = lax.axis_index("lon"), lax.axis_index("lat")
        self.core = lax.rem(self.lon, 2)
        self.x = lax.rem(self.lon // 2, 4)
        self.y = self.lat // 8 * 2 + self.lon // 8
        self.z = lax.rem(self.lat, 8)

    def device(self, y, x, z, core):
        return ((lax.rem(y, 2) * 4 + x) * 2 + core, y // 2 * 8 + z)

    def other_core(self):
        return self.device(self.y, self.x, self.z, 1 - self.core)

    def plane_spot(self, dy, dx):
        return ring(self.y, dy, 4), ring(self.x, dx, 4)

    def plane_peer(self, dy, dx):
        y, x = self.plane_spot(dy, dx)
        return self.device(y, x, self.z, self.core)

    def z_peer(self, dz):
        return self.device(self.y, self.x, ring(self.z, dz, 8), self.core)

    def halo_targets(self, step):
        lon, lat = ring(self.lon, step, 16), ring(self.lat, step, 16)
        return (self.lon, lat), (lon, self.lat), (lon, lat)

    def everyone(self):
        devices = list(self.halo_targets(-1)) + list(self.halo_targets(1)) + [self.other_core()]
        devices += [self.plane_peer(dy, dx) for dy, dx in PLANE]
        return devices + [self.z_peer(dz) for dz in range(1, 8)]


class Halo:
    def __init__(self, spot, packed, landed, send_sem, recv_sem, step):
        targets = spot.halo_targets(step)
        self.packed, self.landed = packed, landed
        self.copies = [
            remote(
                packed.at[pl.ds(start, size), :], landed.at[pl.ds(start - STAY, size), :],
                send_sem.at[i], recv_sem.at[i], targets[i],
            )
            for i, (start, size) in enumerate(PIECES)
        ]

    def start(self):
        for copy in self.copies:
            copy.start()

    def wait(self):
        for copy in self.copies:
            copy.wait()

    def pack(self, ref, table_ref):
        pairs = [ref[i * PAIR:(i + 1) * PAIR, :].astype(F32) for i in range(2)]
        both = jnp.concatenate(pairs, axis=1).astype(BF16)
        self.packed[...] = nn(table_ref[...], both).astype(BF16)

    def unpack(self, table_ref, ref):
        both = nn(table_ref[:, :STAY], self.packed[:STAY, :]) + nn(table_ref[:, STAY:], self.landed[...])
        for i in range(2):
            ref[i * PAIR:(i + 1) * PAIR, :] = both[:, i * C:(i + 1) * C].astype(BF16)


class Sum:
    def __init__(self, spot, flat, full, scratch):
        self.spot, self.flat, self.full = spot, flat, full
        (self.core_in, self.out, self.first_in, self.second_in, core, first_s, first_r,
         second_s, second_r, back_s, back_r, last) = scratch
        self.core_sems = core.at[0], core.at[1]
        self.first_sems, self.second_sems = (first_s, first_r), (second_s, second_r)
        self.back_sems, self.last_sems = (back_s, back_r), (last.at[0], last.at[1])
        self.size = self.first_in.shape[1]
        self.sent = []
        self.count = self.first_in.shape[0] + 1
        self.half = spot.core * (self.count * self.size)
        self.own = self.first_here() * self.size

    def launch(self, src, dst, sems, device, index=None):
        send_sem, recv_sem = sems if index is None else (sems[0].at[index], sems[1].at[index])
        copy = remote(src, dst, send_sem, recv_sem, device)
        copy.start()
        self.sent.append(copy)
        return copy

    def far_first(self, steps, make):
        copies = [make(k, steps[k]) for k in reversed(range(len(steps)))]
        return copies[::-1]

    def to_core(self):
        other = self.count * self.size - self.half
        self.core_copy = self.launch(
            self.flat.at[chunk(other, self.count * self.size)], self.core_in,
            self.core_sems, self.spot.other_core(),
        )

    def to_first(self):
        self.core_copy.wait_recv()
        mine = self.flat[chunk(self.half, self.count * self.size), :].astype(F32)
        self.out[...] = (mine + self.core_in[...].astype(F32)).astype(BF16)
        self.first_copies = self.far_first(self.first_steps, lambda k, step: self.launch(
            self.out.at[chunk(self.first_index(step) * self.size, self.size)],
            self.first_in.at[k], self.first_sems, self.first_peer(step), k,
        ))

    def to_second(self):
        total = self.out[chunk(self.own, self.size), :].astype(F32)
        for k, copy in enumerate(self.first_copies):
            copy.wait_recv()
            total = total + self.first_in[k].astype(F32)
        mine = self.second_in.at[self.second_here()]
        mine[...] = total.astype(BF16)
        self.second_copies = self.far_first(self.second_steps, lambda k, step: self.launch(
            mine, mine, self.second_sems, self.second_peer(step), k,
        ))

    def back_to_first(self):
        for copy in self.second_copies:
            copy.wait_recv()
        total = self.second_in[0].astype(F32)
        for i in range(1, len(self.second_steps) + 1):
            total = total + self.second_in[i].astype(F32)
        own = self.full.at[chunk(self.half + self.own, self.size)]
        own[...] = total.astype(BF16)
        self.back_copies = self.far_first(self.first_steps, lambda k, step: self.launch(
            own, own, self.back_sems, self.first_peer(step), k,
        ))

    def back_to_core(self):
        for copy in self.back_copies:
            copy.wait_recv()
        rows = self.full.at[chunk(self.half, self.count * self.size)]
        self.last_copy = self.launch(rows, rows, self.last_sems, self.spot.other_core())

    def finish(self):
        self.last_copy.wait_recv()

    def drain(self):
        for copy in self.sent:
            copy.wait_send()


class PlaneSum(Sum):
    first_steps, second_steps = PLANE, RING

    def first_here(self):
        return self.spot.y * 4 + self.spot.x

    def first_index(self, step):
        y, x = self.spot.plane_spot(*step)
        return y * 4 + x

    def first_peer(self, step):
        return self.spot.plane_peer(*step)

    def second_here(self):
        return self.spot.z

    def second_peer(self, step):
        return self.spot.z_peer(step)


class RingSum(Sum):
    first_steps, second_steps = RING, PLANE

    def first_here(self):
        return self.spot.z

    def first_index(self, step):
        return ring(self.spot.z, step, 8)

    def first_peer(self, step):
        return self.spot.z_peer(step)

    def second_here(self):
        return self.spot.y * 4 + self.spot.x

    def second_peer(self, step):
        return self.spot.plane_peer(*step)


def sum_scratch(kind, size):
    first, second = len(kind.first_steps), len(kind.second_steps)
    sem = pltpu.SemaphoreType.DMA
    return [
        pltpu.VMEM(((first + 1) * size, 128), BF16),
        pltpu.VMEM(((first + 1) * size, 128), BF16),
        pltpu.VMEM((first, size, 128), BF16),
        pltpu.VMEM((second + 1, size, 128), BF16),
        sem((2,)), sem((first,)), sem((first,)), sem((second,)), sem((second,)),
        sem((first,)), sem((first,)), sem((2,)),
    ]


PARTS = ((PlaneSum, 48), (RingSum, 64), (PlaneSum, 32))


def block_kernel(
    x_hbm, ct_hbm, bias_hbm, ga_hbm, wqkv_hbm, wproj_hbm, gm_hbm, wup_hbm, wdown_hbm,
    out_grid, gx_grid, full0, full1, full2,
    x_in, ct_in, bias_in, ga_in, wqkv_in, wproj_in, gm_in, wup_in, wdown_in, load_sem,
    pack, pack_t, place, place_t,
    x_ref, ct_ref, out_ref, gx_ref, bias32, probs, weights, km_s, vm_s, q_s,
    normed_t, nm_t, mixed_t, ct_t, mixed_s, hid_s, hid_grad_s, nm_s, act_s, gpre_s, gqkv_s, gattn_s,
    packed, landed, halo_send, halo_recv, flat0, flat1, flat2, *sum_refs,
):
    spot = Place()
    barrier = pltpu.get_barrier_semaphore()
    devices = spot.everyone()
    for device in devices[:6]:
        pl.semaphore_signal(barrier, inc=1, device_id=device, device_id_type=MESH)
    loads = []
    for i, (src, dst) in enumerate((
        (x_hbm, x_in), (ct_hbm, ct_in), (bias_hbm, bias_in), (ga_hbm, ga_in), (wqkv_hbm, wqkv_in),
        (wproj_hbm, wproj_in), (gm_hbm, gm_in), (wup_hbm, wup_in), (wdown_hbm, wdown_in),
    )):
        loads.append(pltpu.make_async_copy(src, dst, load_sem.at[i]))
        loads[-1].start()
    for device in devices[6:]:
        pl.semaphore_signal(barrier, inc=1, device_id=device, device_id_type=MESH)
    halos = [
        Halo(spot, packed.at[a], landed.at[a], halo_send.at[a], halo_recv.at[a], step)
        for a, step in enumerate((-1, -1, 1, 1))
    ]
    x_halo, ct_halo, out_halo, gx_halo = halos
    sums = []
    for i, (kind, _) in enumerate(PARTS):
        flat, full = ((flat0, full0), (flat1, full1), (flat2, full2))[i]
        count = len(sum_refs) // len(PARTS)
        sums.append(kind(spot, flat, full, sum_refs[i * count:(i + 1) * count]))
    early, late = sums[:2], sums[2]

    pack[...] = table(pack_rows)
    loads[0].wait()
    x_halo.pack(x_in, pack)
    pl.semaphore_wait(barrier, len(devices))
    x_halo.start()
    pack_t[...] = table_t(pack_rows)
    flat1[5 * C:, :] = jnp.zeros((ROWS[1] - 5 * C, 128), BF16)
    flat2[5 * C:, :] = jnp.zeros((ROWS[2] - 5 * C, 128), BF16)
    place[...] = table(place_rows)
    place_t[...] = table_t(place_rows)
    loads[1].wait()
    ct_halo.pack(ct_in, pack)
    ct_halo.start()
    loads[2].wait()
    is_last = spot.lat == lax.axis_size("lat") - 1
    row_half = (lax.broadcasted_iota(jnp.int32, (WTOK, 1), 0) // WLON) % WLAT < WLAT // 2
    col_half = (lax.broadcasted_iota(jnp.int32, (1, WTOK), 1) // WLON) % WLAT < WLAT // 2
    cut = jnp.logical_and(row_half != col_half, is_last)
    penalty = jnp.where(cut, MASKED, 0.0)
    for h in range(HEADS):
        rows = slice(h * WTOK, (h + 1) * WTOK)
        bias32[rows, :] = bias_in[rows, :].astype(F32).T + penalty
    for load in loads[3:]:
        load.wait()
    x_halo.wait()
    x_halo.unpack(place_t, x_ref)

    scale = HEAD ** (-0.5)
    masks = head_masks()
    ga = ga_in[...]
    gm = gm_in[...]

    def forward():
        x = x_ref[...].astype(F32)
        unit, _ = normalize(x)
        normed = (unit * ga).astype(BF16)
        normed_t[...] = normed.T
        qkv = nn(normed, wqkv_in[...]).astype(BF16)
        q_s[...] = qkv[:, :C]
        k = qkv[:, C:2 * C]
        v = qkv[:, 2 * C:]
        for n in range(4):
            rows = slice(n * WTOK, (n + 1) * WTOK)
            km = jnp.concatenate([k[rows] * masks[h] for h in range(HEADS)], axis=0)
            vm = jnp.concatenate([v[rows] * masks[h] for h in range(HEADS)], axis=0)
            km_s[n] = km
            vm_s[n] = vm
            s = (nt(km, q_s[rows, :]) * scale + bias32[...]).reshape(HEADS, WTOK, WTOK)
            e = jnp.exp(s - jnp.max(s, axis=1, keepdims=True))
            p = e * (1.0 / jnp.sum(e, axis=1, keepdims=True))
            probs[n * HEADS:(n + 1) * HEADS] = p
            weights[n] = p.astype(BF16).reshape(HEADS * WTOK, WTOK)
            mixed_s[rows, :] = tn(weights[n], vm).astype(BF16)

    def mlp():
        hidden = (x_ref[...].astype(F32) + nn(mixed_s[...], wproj_in[...])).astype(BF16)
        hid_s[...] = hidden
        unit, inv = normalize(hidden.astype(F32))
        nm_s[...] = (unit * gm).astype(BF16)
        nm_t[...] = nm_s[...].T
        grad_nm = jnp.zeros((TOK, C), F32)
        for f in range(3):
            cols = slice(f * 256, (f + 1) * 256)
            z = nn(nm_s[...], wup_in[:, cols])
            phi = 0.5 * (1.0 + lax.erf(z * (0.5 ** 0.5)))
            act_s[:, cols] = (z * phi).astype(BF16)
            slope = phi + z * (jnp.exp(-0.5 * z * z) * 0.3989422804014327)
            gpre = (nn(ct_ref[...], wdown_in[:, cols]) * slope).astype(BF16)
            gpre_s[:, cols] = gpre
            grad_nm = grad_nm + nt(gpre, wup_in[:, cols])
        grad_hidden = (ct_ref[...].astype(F32) + norm_back(unit, inv, gm, grad_nm)).astype(BF16)
        hid_grad_s[...] = grad_hidden
        gattn_s[...] = nt(grad_hidden, wproj_in[...]).astype(BF16)

    def attention_back(n):
        rows = slice(n * WTOK, (n + 1) * WTOK)
        up = gattn_s[rows, :]
        p = probs[n * HEADS:(n + 1) * HEADS]
        gp = nt(vm_s[n], up).reshape(HEADS, WTOK, WTOK)
        inner = jnp.sum(p * gp, axis=1, keepdims=True)
        gs = (p * (gp - inner) * scale).astype(BF16).reshape(HEADS * WTOK, WTOK)
        gv_all = nn(weights[n], up)
        gk_all = nn(gs, q_s[rows, :])
        gq = tn(gs, km_s[n])
        gk = jnp.zeros((WTOK, C), F32)
        gv = jnp.zeros((WTOK, C), F32)
        for h in range(HEADS):
            gk = jnp.where(masks[h] > 0, gk_all[h * WTOK:(h + 1) * WTOK], gk)
            gv = jnp.where(masks[h] > 0, gv_all[h * WTOK:(h + 1) * WTOK], gv)
        gqkv_s[rows, :] = jnp.concatenate([gq, gk, gv], axis=1).astype(BF16)

    def output():
        out_ref[...] = (hid_s[...].astype(F32) + nt(act_s[...], wdown_in[...])).astype(BF16)

    def input_grad():
        grad_rolled = nt(gqkv_s[...], wqkv_in[...]).astype(BF16).astype(F32)
        unit, inv = normalize(x_ref[...].astype(F32))
        grad_x = norm_back(unit, inv, ga, grad_rolled)
        gx_ref[...] = (hid_grad_s[...].astype(F32) + grad_x).astype(BF16)

    def store_blocks(flat, base, values):
        for t in range(values.shape[1] // 128):
            flat[base + t * C:base + (t + 1) * C, :] = values[:, t * 128:(t + 1) * 128].astype(BF16)

    forward()
    mixed_t[...] = mixed_s[...].T
    ct_halo.wait()
    ct_halo.unpack(place_t, ct_ref)
    ct_t[...] = ct_ref[...].T
    mlp()
    grad_up = nn(nm_t[...], gpre_s[...])
    grad_proj = nn(mixed_t[...], hid_grad_s[...])
    store_blocks(flat1, 0, grad_up[:, :640])
    store_blocks(flat0, 0, nn(ct_t[...], act_s[...]))
    store_blocks(flat0, 6 * C, grad_proj)
    store_blocks(flat0, 7 * C, grad_up[:, 640:])
    for part in early:
        part.to_core()
    attention_back(0)
    attention_back(1)
    for part in early:
        part.to_first()
    attention_back(2)
    attention_back(3)
    grad_qkv = nn(normed_t[...], gqkv_s[...])
    store_blocks(flat2, 0, grad_qkv)
    store_blocks(flat2, 4 * C, jnp.concatenate([grad_qkv[:, 512:], grad_proj[:, 128:]], axis=1))
    late.to_core()
    late.to_first()
    output()
    out_halo.pack(out_ref, place)
    input_grad()
    gx_halo.pack(gx_ref, place)
    for part in sums:
        part.to_second()
    out_halo.start()
    for part in sums:
        part.back_to_first()
    gx_halo.start()
    out_halo.wait()
    out_halo.unpack(pack_t, out_grid)
    for part in sums:
        part.back_to_core()
    gx_halo.wait()
    gx_halo.unpack(pack_t, gx_grid)
    for part in sums:
        part.finish()
    for part in sums:
        part.drain()


def block_call(x, ct, bias, gain_attn, w_qkv, w_proj, gain_mlp, w_up, w_down):
    shape = jax.ShapeDtypeStruct
    args = (x, ct, bias, gain_attn, w_qkv, w_proj, gain_mlp, w_up, w_down)
    sem = pltpu.SemaphoreType.DMA
    return pl.pallas_call(
        block_kernel,
        out_shape=(
            shape((TOK, C), BF16),
            shape((TOK, C), BF16),
            *[shape((rows, 128), BF16) for rows in ROWS],
        ),
        in_specs=[HBM] * 9,
        out_specs=(VMEM,) * 5,
        scratch_shapes=[
            *[pltpu.VMEM(arg.shape, arg.dtype) for arg in args], sem((9,)),
            pltpu.VMEM((PACKED, PAIR), BF16),
            pltpu.VMEM((PAIR, PACKED), BF16),
            pltpu.VMEM((PACKED, PAIR), BF16),
            pltpu.VMEM((PAIR, PACKED), BF16),
            pltpu.VMEM((TOK, C), BF16),
            pltpu.VMEM((TOK, C), BF16),
            pltpu.VMEM((TOK, C), BF16),
            pltpu.VMEM((TOK, C), BF16),
            pltpu.VMEM((HEADS * WTOK, WTOK), F32),
            pltpu.VMEM((4 * HEADS, WTOK, WTOK), F32),
            pltpu.VMEM((4, HEADS * WTOK, WTOK), BF16),
            pltpu.VMEM((4, HEADS * WTOK, C), BF16),
            pltpu.VMEM((4, HEADS * WTOK, C), BF16),
            pltpu.VMEM((TOK, C), BF16),
            *[pltpu.VMEM((C, TOK), BF16)] * 4,
            pltpu.VMEM((TOK, C), BF16),
            pltpu.VMEM((TOK, C), BF16),
            pltpu.VMEM((TOK, C), BF16),
            pltpu.VMEM((TOK, C), BF16),
            pltpu.VMEM((TOK, FF), BF16),
            pltpu.VMEM((TOK, FF), BF16),
            pltpu.VMEM((TOK, 3 * C), BF16),
            pltpu.VMEM((TOK, C), BF16),
            pltpu.VMEM((4, PACKED, 2 * C), BF16),
            pltpu.VMEM((4, PACKED - STAY, 2 * C), BF16),
            sem((4, 3)), sem((4, 3)),
            *[pltpu.VMEM((rows, 128), BF16) for rows in ROWS],
            *[ref for kind, size in PARTS for ref in sum_scratch(kind, size)],
        ],
        compiler_params=pltpu.CompilerParams(
            collective_id=0, has_side_effects=True, vmem_limit_bytes=56 * 2**20
        ),
        name="block",
    )(*args)


def finish_kernel(
    out_in, gx_in, full0_hbm, full1_hbm, full2_hbm, wqkv_hbm, wup_hbm, gain_a_hbm, gain_m_hbm,
    out_hbm, gx_hbm, qkv_hbm, proj_hbm, up_hbm, down_hbm, ga_hbm, gm_hbm,
    full0, full1, full2, wqkv, wup, gain_a, gain_m,
    out_ref, gx_ref, qkv_ref, proj_ref, up_ref, down_ref, ga_ref, gm_ref, in_sem, out_sem,
):
    def read(i, src, dst):
        copy = pltpu.make_async_copy(src, dst, in_sem.at[i])
        copy.start()
        return copy

    written = []

    def write(i, src, dst):
        written.append(pltpu.make_async_copy(src, dst, out_sem.at[i]))
        written[-1].start()

    def block(full, t):
        return full[t * C:(t + 1) * C, :].astype(F32) * FACTOR

    copies = [
        read(i, src, dst) for i, (src, dst) in enumerate((
            (full0_hbm, full0), (full1_hbm, full1), (full2_hbm, full2), (out_in, out_ref),
            (gx_in, gx_ref), (wqkv_hbm, wqkv), (wup_hbm, wup), (gain_a_hbm, gain_a),
            (gain_m_hbm, gain_m),
        ))
    ]
    copies[0].wait()
    for t in range(6):
        down_ref[:, t * 128:(t + 1) * 128] = block(full0, t)
    write(0, down_ref, down_hbm)
    copies[1].wait()
    for t in range(6):
        up_ref[:, t * 128:(t + 1) * 128] = block(full1, t) if t < 5 else block(full0, 7)
    write(1, up_ref, up_hbm)
    copies[2].wait()
    for t in range(4):
        qkv_ref[:, t * 128:(t + 1) * 128] = block(full2, t)
    mixed_tile = block(full2, 4)
    qkv_ref[:, 512:] = mixed_tile[:, :64]
    write(2, qkv_ref, qkv_hbm)
    proj_ref[:, :128] = block(full0, 6)
    proj_ref[:, 128:] = mixed_tile[:, 64:]
    write(3, proj_ref, proj_hbm)
    copies[3].wait()
    write(4, out_ref, out_hbm)
    copies[4].wait()
    write(5, gx_ref, gx_hbm)
    for copy in copies[5:]:
        copy.wait()
    for weight, grad, gain, ref in ((wqkv, qkv_ref, gain_a, ga_ref), (wup, up_ref, gain_m, gm_ref)):
        product = weight[...].astype(F32) * grad[...]
        total = lax.dot_general(
            jnp.ones((8, product.shape[1]), F32), product, (((1,), (1,)), ((), ())),
            precision=lax.Precision.HIGHEST, preferred_element_type=F32,
        )
        ref[...] = total[:1] / gain[...]
    write(6, ga_ref, ga_hbm)
    write(7, gm_ref, gm_hbm)
    for copy in written:
        copy.wait()


def finish_call(out, gx, full, w_qkv, w_up, gain_attn, gain_mlp):
    shape = jax.ShapeDtypeStruct
    results = (
        shape((TOK, C), BF16),
        shape((TOK, C), BF16),
        shape((C, 3 * C), F32),
        shape((C, C), F32),
        shape((C, FF), F32),
        shape((C, FF), F32),
        shape((1, C), F32),
        shape((1, C), F32),
    )
    return pl.pallas_call(
        finish_kernel,
        out_shape=results,
        in_specs=[HBM] * 9,
        out_specs=(HBM,) * 8,
        scratch_shapes=[
            *[pltpu.VMEM((rows, 128), BF16) for rows in ROWS],
            pltpu.VMEM((C, 3 * C), BF16),
            pltpu.VMEM((C, FF), BF16),
            pltpu.VMEM((1, C), F32),
            pltpu.VMEM((1, C), F32),
            *[pltpu.VMEM(result.shape, result.dtype) for result in results],
            pltpu.SemaphoreType.DMA((9,)),
            pltpu.SemaphoreType.DMA((8,)),
        ],
        compiler_params=pltpu.CompilerParams(vmem_limit_bytes=56 * 2**20),
        name="finish",
    )(out, gx, *full, w_qkv, w_up, gain_attn, gain_mlp)


def body(fields, gain_attn, w_qkv, bias, w_proj, gain_mlp, w_up, w_down, cotangent):
    out, gx, *full = block_call(
        fields.reshape(TOK, C), cotangent.reshape(TOK, C), bias.reshape(HEADS * WTOK, WTOK),
        gain_attn.reshape(1, C), w_qkv, w_proj, gain_mlp.reshape(1, C), w_up, w_down.T,
    )
    out, gx, qkv, proj, up, down, ga, gm = finish_call(
        out, gx, full, w_qkv, w_up, gain_attn.reshape(1, C), gain_mlp.reshape(1, C),
    )
    return (
        out.reshape(fields.shape), gx.reshape(fields.shape), qkv, proj, up, down.T,
        ga.reshape(C), gm.reshape(C),
    )


def solution(mesh):
    grid = P(None, "lat", "lon", None)
    in_specs = (grid, P(), P(), P("lat", None, None, None), P(), P(), P(), P(), grid)
    out_specs = (grid, grid, P(), P(), P(), P(), P(), P())
    return jax.shard_map(body, mesh=mesh, in_specs=in_specs, out_specs=out_specs, check_vma=False)
```

```python
import jax
import jax.numpy as jnp
from jax import lax
from jax.experimental import pallas as pl
from jax.experimental.pallas import tpu as pltpu
from jax.sharding import PartitionSpec as P

WLAT = 6
WLON = 12
WTOK = 144
HEADS = 6
HEAD = 32
C = 192
FF = 768
TOK = 576
NORM_EPS = 1e-05
MASKED = -1e30
FACTOR = 1.0 / 384.0

STAY = 112
PACKED = 320
PIECES = ((112, 112), (224, 48), (272, 48))
PAIR = 288

ROWS = (1536, 1024, 1024)

F32 = jnp.float32
BF16 = jnp.bfloat16
MESH = pl.DeviceIdType.MESH
VMEM = pl.BlockSpec(memory_space=pltpu.VMEM)
HBM = pl.BlockSpec(memory_space=pltpu.HBM)


def nn(left, right):
    return lax.dot_general(left, right, (((1,), (0,)), ((), ())), preferred_element_type=F32)


def nt(left, right):
    return lax.dot_general(left, right, (((1,), (1,)), ((), ())), preferred_element_type=F32)


def tn(left, right):
    return lax.dot_general(left, right, (((0,), (0,)), ((), ())), preferred_element_type=F32)


def row_mean(values):
    return jnp.sum(values, axis=-1, keepdims=True) * (1.0 / C)


def normalize(values):
    center = values - row_mean(values)
    inv = lax.rsqrt(row_mean(center * center) + NORM_EPS)
    return center * inv, inv


def norm_back(unit, inv, gain, upstream):
    scaled = upstream * gain
    grad = inv * (scaled - row_mean(scaled) - unit * row_mean(scaled * unit))
    return grad


def head_masks():
    head_of = lax.broadcasted_iota(jnp.int32, (1, C), 1) // HEAD
    return [jnp.where(head_of == h, 1.0, 0.0).astype(BF16) for h in range(HEADS)]


def piece_row(level, row, col):
    stay_row = row >= 3
    low = jnp.where(stay_row, row - 3, row)
    wide = level * 54 + low * 18 + col - 6
    thin = level * 18 + low * 6 + col
    right = jnp.where(stay_row, wide, wide + PIECES[0][0])
    left = jnp.where(stay_row, thin + PIECES[1][0], thin + PIECES[2][0])
    return jnp.where(col >= 6, right, left)


def pack_rows(token):
    return piece_row(token // 144, token % 144 // 24, token % 24)


def place_rows(token):
    col = token % WLON + token // 144 * WLON
    return piece_row(token % 144 // 72, (token % 72 // WLON + 3) % 6, (col + 6) % 24)


def table(rows_of):
    token = lax.broadcasted_iota(jnp.int32, (1, PAIR), 1)
    piece = lax.broadcasted_iota(jnp.int32, (PACKED, PAIR), 0)
    return jnp.where(piece == rows_of(token), 1.0, 0.0).astype(BF16)


def table_t(rows_of):
    token = lax.broadcasted_iota(jnp.int32, (PAIR, 1), 0)
    piece = lax.broadcasted_iota(jnp.int32, (PAIR, PACKED), 1)
    return jnp.where(piece == rows_of(token), 1.0, 0.0).astype(BF16)


def remote(src, dst, send_sem, recv_sem, device):
    return pltpu.make_async_remote_copy(
        src_ref=src, dst_ref=dst, send_sem=send_sem, recv_sem=recv_sem,
        device_id=device, device_id_type=MESH,
    )


def ring(index, step, size):
    return lax.rem(index + step + size, size)


def chunk(start, size):
    return pl.ds(pl.multiple_of(start, 16), size)


def near(steps, size):
    return sorted(steps, key=lambda step: sum(min(d, n - d) for d, n in zip(step, size)))


PLANE = near([(dy, dx) for dy in range(4) for dx in range(4) if (dy, dx) != (0, 0)], (4, 4))
RING = [dz for dz, in near([(dz,) for dz in range(1, 8)], (8,))]


class Place:
    def __init__(self):
        self.lon, self.lat = lax.axis_index("lon"), lax.axis_index("lat")
        self.core = lax.rem(self.lon, 2)
        self.x = lax.rem(self.lon // 2, 4)
        self.y = self.lat // 8 * 2 + self.lon // 8
        self.z = lax.rem(self.lat, 8)

    def device(self, y, x, z, core):
        return ((lax.rem(y, 2) * 4 + x) * 2 + core, y // 2 * 8 + z)

    def other_core(self):
        return self.device(self.y, self.x, self.z, 1 - self.core)

    def plane_spot(self, dy, dx):
        return ring(self.y, dy, 4), ring(self.x, dx, 4)

    def plane_peer(self, dy, dx):
        y, x = self.plane_spot(dy, dx)
        return self.device(y, x, self.z, self.core)

    def z_peer(self, dz):
        return self.device(self.y, self.x, ring(self.z, dz, 8), self.core)

    def halo_targets(self, step):
        lon, lat = ring(self.lon, step, 16), ring(self.lat, step, 16)
        return (self.lon, lat), (lon, self.lat), (lon, lat)

    def everyone(self):
        devices = list(self.halo_targets(-1)) + list(self.halo_targets(1)) + [self.other_core()]
        devices += [self.plane_peer(dy, dx) for dy, dx in PLANE]
        return devices + [self.z_peer(dz) for dz in range(1, 8)]


class Halo:
    def __init__(self, spot, packed, landed, send_sem, recv_sem, step):
        targets = spot.halo_targets(step)
        self.packed, self.landed = packed, landed
        self.copies = [
            remote(
                packed.at[pl.ds(start, size), :], landed.at[pl.ds(start - STAY, size), :],
                send_sem.at[i], recv_sem.at[i], targets[i],
            )
            for i, (start, size) in enumerate(PIECES)
        ]

    def start(self):
        for copy in self.copies:
            copy.start()

    def wait_sent(self):
        for copy in self.copies:
            copy.wait_send()

    def wait_landed(self):
        for copy in self.copies:
            copy.wait_recv()

    def wait(self):
        self.wait_sent()
        self.wait_landed()

    def pack(self, ref, table_ref):
        pairs = [ref[i * PAIR:(i + 1) * PAIR, :].astype(F32) for i in range(2)]
        both = jnp.concatenate(pairs, axis=1).astype(BF16)
        self.packed[...] = nn(table_ref[...], both).astype(BF16)

    def unpack(self, table_ref, ref):
        both = nn(table_ref[:, :STAY], self.packed[:STAY, :]) + nn(table_ref[:, STAY:], self.landed[...])
        for i in range(2):
            ref[i * PAIR:(i + 1) * PAIR, :] = both[:, i * C:(i + 1) * C].astype(BF16)


class Sum:
    def __init__(self, spot, flat, full, scratch):
        self.spot, self.flat, self.full = spot, flat, full
        (self.core_in, self.out, self.first_in, self.second_in, core, first_s, first_r,
         second_s, second_r, back_s, back_r, last) = scratch
        self.core_sems = core.at[0], core.at[1]
        self.first_sems, self.second_sems = (first_s, first_r), (second_s, second_r)
        self.back_sems, self.last_sems = (back_s, back_r), (last.at[0], last.at[1])
        self.size = self.first_in.shape[1]
        self.sent = []
        self.count = self.first_in.shape[0] + 1
        self.half = spot.core * (self.count * self.size)
        self.own = self.first_here() * self.size

    def launch(self, src, dst, sems, device, index=None):
        send_sem, recv_sem = sems if index is None else (sems[0].at[index], sems[1].at[index])
        copy = remote(src, dst, send_sem, recv_sem, device)
        copy.start()
        self.sent.append(copy)
        return copy

    def far_first(self, steps, make):
        copies = [make(k, steps[k]) for k in reversed(range(len(steps)))]
        return copies[::-1]

    def to_core(self):
        other = self.count * self.size - self.half
        self.core_copy = self.launch(
            self.flat.at[chunk(other, self.count * self.size)], self.core_in,
            self.core_sems, self.spot.other_core(),
        )

    def to_first(self):
        self.core_copy.wait_recv()
        mine = self.flat[chunk(self.half, self.count * self.size), :].astype(F32)
        self.out[...] = (mine + self.core_in[...].astype(F32)).astype(BF16)
        self.first_copies = self.far_first(self.first_steps, lambda k, step: self.launch(
            self.out.at[chunk(self.first_index(step) * self.size, self.size)],
            self.first_in.at[k], self.first_sems, self.first_peer(step), k,
        ))

    def to_second(self):
        total = self.out[chunk(self.own, self.size), :].astype(F32)
        for k, copy in enumerate(self.first_copies):
            copy.wait_recv()
            total = total + self.first_in[k].astype(F32)
        mine = self.second_in.at[self.second_here()]
        mine[...] = total.astype(BF16)
        self.second_copies = self.far_first(self.second_steps, lambda k, step: self.launch(
            mine, mine, self.second_sems, self.second_peer(step), k,
        ))

    def back_to_first(self):
        for copy in self.second_copies:
            copy.wait_recv()
        total = self.second_in[0].astype(F32)
        for i in range(1, len(self.second_steps) + 1):
            total = total + self.second_in[i].astype(F32)
        own = self.full.at[chunk(self.half + self.own, self.size)]
        own[...] = total.astype(BF16)
        self.back_copies = self.far_first(self.first_steps, lambda k, step: self.launch(
            own, own, self.back_sems, self.first_peer(step), k,
        ))

    def back_to_core(self):
        for copy in self.back_copies:
            copy.wait_recv()
        rows = self.full.at[chunk(self.half, self.count * self.size)]
        self.last_copy = self.launch(rows, rows, self.last_sems, self.spot.other_core())

    def finish(self):
        self.last_copy.wait_recv()

    def drain(self):
        for copy in self.sent:
            copy.wait_send()


class PlaneSum(Sum):
    first_steps, second_steps = PLANE, RING

    def first_here(self):
        return self.spot.y * 4 + self.spot.x

    def first_index(self, step):
        y, x = self.spot.plane_spot(*step)
        return y * 4 + x

    def first_peer(self, step):
        return self.spot.plane_peer(*step)

    def second_here(self):
        return self.spot.z

    def second_peer(self, step):
        return self.spot.z_peer(step)


class RingSum(Sum):
    first_steps, second_steps = RING, PLANE

    def first_here(self):
        return self.spot.z

    def first_index(self, step):
        return ring(self.spot.z, step, 8)

    def first_peer(self, step):
        return self.spot.z_peer(step)

    def second_here(self):
        return self.spot.y * 4 + self.spot.x

    def second_peer(self, step):
        return self.spot.plane_peer(*step)


def sum_scratch(kind, size):
    first, second = len(kind.first_steps), len(kind.second_steps)
    sem = pltpu.SemaphoreType.DMA
    return [
        pltpu.VMEM(((first + 1) * size, 128), BF16),
        pltpu.VMEM(((first + 1) * size, 128), BF16),
        pltpu.VMEM((first, size, 128), BF16),
        pltpu.VMEM((second + 1, size, 128), BF16),
        sem((2,)), sem((first,)), sem((first,)), sem((second,)), sem((second,)),
        sem((first,)), sem((first,)), sem((2,)),
    ]


PARTS = ((PlaneSum, 48), (RingSum, 64), (PlaneSum, 32))


def block_kernel(
    x_hbm, ct_hbm, bias_hbm, ga_hbm, wqkv_hbm, wproj_hbm, gm_hbm, wup_hbm, wdown_hbm,
    out_grid, gx_grid, full0, full1, full2,
    x_in, ct_in, bias_in, ga_in, wqkv_in, wproj_in, gm_in, wup_in, wdown_in, load_sem,
    pack, pack_t, place, place_t,
    x_ref, ct_ref, out_ref, gx_ref, bias32, probs, weights, km_s, vm_s, q_s,
    normed_t, nm_t, mixed_t, ct_t, mixed_s, hid_s, hid_grad_s, nm_s, act_s, gpre_s, gqkv_s, gattn_s,
    packed, landed, halo_send, halo_recv, flat0, flat1, flat2, *sum_refs,
):
    spot = Place()
    barrier = pltpu.get_barrier_semaphore()
    devices = spot.everyone()
    for device in devices[:6]:
        pl.semaphore_signal(barrier, inc=1, device_id=device, device_id_type=MESH)
    loads = []
    for i, (src, dst) in enumerate((
        (x_hbm, x_in), (ct_hbm, ct_in), (bias_hbm, bias_in), (ga_hbm, ga_in), (wqkv_hbm, wqkv_in),
        (wproj_hbm, wproj_in), (gm_hbm, gm_in), (wup_hbm, wup_in), (wdown_hbm, wdown_in),
    )):
        loads.append(pltpu.make_async_copy(src, dst, load_sem.at[i]))
        loads[-1].start()
    for device in devices[6:]:
        pl.semaphore_signal(barrier, inc=1, device_id=device, device_id_type=MESH)
    halos = [
        Halo(spot, packed.at[a], landed.at[a], halo_send.at[a], halo_recv.at[a], step)
        for a, step in enumerate((-1, -1, 1, 1))
    ]
    x_halo, ct_halo, out_halo, gx_halo = halos
    sums = []
    for i, (kind, _) in enumerate(PARTS):
        flat, full = ((flat0, full0), (flat1, full1), (flat2, full2))[i]
        count = len(sum_refs) // len(PARTS)
        sums.append(kind(spot, flat, full, sum_refs[i * count:(i + 1) * count]))
    early, late = sums[:2], sums[2]

    pack[...] = table(pack_rows)
    loads[0].wait()
    x_halo.pack(x_in, pack)
    pl.semaphore_wait(barrier, len(devices))
    x_halo.start()
    pack_t[...] = table_t(pack_rows)
    flat1[5 * C:, :] = jnp.zeros((ROWS[1] - 5 * C, 128), BF16)
    flat2[5 * C:, :] = jnp.zeros((ROWS[2] - 5 * C, 128), BF16)
    place[...] = table(place_rows)
    place_t[...] = table_t(place_rows)
    loads[1].wait()
    ct_halo.pack(ct_in, pack)
    loads[2].wait()
    is_last = spot.lat == lax.axis_size("lat") - 1
    row_half = (lax.broadcasted_iota(jnp.int32, (WTOK, 1), 0) // WLON) % WLAT < WLAT // 2
    col_half = (lax.broadcasted_iota(jnp.int32, (1, WTOK), 1) // WLON) % WLAT < WLAT // 2
    cut = jnp.logical_and(row_half != col_half, is_last)
    penalty = jnp.where(cut, MASKED, 0.0)
    for h in range(HEADS):
        rows = slice(h * WTOK, (h + 1) * WTOK)
        bias32[rows, :] = bias_in[rows, :].astype(F32).T + penalty
    for load in loads[3:]:
        load.wait()
    x_halo.wait_sent()
    ct_halo.start()
    x_halo.wait_landed()
    x_halo.unpack(place_t, x_ref)

    scale = HEAD ** (-0.5)
    masks = head_masks()
    ga = ga_in[...]
    gm = gm_in[...]

    def forward():
        x = x_ref[...].astype(F32)
        unit, _ = normalize(x)
        normed = (unit * ga).astype(BF16)
        normed_t[...] = normed.T
        qkv = nn(normed, wqkv_in[...]).astype(BF16)
        q_s[...] = qkv[:, :C]
        k = qkv[:, C:2 * C]
        v = qkv[:, 2 * C:]
        for n in range(4):
            rows = slice(n * WTOK, (n + 1) * WTOK)
            km = jnp.concatenate([k[rows] * masks[h] for h in range(HEADS)], axis=0)
            vm = jnp.concatenate([v[rows] * masks[h] for h in range(HEADS)], axis=0)
            km_s[n] = km
            vm_s[n] = vm
            s = (nt(km, q_s[rows, :]) * scale + bias32[...]).reshape(HEADS, WTOK, WTOK)
            e = jnp.exp(s - jnp.max(s, axis=1, keepdims=True))
            p = e * (1.0 / jnp.sum(e, axis=1, keepdims=True))
            probs[n * HEADS:(n + 1) * HEADS] = p
            weights[n] = p.astype(BF16).reshape(HEADS * WTOK, WTOK)
            mixed_s[rows, :] = tn(weights[n], vm).astype(BF16)

    def mlp():
        hidden = (x_ref[...].astype(F32) + nn(mixed_s[...], wproj_in[...])).astype(BF16)
        hid_s[...] = hidden
        unit, inv = normalize(hidden.astype(F32))
        nm_s[...] = (unit * gm).astype(BF16)
        nm_t[...] = nm_s[...].T
        grad_nm = jnp.zeros((TOK, C), F32)
        for f in range(3):
            cols = slice(f * 256, (f + 1) * 256)
            z = nn(nm_s[...], wup_in[:, cols])
            phi = 0.5 * (1.0 + lax.erf(z * (0.5 ** 0.5)))
            act_s[:, cols] = (z * phi).astype(BF16)
            slope = phi + z * (jnp.exp(-0.5 * z * z) * 0.3989422804014327)
            gpre = (nn(ct_ref[...], wdown_in[:, cols]) * slope).astype(BF16)
            gpre_s[:, cols] = gpre
            grad_nm = grad_nm + nt(gpre, wup_in[:, cols])
        grad_hidden = (ct_ref[...].astype(F32) + norm_back(unit, inv, gm, grad_nm)).astype(BF16)
        hid_grad_s[...] = grad_hidden
        gattn_s[...] = nt(grad_hidden, wproj_in[...]).astype(BF16)

    def attention_back(n):
        rows = slice(n * WTOK, (n + 1) * WTOK)
        up = gattn_s[rows, :]
        p = probs[n * HEADS:(n + 1) * HEADS]
        gp = nt(vm_s[n], up).reshape(HEADS, WTOK, WTOK)
        inner = jnp.sum(p * gp, axis=1, keepdims=True)
        gs = (p * (gp - inner) * scale).astype(BF16).reshape(HEADS * WTOK, WTOK)
        gv_all = nn(weights[n], up)
        gk_all = nn(gs, q_s[rows, :])
        gq = tn(gs, km_s[n])
        gk = jnp.zeros((WTOK, C), F32)
        gv = jnp.zeros((WTOK, C), F32)
        for h in range(HEADS):
            gk = jnp.where(masks[h] > 0, gk_all[h * WTOK:(h + 1) * WTOK], gk)
            gv = jnp.where(masks[h] > 0, gv_all[h * WTOK:(h + 1) * WTOK], gv)
        gqkv_s[rows, :] = jnp.concatenate([gq, gk, gv], axis=1).astype(BF16)

    def output():
        out_ref[...] = (hid_s[...].astype(F32) + nt(act_s[...], wdown_in[...])).astype(BF16)

    def input_grad():
        grad_rolled = nt(gqkv_s[...], wqkv_in[...]).astype(BF16).astype(F32)
        unit, inv = normalize(x_ref[...].astype(F32))
        grad_x = norm_back(unit, inv, ga, grad_rolled)
        gx_ref[...] = (hid_grad_s[...].astype(F32) + grad_x).astype(BF16)

    def store_blocks(flat, base, values):
        for t in range(values.shape[1] // 128):
            flat[base + t * C:base + (t + 1) * C, :] = values[:, t * 128:(t + 1) * 128].astype(BF16)

    forward()
    mixed_t[...] = mixed_s[...].T
    ct_halo.wait()
    ct_halo.unpack(place_t, ct_ref)
    ct_t[...] = ct_ref[...].T
    mlp()
    grad_up = nn(nm_t[...], gpre_s[...])
    grad_proj = nn(mixed_t[...], hid_grad_s[...])
    store_blocks(flat1, 0, grad_up[:, :640])
    store_blocks(flat0, 0, nn(ct_t[...], act_s[...]))
    store_blocks(flat0, 6 * C, grad_proj)
    store_blocks(flat0, 7 * C, grad_up[:, 640:])
    for part in early:
        part.to_core()
    attention_back(0)
    attention_back(1)
    for part in early:
        part.to_first()
    attention_back(2)
    attention_back(3)
    grad_qkv = nn(normed_t[...], gqkv_s[...])
    store_blocks(flat2, 0, grad_qkv)
    store_blocks(flat2, 4 * C, jnp.concatenate([grad_qkv[:, 512:], grad_proj[:, 128:]], axis=1))
    late.to_core()
    late.to_first()
    output()
    out_halo.pack(out_ref, place)
    out_halo.start()
    input_grad()
    gx_halo.pack(gx_ref, place)
    for part in sums:
        part.to_second()
    gx_halo.start()
    for part in sums:
        part.back_to_first()
    out_halo.wait()
    out_halo.unpack(pack_t, out_grid)
    for part in sums:
        part.back_to_core()
    gx_halo.wait()
    gx_halo.unpack(pack_t, gx_grid)
    for part in sums:
        part.finish()
    for part in sums:
        part.drain()


def block_call(x, ct, bias, gain_attn, w_qkv, w_proj, gain_mlp, w_up, w_down):
    shape = jax.ShapeDtypeStruct
    args = (x, ct, bias, gain_attn, w_qkv, w_proj, gain_mlp, w_up, w_down)
    sem = pltpu.SemaphoreType.DMA
    return pl.pallas_call(
        block_kernel,
        out_shape=(
            shape((TOK, C), BF16),
            shape((TOK, C), BF16),
            *[shape((rows, 128), BF16) for rows in ROWS],
        ),
        in_specs=[HBM] * 9,
        out_specs=(VMEM,) * 5,
        scratch_shapes=[
            *[pltpu.VMEM(arg.shape, arg.dtype) for arg in args], sem((9,)),
            pltpu.VMEM((PACKED, PAIR), BF16),
            pltpu.VMEM((PAIR, PACKED), BF16),
            pltpu.VMEM((PACKED, PAIR), BF16),
            pltpu.VMEM((PAIR, PACKED), BF16),
            pltpu.VMEM((TOK, C), BF16),
            pltpu.VMEM((TOK, C), BF16),
            pltpu.VMEM((TOK, C), BF16),
            pltpu.VMEM((TOK, C), BF16),
            pltpu.VMEM((HEADS * WTOK, WTOK), F32),
            pltpu.VMEM((4 * HEADS, WTOK, WTOK), F32),
            pltpu.VMEM((4, HEADS * WTOK, WTOK), BF16),
            pltpu.VMEM((4, HEADS * WTOK, C), BF16),
            pltpu.VMEM((4, HEADS * WTOK, C), BF16),
            pltpu.VMEM((TOK, C), BF16),
            *[pltpu.VMEM((C, TOK), BF16)] * 4,
            pltpu.VMEM((TOK, C), BF16),
            pltpu.VMEM((TOK, C), BF16),
            pltpu.VMEM((TOK, C), BF16),
            pltpu.VMEM((TOK, C), BF16),
            pltpu.VMEM((TOK, FF), BF16),
            pltpu.VMEM((TOK, FF), BF16),
            pltpu.VMEM((TOK, 3 * C), BF16),
            pltpu.VMEM((TOK, C), BF16),
            pltpu.VMEM((4, PACKED, 2 * C), BF16),
            pltpu.VMEM((4, PACKED - STAY, 2 * C), BF16),
            sem((4, 3)), sem((4, 3)),
            *[pltpu.VMEM((rows, 128), BF16) for rows in ROWS],
            *[ref for kind, size in PARTS for ref in sum_scratch(kind, size)],
        ],
        compiler_params=pltpu.CompilerParams(
            collective_id=0, has_side_effects=True, vmem_limit_bytes=56 * 2**20
        ),
        name="block",
    )(*args)


def finish_kernel(
    out_in, gx_in, full0_hbm, full1_hbm, full2_hbm, wqkv_hbm, wup_hbm, gain_a_hbm, gain_m_hbm,
    out_hbm, gx_hbm, qkv_hbm, proj_hbm, up_hbm, down_hbm, ga_hbm, gm_hbm,
    full0, full1, full2, wqkv, wup, gain_a, gain_m,
    out_ref, gx_ref, qkv_ref, proj_ref, up_ref, down_ref, ga_ref, gm_ref, in_sem, out_sem,
):
    def read(i, src, dst):
        copy = pltpu.make_async_copy(src, dst, in_sem.at[i])
        copy.start()
        return copy

    written = []

    def write(i, src, dst):
        written.append(pltpu.make_async_copy(src, dst, out_sem.at[i]))
        written[-1].start()

    def block(full, t):
        return full[t * C:(t + 1) * C, :].astype(F32) * FACTOR

    copies = [
        read(i, src, dst) for i, (src, dst) in enumerate((
            (full0_hbm, full0), (full1_hbm, full1), (full2_hbm, full2), (out_in, out_ref),
            (gx_in, gx_ref), (wqkv_hbm, wqkv), (wup_hbm, wup), (gain_a_hbm, gain_a),
            (gain_m_hbm, gain_m),
        ))
    ]
    copies[0].wait()
    for t in range(6):
        down_ref[:, t * 128:(t + 1) * 128] = block(full0, t)
    write(0, down_ref, down_hbm)
    copies[1].wait()
    for t in range(6):
        up_ref[:, t * 128:(t + 1) * 128] = block(full1, t) if t < 5 else block(full0, 7)
    write(1, up_ref, up_hbm)
    copies[2].wait()
    for t in range(4):
        qkv_ref[:, t * 128:(t + 1) * 128] = block(full2, t)
    mixed_tile = block(full2, 4)
    qkv_ref[:, 512:] = mixed_tile[:, :64]
    write(2, qkv_ref, qkv_hbm)
    proj_ref[:, :128] = block(full0, 6)
    proj_ref[:, 128:] = mixed_tile[:, 64:]
    write(3, proj_ref, proj_hbm)
    copies[3].wait()
    write(4, out_ref, out_hbm)
    copies[4].wait()
    write(5, gx_ref, gx_hbm)
    for copy in copies[5:]:
        copy.wait()
    for weight, grad, gain, ref in ((wqkv, qkv_ref, gain_a, ga_ref), (wup, up_ref, gain_m, gm_ref)):
        product = weight[...].astype(F32) * grad[...]
        total = lax.dot_general(
            jnp.ones((8, product.shape[1]), F32), product, (((1,), (1,)), ((), ())),
            precision=lax.Precision.HIGHEST, preferred_element_type=F32,
        )
        ref[...] = total[:1] / gain[...]
    write(6, ga_ref, ga_hbm)
    write(7, gm_ref, gm_hbm)
    for copy in written:
        copy.wait()


def finish_call(out, gx, full, w_qkv, w_up, gain_attn, gain_mlp):
    shape = jax.ShapeDtypeStruct
    results = (
        shape((TOK, C), BF16),
        shape((TOK, C), BF16),
        shape((C, 3 * C), F32),
        shape((C, C), F32),
        shape((C, FF), F32),
        shape((C, FF), F32),
        shape((1, C), F32),
        shape((1, C), F32),
    )
    return pl.pallas_call(
        finish_kernel,
        out_shape=results,
        in_specs=[HBM] * 9,
        out_specs=(HBM,) * 8,
        scratch_shapes=[
            *[pltpu.VMEM((rows, 128), BF16) for rows in ROWS],
            pltpu.VMEM((C, 3 * C), BF16),
            pltpu.VMEM((C, FF), BF16),
            pltpu.VMEM((1, C), F32),
            pltpu.VMEM((1, C), F32),
            *[pltpu.VMEM(result.shape, result.dtype) for result in results],
            pltpu.SemaphoreType.DMA((9,)),
            pltpu.SemaphoreType.DMA((8,)),
        ],
        compiler_params=pltpu.CompilerParams(vmem_limit_bytes=56 * 2**20),
        name="finish",
    )(out, gx, *full, w_qkv, w_up, gain_attn, gain_mlp)


def body(fields, gain_attn, w_qkv, bias, w_proj, gain_mlp, w_up, w_down, cotangent):
    out, gx, *full = block_call(
        fields.reshape(TOK, C), cotangent.reshape(TOK, C), bias.reshape(HEADS * WTOK, WTOK),
        gain_attn.reshape(1, C), w_qkv, w_proj, gain_mlp.reshape(1, C), w_up, w_down.T,
    )
    out, gx, qkv, proj, up, down, ga, gm = finish_call(
        out, gx, full, w_qkv, w_up, gain_attn.reshape(1, C), gain_mlp.reshape(1, C),
    )
    return (
        out.reshape(fields.shape), gx.reshape(fields.shape), qkv, proj, up, down.T,
        ga.reshape(C), gm.reshape(C),
    )


def solution(mesh):
    grid = P(None, "lat", "lon", None)
    in_specs = (grid, P(), P(), P("lat", None, None, None), P(), P(), P(), P(), grid)
    out_specs = (grid, grid, P(), P(), P(), P(), P(), P())
    return jax.shard_map(body, mesh=mesh, in_specs=in_specs, out_specs=out_specs, check_vma=False)
```

```python
import jax
import jax.numpy as jnp
from jax import lax
from jax.experimental import pallas as pl
from jax.experimental.pallas import tpu as pltpu
from jax.sharding import PartitionSpec as P

WLAT = 6
WLON = 12
WTOK = 144
HEADS = 6
HEAD = 32
C = 192
FF = 768
TOK = 576
NORM_EPS = 1e-05
MASKED = -1e30
FACTOR = 1.0 / 384.0

STAY = 112
PACKED = 320
PIECES = ((112, 112), (224, 48), (272, 48))
PAIR = 288

ROWS = (1536, 1024, 1024)

F32 = jnp.float32
BF16 = jnp.bfloat16
MESH = pl.DeviceIdType.MESH
VMEM = pl.BlockSpec(memory_space=pltpu.VMEM)
HBM = pl.BlockSpec(memory_space=pltpu.HBM)


def nn(left, right):
    return lax.dot_general(left, right, (((1,), (0,)), ((), ())), preferred_element_type=F32)


def nt(left, right):
    return lax.dot_general(left, right, (((1,), (1,)), ((), ())), preferred_element_type=F32)


def tn(left, right):
    return lax.dot_general(left, right, (((0,), (0,)), ((), ())), preferred_element_type=F32)


def row_mean(values):
    return jnp.sum(values, axis=-1, keepdims=True) * (1.0 / C)


def normalize(values):
    center = values - row_mean(values)
    inv = lax.rsqrt(row_mean(center * center) + NORM_EPS)
    return center * inv, inv


def norm_back(unit, inv, gain, upstream):
    scaled = upstream * gain
    grad = inv * (scaled - row_mean(scaled) - unit * row_mean(scaled * unit))
    return grad


def head_masks():
    head_of = lax.broadcasted_iota(jnp.int32, (1, C), 1) // HEAD
    return [jnp.where(head_of == h, 1.0, 0.0).astype(BF16) for h in range(HEADS)]


def piece_row(level, row, col):
    stay_row = row >= 3
    low = jnp.where(stay_row, row - 3, row)
    wide = level * 54 + low * 18 + col - 6
    thin = level * 18 + low * 6 + col
    right = jnp.where(stay_row, wide, wide + PIECES[0][0])
    left = jnp.where(stay_row, thin + PIECES[1][0], thin + PIECES[2][0])
    return jnp.where(col >= 6, right, left)


def pack_rows(token):
    return piece_row(token // 144, token % 144 // 24, token % 24)


def place_rows(token):
    col = token % WLON + token // 144 * WLON
    return piece_row(token % 144 // 72, (token % 72 // WLON + 3) % 6, (col + 6) % 24)


def table(rows_of):
    token = lax.broadcasted_iota(jnp.int32, (1, PAIR), 1)
    piece = lax.broadcasted_iota(jnp.int32, (PACKED, PAIR), 0)
    return jnp.where(piece == rows_of(token), 1.0, 0.0).astype(BF16)


def table_t(rows_of):
    token = lax.broadcasted_iota(jnp.int32, (PAIR, 1), 0)
    piece = lax.broadcasted_iota(jnp.int32, (PAIR, PACKED), 1)
    return jnp.where(piece == rows_of(token), 1.0, 0.0).astype(BF16)


def remote(src, dst, send_sem, recv_sem, device):
    return pltpu.make_async_remote_copy(
        src_ref=src, dst_ref=dst, send_sem=send_sem, recv_sem=recv_sem,
        device_id=device, device_id_type=MESH,
    )


def ring(index, step, size):
    return lax.rem(index + step + size, size)


def chunk(start, size):
    return pl.ds(pl.multiple_of(start, 16), size)


def near(steps, size):
    return sorted(steps, key=lambda step: sum(min(d, n - d) for d, n in zip(step, size)))


PLANE = near([(dy, dx) for dy in range(4) for dx in range(4) if (dy, dx) != (0, 0)], (4, 4))
RING = [dz for dz, in near([(dz,) for dz in range(1, 8)], (8,))]


class Place:
    def __init__(self):
        self.lon, self.lat = lax.axis_index("lon"), lax.axis_index("lat")
        self.core = lax.rem(self.lon, 2)
        self.x = lax.rem(self.lon // 2, 4)
        self.y = self.lat // 8 * 2 + self.lon // 8
        self.z = lax.rem(self.lat, 8)

    def device(self, y, x, z, core):
        return ((lax.rem(y, 2) * 4 + x) * 2 + core, y // 2 * 8 + z)

    def other_core(self):
        return self.device(self.y, self.x, self.z, 1 - self.core)

    def plane_spot(self, dy, dx):
        return ring(self.y, dy, 4), ring(self.x, dx, 4)

    def plane_peer(self, dy, dx):
        y, x = self.plane_spot(dy, dx)
        return self.device(y, x, self.z, self.core)

    def z_peer(self, dz):
        return self.device(self.y, self.x, ring(self.z, dz, 8), self.core)

    def halo_targets(self, step):
        lon, lat = ring(self.lon, step, 16), ring(self.lat, step, 16)
        return (self.lon, lat), (lon, self.lat), (lon, lat)

    def everyone(self):
        devices = list(self.halo_targets(-1)) + list(self.halo_targets(1)) + [self.other_core()]
        devices += [self.plane_peer(dy, dx) for dy, dx in PLANE]
        return devices + [self.z_peer(dz) for dz in range(1, 8)]


class Halo:
    def __init__(self, spot, packed, landed, send_sem, recv_sem, step):
        targets = spot.halo_targets(step)
        self.packed, self.landed = packed, landed
        self.copies = [
            remote(
                packed.at[pl.ds(start, size), :], landed.at[pl.ds(start - STAY, size), :],
                send_sem.at[i], recv_sem.at[i], targets[i],
            )
            for i, (start, size) in enumerate(PIECES)
        ]

    def start(self):
        for copy in self.copies:
            copy.start()

    def wait(self):
        for copy in self.copies:
            copy.wait()

    def pack(self, ref, table_ref):
        pairs = [ref[i * PAIR:(i + 1) * PAIR, :].astype(F32) for i in range(2)]
        both = jnp.concatenate(pairs, axis=1).astype(BF16)
        self.packed[...] = nn(table_ref[...], both).astype(BF16)

    def unpack(self, table_ref, ref):
        both = nn(table_ref[:, :STAY], self.packed[:STAY, :]) + nn(table_ref[:, STAY:], self.landed[...])
        for i in range(2):
            ref[i * PAIR:(i + 1) * PAIR, :] = both[:, i * C:(i + 1) * C].astype(BF16)


class Sum:
    def __init__(self, spot, flat, full, scratch):
        self.spot, self.flat, self.full = spot, flat, full
        (self.core_in, self.out, self.first_in, self.second_in, core, first_s, first_r,
         second_s, second_r, back_s, back_r, last) = scratch
        self.core_sems = core.at[0], core.at[1]
        self.first_sems, self.second_sems = (first_s, first_r), (second_s, second_r)
        self.back_sems, self.last_sems = (back_s, back_r), (last.at[0], last.at[1])
        self.size = self.first_in.shape[1]
        self.sent = []
        self.count = self.first_in.shape[0] + 1
        self.half = spot.core * (self.count * self.size)
        self.own = self.first_here() * self.size

    def launch(self, src, dst, sems, device, index=None):
        send_sem, recv_sem = sems if index is None else (sems[0].at[index], sems[1].at[index])
        copy = remote(src, dst, send_sem, recv_sem, device)
        copy.start()
        self.sent.append(copy)
        return copy

    def far_first(self, steps, make):
        copies = [make(k, steps[k]) for k in reversed(range(len(steps)))]
        return copies[::-1]

    def to_core(self):
        other = self.count * self.size - self.half
        self.core_copy = self.launch(
            self.flat.at[chunk(other, self.count * self.size)], self.core_in,
            self.core_sems, self.spot.other_core(),
        )

    def to_first(self):
        self.core_copy.wait_recv()
        mine = self.flat[chunk(self.half, self.count * self.size), :].astype(F32)
        self.out[...] = (mine + self.core_in[...].astype(F32)).astype(BF16)
        self.first_copies = self.far_first(self.first_steps, lambda k, step: self.launch(
            self.out.at[chunk(self.first_index(step) * self.size, self.size)],
            self.first_in.at[k], self.first_sems, self.first_peer(step), k,
        ))

    def to_second(self):
        total = self.out[chunk(self.own, self.size), :].astype(F32)
        for k, copy in enumerate(self.first_copies):
            copy.wait_recv()
            total = total + self.first_in[k].astype(F32)
        mine = self.second_in.at[self.second_here()]
        mine[...] = total.astype(BF16)
        self.second_copies = self.far_first(self.second_steps, lambda k, step: self.launch(
            mine, mine, self.second_sems, self.second_peer(step), k,
        ))

    def back_to_first(self):
        for copy in self.second_copies:
            copy.wait_recv()
        total = self.second_in[0].astype(F32)
        for i in range(1, len(self.second_steps) + 1):
            total = total + self.second_in[i].astype(F32)
        own = self.full.at[chunk(self.half + self.own, self.size)]
        own[...] = total.astype(BF16)
        self.back_copies = self.far_first(self.first_steps, lambda k, step: self.launch(
            own, own, self.back_sems, self.first_peer(step), k,
        ))

    def back_to_core(self):
        for copy in self.back_copies:
            copy.wait_recv()
        rows = self.full.at[chunk(self.half, self.count * self.size)]
        self.last_copy = self.launch(rows, rows, self.last_sems, self.spot.other_core())

    def finish(self):
        self.last_copy.wait_recv()

    def drain(self):
        for copy in self.sent:
            copy.wait_send()


class PlaneSum(Sum):
    first_steps, second_steps = PLANE, RING

    def first_here(self):
        return self.spot.y * 4 + self.spot.x

    def first_index(self, step):
        y, x = self.spot.plane_spot(*step)
        return y * 4 + x

    def first_peer(self, step):
        return self.spot.plane_peer(*step)

    def second_here(self):
        return self.spot.z

    def second_peer(self, step):
        return self.spot.z_peer(step)


class RingSum(Sum):
    first_steps, second_steps = RING, PLANE

    def first_here(self):
        return self.spot.z

    def first_index(self, step):
        return ring(self.spot.z, step, 8)

    def first_peer(self, step):
        return self.spot.z_peer(step)

    def second_here(self):
        return self.spot.y * 4 + self.spot.x

    def second_peer(self, step):
        return self.spot.plane_peer(*step)


def sum_scratch(kind, size):
    first, second = len(kind.first_steps), len(kind.second_steps)
    sem = pltpu.SemaphoreType.DMA
    return [
        pltpu.VMEM(((first + 1) * size, 128), BF16),
        pltpu.VMEM(((first + 1) * size, 128), BF16),
        pltpu.VMEM((first, size, 128), BF16),
        pltpu.VMEM((second + 1, size, 128), BF16),
        sem((2,)), sem((first,)), sem((first,)), sem((second,)), sem((second,)),
        sem((first,)), sem((first,)), sem((2,)),
    ]


PARTS = ((PlaneSum, 48), (RingSum, 64), (PlaneSum, 32))


def block_kernel(
    x_hbm, ct_hbm, bias_hbm, ga_hbm, wqkv_hbm, wproj_hbm, gm_hbm, wup_hbm, wdown_hbm,
    out_grid, gx_grid, full0, full1, full2,
    x_in, ct_in, bias_in, ga_in, wqkv_in, wproj_in, gm_in, wup_in, wdown_in, load_sem,
    pack, pack_t, place, place_t,
    x_ref, ct_ref, out_ref, gx_ref, bias32, probs, weights, km_s, vm_s, q_s,
    normed_t, nm_t, mixed_t, ct_t, mixed_s, hid_s, hid_grad_s, nm_s, act_s, gpre_s, gqkv_s, gattn_s,
    packed, landed, halo_send, halo_recv, flat0, flat1, flat2, *sum_refs,
):
    spot = Place()
    barrier = pltpu.get_barrier_semaphore()
    devices = spot.everyone()
    for device in devices[:6]:
        pl.semaphore_signal(barrier, inc=1, device_id=device, device_id_type=MESH)
    loads = []
    for i, (src, dst) in enumerate((
        (x_hbm, x_in), (ct_hbm, ct_in), (bias_hbm, bias_in), (ga_hbm, ga_in), (wqkv_hbm, wqkv_in),
        (wproj_hbm, wproj_in), (gm_hbm, gm_in), (wup_hbm, wup_in), (wdown_hbm, wdown_in),
    )):
        loads.append(pltpu.make_async_copy(src, dst, load_sem.at[i]))
        loads[-1].start()
    for device in devices[6:]:
        pl.semaphore_signal(barrier, inc=1, device_id=device, device_id_type=MESH)
    halos = [
        Halo(spot, packed.at[a], landed.at[a], halo_send.at[a], halo_recv.at[a], step)
        for a, step in enumerate((-1, -1, 1, 1))
    ]
    x_halo, ct_halo, out_halo, gx_halo = halos
    sums = []
    for i, (kind, _) in enumerate(PARTS):
        flat, full = ((flat0, full0), (flat1, full1), (flat2, full2))[i]
        count = len(sum_refs) // len(PARTS)
        sums.append(kind(spot, flat, full, sum_refs[i * count:(i + 1) * count]))
    early, late = sums[:2], sums[2]

    pack[...] = table(pack_rows)
    loads[0].wait()
    x_halo.pack(x_in, pack)
    pl.semaphore_wait(barrier, len(devices))
    x_halo.start()
    pack_t[...] = table_t(pack_rows)
    flat1[5 * C:, :] = jnp.zeros((ROWS[1] - 5 * C, 128), BF16)
    flat2[5 * C:, :] = jnp.zeros((ROWS[2] - 5 * C, 128), BF16)
    place[...] = table(place_rows)
    place_t[...] = table_t(place_rows)
    loads[1].wait()
    ct_halo.pack(ct_in, pack)
    ct_halo.start()
    loads[2].wait()
    is_last = spot.lat == lax.axis_size("lat") - 1
    row_half = (lax.broadcasted_iota(jnp.int32, (WTOK, 1), 0) // WLON) % WLAT < WLAT // 2
    col_half = (lax.broadcasted_iota(jnp.int32, (1, WTOK), 1) // WLON) % WLAT < WLAT // 2
    cut = jnp.logical_and(row_half != col_half, is_last)
    penalty = jnp.where(cut, MASKED, 0.0)
    for h in range(HEADS):
        rows = slice(h * WTOK, (h + 1) * WTOK)
        bias32[rows, :] = bias_in[rows, :].astype(F32).T + penalty
    for load in loads[3:]:
        load.wait()
    x_halo.wait()
    x_halo.unpack(place_t, x_ref)

    scale = HEAD ** (-0.5)
    masks = head_masks()
    ga = ga_in[...]
    gm = gm_in[...]

    def forward():
        x = x_ref[...].astype(F32)
        unit, _ = normalize(x)
        normed = (unit * ga).astype(BF16)
        normed_t[...] = normed.T
        qkv = nn(normed, wqkv_in[...]).astype(BF16)
        q_s[...] = qkv[:, :C]
        k = qkv[:, C:2 * C]
        v = qkv[:, 2 * C:]
        for n in range(4):
            rows = slice(n * WTOK, (n + 1) * WTOK)
            km = jnp.concatenate([k[rows] * masks[h] for h in range(HEADS)], axis=0)
            vm = jnp.concatenate([v[rows] * masks[h] for h in range(HEADS)], axis=0)
            km_s[n] = km
            vm_s[n] = vm
            s = (nt(km, q_s[rows, :]) * scale + bias32[...]).reshape(HEADS, WTOK, WTOK)
            e = jnp.exp(s - jnp.max(s, axis=1, keepdims=True))
            p = e * (1.0 / jnp.sum(e, axis=1, keepdims=True))
            probs[n * HEADS:(n + 1) * HEADS] = p
            weights[n] = p.astype(BF16).reshape(HEADS * WTOK, WTOK)
            mixed_s[rows, :] = tn(weights[n], vm).astype(BF16)

    def mlp():
        hidden = (x_ref[...].astype(F32) + nn(mixed_s[...], wproj_in[...])).astype(BF16)
        hid_s[...] = hidden
        unit, inv = normalize(hidden.astype(F32))
        nm_s[...] = (unit * gm).astype(BF16)
        nm_t[...] = nm_s[...].T
        grad_nm = jnp.zeros((TOK, C), F32)
        for f in range(3):
            cols = slice(f * 256, (f + 1) * 256)
            z = nn(nm_s[...], wup_in[:, cols])
            phi = 0.5 * (1.0 + lax.erf(z * (0.5 ** 0.5)))
            act_s[:, cols] = (z * phi).astype(BF16)
            slope = phi + z * (jnp.exp(-0.5 * z * z) * 0.3989422804014327)
            gpre = (nn(ct_ref[...], wdown_in[:, cols]) * slope).astype(BF16)
            gpre_s[:, cols] = gpre
            grad_nm = grad_nm + nt(gpre, wup_in[:, cols])
        grad_hidden = (ct_ref[...].astype(F32) + norm_back(unit, inv, gm, grad_nm)).astype(BF16)
        hid_grad_s[...] = grad_hidden
        gattn_s[...] = nt(grad_hidden, wproj_in[...]).astype(BF16)

    def attention_back(n):
        rows = slice(n * WTOK, (n + 1) * WTOK)
        up = gattn_s[rows, :]
        p = probs[n * HEADS:(n + 1) * HEADS]
        gp = nt(vm_s[n], up).reshape(HEADS, WTOK, WTOK)
        inner = jnp.sum(p * gp, axis=1, keepdims=True)
        gs = (p * (gp - inner) * scale).astype(BF16).reshape(HEADS * WTOK, WTOK)
        gv_all = nn(weights[n], up)
        gk_all = nn(gs, q_s[rows, :])
        gq = tn(gs, km_s[n])
        gk = jnp.zeros((WTOK, C), F32)
        gv = jnp.zeros((WTOK, C), F32)
        for h in range(HEADS):
            gk = jnp.where(masks[h] > 0, gk_all[h * WTOK:(h + 1) * WTOK], gk)
            gv = jnp.where(masks[h] > 0, gv_all[h * WTOK:(h + 1) * WTOK], gv)
        gqkv_s[rows, :] = jnp.concatenate([gq, gk, gv], axis=1).astype(BF16)

    def output():
        out_ref[...] = (hid_s[...].astype(F32) + nt(act_s[...], wdown_in[...])).astype(BF16)

    def input_grad():
        grad_rolled = nt(gqkv_s[...], wqkv_in[...]).astype(BF16).astype(F32)
        unit, inv = normalize(x_ref[...].astype(F32))
        grad_x = norm_back(unit, inv, ga, grad_rolled)
        gx_ref[...] = (hid_grad_s[...].astype(F32) + grad_x).astype(BF16)

    def store_blocks(flat, base, values):
        for t in range(values.shape[1] // 128):
            flat[base + t * C:base + (t + 1) * C, :] = values[:, t * 128:(t + 1) * 128].astype(BF16)

    forward()
    mixed_t[...] = mixed_s[...].T
    ct_halo.wait()
    ct_halo.unpack(place_t, ct_ref)
    ct_t[...] = ct_ref[...].T
    mlp()
    grad_up = nn(nm_t[...], gpre_s[...])
    grad_proj = nn(mixed_t[...], hid_grad_s[...])
    store_blocks(flat1, 0, grad_up[:, :640])
    store_blocks(flat0, 0, nn(ct_t[...], act_s[...]))
    store_blocks(flat0, 6 * C, grad_proj)
    store_blocks(flat0, 7 * C, grad_up[:, 640:])
    for part in early:
        part.to_core()
    output()
    out_halo.pack(out_ref, place)
    for part in early:
        part.to_first()
    out_halo.start()
    for n in range(4):
        attention_back(n)
    grad_qkv = nn(normed_t[...], gqkv_s[...])
    store_blocks(flat2, 0, grad_qkv)
    store_blocks(flat2, 4 * C, jnp.concatenate([grad_qkv[:, 512:], grad_proj[:, 128:]], axis=1))
    late.to_core()
    late.to_first()
    input_grad()
    gx_halo.pack(gx_ref, place)
    gx_halo.start()
    for part in sums:
        part.to_second()
    out_halo.wait()
    out_halo.unpack(pack_t, out_grid)
    for part in sums:
        part.back_to_first()
    gx_halo.wait()
    gx_halo.unpack(pack_t, gx_grid)
    for part in sums:
        part.back_to_core()
    for part in sums:
        part.finish()
    for part in sums:
        part.drain()


def block_call(x, ct, bias, gain_attn, w_qkv, w_proj, gain_mlp, w_up, w_down):
    shape = jax.ShapeDtypeStruct
    args = (x, ct, bias, gain_attn, w_qkv, w_proj, gain_mlp, w_up, w_down)
    sem = pltpu.SemaphoreType.DMA
    return pl.pallas_call(
        block_kernel,
        out_shape=(
            shape((TOK, C), BF16),
            shape((TOK, C), BF16),
            *[shape((rows, 128), BF16) for rows in ROWS],
        ),
        in_specs=[HBM] * 9,
        out_specs=(VMEM,) * 5,
        scratch_shapes=[
            *[pltpu.VMEM(arg.shape, arg.dtype) for arg in args], sem((9,)),
            pltpu.VMEM((PACKED, PAIR), BF16),
            pltpu.VMEM((PAIR, PACKED), BF16),
            pltpu.VMEM((PACKED, PAIR), BF16),
            pltpu.VMEM((PAIR, PACKED), BF16),
            pltpu.VMEM((TOK, C), BF16),
            pltpu.VMEM((TOK, C), BF16),
            pltpu.VMEM((TOK, C), BF16),
            pltpu.VMEM((TOK, C), BF16),
            pltpu.VMEM((HEADS * WTOK, WTOK), F32),
            pltpu.VMEM((4 * HEADS, WTOK, WTOK), F32),
            pltpu.VMEM((4, HEADS * WTOK, WTOK), BF16),
            pltpu.VMEM((4, HEADS * WTOK, C), BF16),
            pltpu.VMEM((4, HEADS * WTOK, C), BF16),
            pltpu.VMEM((TOK, C), BF16),
            *[pltpu.VMEM((C, TOK), BF16)] * 4,
            pltpu.VMEM((TOK, C), BF16),
            pltpu.VMEM((TOK, C), BF16),
            pltpu.VMEM((TOK, C), BF16),
            pltpu.VMEM((TOK, C), BF16),
            pltpu.VMEM((TOK, FF), BF16),
            pltpu.VMEM((TOK, FF), BF16),
            pltpu.VMEM((TOK, 3 * C), BF16),
            pltpu.VMEM((TOK, C), BF16),
            pltpu.VMEM((4, PACKED, 2 * C), BF16),
            pltpu.VMEM((4, PACKED - STAY, 2 * C), BF16),
            sem((4, 3)), sem((4, 3)),
            *[pltpu.VMEM((rows, 128), BF16) for rows in ROWS],
            *[ref for kind, size in PARTS for ref in sum_scratch(kind, size)],
        ],
        compiler_params=pltpu.CompilerParams(
            collective_id=0, has_side_effects=True, vmem_limit_bytes=56 * 2**20
        ),
        name="block",
    )(*args)


def finish_kernel(
    out_in, gx_in, full0_hbm, full1_hbm, full2_hbm, wqkv_hbm, wup_hbm, gain_a_hbm, gain_m_hbm,
    out_hbm, gx_hbm, qkv_hbm, proj_hbm, up_hbm, down_hbm, ga_hbm, gm_hbm,
    full0, full1, full2, wqkv, wup, gain_a, gain_m,
    out_ref, gx_ref, qkv_ref, proj_ref, up_ref, down_ref, ga_ref, gm_ref, in_sem, out_sem,
):
    def read(i, src, dst):
        copy = pltpu.make_async_copy(src, dst, in_sem.at[i])
        copy.start()
        return copy

    written = []

    def write(i, src, dst):
        written.append(pltpu.make_async_copy(src, dst, out_sem.at[i]))
        written[-1].start()

    def block(full, t):
        return full[t * C:(t + 1) * C, :].astype(F32) * FACTOR

    copies = [
        read(i, src, dst) for i, (src, dst) in enumerate((
            (full0_hbm, full0), (full1_hbm, full1), (full2_hbm, full2), (out_in, out_ref),
            (gx_in, gx_ref), (wqkv_hbm, wqkv), (wup_hbm, wup), (gain_a_hbm, gain_a),
            (gain_m_hbm, gain_m),
        ))
    ]
    copies[0].wait()
    for t in range(6):
        down_ref[:, t * 128:(t + 1) * 128] = block(full0, t)
    write(0, down_ref, down_hbm)
    copies[1].wait()
    for t in range(6):
        up_ref[:, t * 128:(t + 1) * 128] = block(full1, t) if t < 5 else block(full0, 7)
    write(1, up_ref, up_hbm)
    copies[2].wait()
    for t in range(4):
        qkv_ref[:, t * 128:(t + 1) * 128] = block(full2, t)
    mixed_tile = block(full2, 4)
    qkv_ref[:, 512:] = mixed_tile[:, :64]
    write(2, qkv_ref, qkv_hbm)
    proj_ref[:, :128] = block(full0, 6)
    proj_ref[:, 128:] = mixed_tile[:, 64:]
    write(3, proj_ref, proj_hbm)
    copies[3].wait()
    write(4, out_ref, out_hbm)
    copies[4].wait()
    write(5, gx_ref, gx_hbm)
    for copy in copies[5:]:
        copy.wait()
    for weight, grad, gain, ref in ((wqkv, qkv_ref, gain_a, ga_ref), (wup, up_ref, gain_m, gm_ref)):
        product = weight[...].astype(F32) * grad[...]
        total = lax.dot_general(
            jnp.ones((8, product.shape[1]), F32), product, (((1,), (1,)), ((), ())),
            precision=lax.Precision.HIGHEST, preferred_element_type=F32,
        )
        ref[...] = total[:1] / gain[...]
    write(6, ga_ref, ga_hbm)
    write(7, gm_ref, gm_hbm)
    for copy in written:
        copy.wait()


def finish_call(out, gx, full, w_qkv, w_up, gain_attn, gain_mlp):
    shape = jax.ShapeDtypeStruct
    results = (
        shape((TOK, C), BF16),
        shape((TOK, C), BF16),
        shape((C, 3 * C), F32),
        shape((C, C), F32),
        shape((C, FF), F32),
        shape((C, FF), F32),
        shape((1, C), F32),
        shape((1, C), F32),
    )
    return pl.pallas_call(
        finish_kernel,
        out_shape=results,
        in_specs=[HBM] * 9,
        out_specs=(HBM,) * 8,
        scratch_shapes=[
            *[pltpu.VMEM((rows, 128), BF16) for rows in ROWS],
            pltpu.VMEM((C, 3 * C), BF16),
            pltpu.VMEM((C, FF), BF16),
            pltpu.VMEM((1, C), F32),
            pltpu.VMEM((1, C), F32),
            *[pltpu.VMEM(result.shape, result.dtype) for result in results],
            pltpu.SemaphoreType.DMA((9,)),
            pltpu.SemaphoreType.DMA((8,)),
        ],
        compiler_params=pltpu.CompilerParams(vmem_limit_bytes=56 * 2**20),
        name="finish",
    )(out, gx, *full, w_qkv, w_up, gain_attn, gain_mlp)


def body(fields, gain_attn, w_qkv, bias, w_proj, gain_mlp, w_up, w_down, cotangent):
    out, gx, *full = block_call(
        fields.reshape(TOK, C), cotangent.reshape(TOK, C), bias.reshape(HEADS * WTOK, WTOK),
        gain_attn.reshape(1, C), w_qkv, w_proj, gain_mlp.reshape(1, C), w_up, w_down.T,
    )
    out, gx, qkv, proj, up, down, ga, gm = finish_call(
        out, gx, full, w_qkv, w_up, gain_attn.reshape(1, C), gain_mlp.reshape(1, C),
    )
    return (
        out.reshape(fields.shape), gx.reshape(fields.shape), qkv, proj, up, down.T,
        ga.reshape(C), gm.reshape(C),
    )


def solution(mesh):
    grid = P(None, "lat", "lon", None)
    in_specs = (grid, P(), P(), P("lat", None, None, None), P(), P(), P(), P(), grid)
    out_specs = (grid, grid, P(), P(), P(), P(), P(), P())
    return jax.shard_map(body, mesh=mesh, in_specs=in_specs, out_specs=out_specs, check_vma=False)
```

```python
import jax
import jax.numpy as jnp
from jax import lax
from jax.experimental import pallas as pl
from jax.experimental.pallas import tpu as pltpu
from jax.sharding import PartitionSpec as P

WLAT = 6
WLON = 12
WTOK = 144
HEADS = 6
HEAD = 32
C = 192
FF = 768
TOK = 576
NORM_EPS = 1e-05
MASKED = -1e30
FACTOR = 1.0 / 384.0

STAY = 112
PACKED = 320
PIECES = ((112, 112), (224, 48), (272, 48))
PAIR = 288

ROWS = (1536, 1024, 1024)

F32 = jnp.float32
BF16 = jnp.bfloat16
MESH = pl.DeviceIdType.MESH
VMEM = pl.BlockSpec(memory_space=pltpu.VMEM)
HBM = pl.BlockSpec(memory_space=pltpu.HBM)


def nn(left, right):
    return lax.dot_general(left, right, (((1,), (0,)), ((), ())), preferred_element_type=F32)


def nt(left, right):
    return lax.dot_general(left, right, (((1,), (1,)), ((), ())), preferred_element_type=F32)


def tn(left, right):
    return lax.dot_general(left, right, (((0,), (0,)), ((), ())), preferred_element_type=F32)


def row_mean(values):
    return jnp.sum(values, axis=-1, keepdims=True) * (1.0 / C)


def normalize(values):
    center = values - row_mean(values)
    inv = lax.rsqrt(row_mean(center * center) + NORM_EPS)
    return center * inv, inv


def norm_back(unit, inv, gain, upstream):
    scaled = upstream * gain
    grad = inv * (scaled - row_mean(scaled) - unit * row_mean(scaled * unit))
    return grad


def head_masks():
    head_of = lax.broadcasted_iota(jnp.int32, (1, C), 1) // HEAD
    return [jnp.where(head_of == h, 1.0, 0.0).astype(BF16) for h in range(HEADS)]


def piece_row(level, row, col):
    stay_row = row >= 3
    low = jnp.where(stay_row, row - 3, row)
    wide = level * 54 + low * 18 + col - 6
    thin = level * 18 + low * 6 + col
    right = jnp.where(stay_row, wide, wide + PIECES[0][0])
    left = jnp.where(stay_row, thin + PIECES[1][0], thin + PIECES[2][0])
    return jnp.where(col >= 6, right, left)


def pack_rows(token):
    return piece_row(token // 144, token % 144 // 24, token % 24)


def place_rows(token):
    col = token % WLON + token // 144 * WLON
    return piece_row(token % 144 // 72, (token % 72 // WLON + 3) % 6, (col + 6) % 24)


def table(rows_of):
    token = lax.broadcasted_iota(jnp.int32, (1, PAIR), 1)
    piece = lax.broadcasted_iota(jnp.int32, (PACKED, PAIR), 0)
    return jnp.where(piece == rows_of(token), 1.0, 0.0).astype(BF16)


def table_t(rows_of):
    token = lax.broadcasted_iota(jnp.int32, (PAIR, 1), 0)
    piece = lax.broadcasted_iota(jnp.int32, (PAIR, PACKED), 1)
    return jnp.where(piece == rows_of(token), 1.0, 0.0).astype(BF16)


def remote(src, dst, send_sem, recv_sem, device):
    return pltpu.make_async_remote_copy(
        src_ref=src, dst_ref=dst, send_sem=send_sem, recv_sem=recv_sem,
        device_id=device, device_id_type=MESH,
    )


def ring(index, step, size):
    return lax.rem(index + step + size, size)


def chunk(start, size):
    return pl.ds(pl.multiple_of(start, 16), size)


def near(steps, size):
    return sorted(steps, key=lambda step: sum(min(d, n - d) for d, n in zip(step, size)))


PLANE = near([(dy, dx) for dy in range(4) for dx in range(4) if (dy, dx) != (0, 0)], (4, 4))
RING = [dz for dz, in near([(dz,) for dz in range(1, 8)], (8,))]


class Place:
    def __init__(self):
        self.lon, self.lat = lax.axis_index("lon"), lax.axis_index("lat")
        self.core = lax.rem(self.lon, 2)
        self.x = lax.rem(self.lon // 2, 4)
        self.y = self.lat // 8 * 2 + self.lon // 8
        self.z = lax.rem(self.lat, 8)

    def device(self, y, x, z, core):
        return ((lax.rem(y, 2) * 4 + x) * 2 + core, y // 2 * 8 + z)

    def other_core(self):
        return self.device(self.y, self.x, self.z, 1 - self.core)

    def plane_spot(self, dy, dx):
        return ring(self.y, dy, 4), ring(self.x, dx, 4)

    def plane_peer(self, dy, dx):
        y, x = self.plane_spot(dy, dx)
        return self.device(y, x, self.z, self.core)

    def z_peer(self, dz):
        return self.device(self.y, self.x, ring(self.z, dz, 8), self.core)

    def halo_targets(self, step):
        lon, lat = ring(self.lon, step, 16), ring(self.lat, step, 16)
        return (self.lon, lat), (lon, self.lat), (lon, lat)

    def everyone(self):
        devices = list(self.halo_targets(-1)) + list(self.halo_targets(1)) + [self.other_core()]
        devices += [self.plane_peer(dy, dx) for dy, dx in PLANE]
        return devices + [self.z_peer(dz) for dz in range(1, 8)]


class Halo:
    def __init__(self, spot, packed, landed, send_sem, recv_sem, step):
        targets = spot.halo_targets(step)
        self.packed, self.landed = packed, landed
        self.copies = [
            remote(
                packed.at[pl.ds(start, size), :], landed.at[pl.ds(start - STAY, size), :],
                send_sem.at[i], recv_sem.at[i], targets[i],
            )
            for i, (start, size) in enumerate(PIECES)
        ]

    def start(self):
        for copy in self.copies:
            copy.start()

    def wait(self):
        for copy in self.copies:
            copy.wait()

    def pack(self, ref, table_ref):
        pairs = [ref[i * PAIR:(i + 1) * PAIR, :].astype(F32) for i in range(2)]
        both = jnp.concatenate(pairs, axis=1).astype(BF16)
        self.packed[...] = nn(table_ref[...], both).astype(BF16)

    def unpack(self, table_ref, ref):
        both = nn(table_ref[:, :STAY], self.packed[:STAY, :]) + nn(table_ref[:, STAY:], self.landed[...])
        for i in range(2):
            ref[i * PAIR:(i + 1) * PAIR, :] = both[:, i * C:(i + 1) * C].astype(BF16)


class Sum:
    def __init__(self, spot, flat, full, scratch):
        self.spot, self.flat, self.full = spot, flat, full
        (self.core_in, self.out, self.first_in, self.second_in, core, first_s, first_r,
         second_s, second_r, back_s, back_r, last) = scratch
        self.core_sems = core.at[0], core.at[1]
        self.first_sems, self.second_sems = (first_s, first_r), (second_s, second_r)
        self.back_sems, self.last_sems = (back_s, back_r), (last.at[0], last.at[1])
        self.size = self.first_in.shape[1]
        self.sent = []
        self.count = self.first_in.shape[0] + 1
        self.half = spot.core * (self.count * self.size)
        self.own = self.first_here() * self.size

    def launch(self, src, dst, sems, device, index=None):
        send_sem, recv_sem = sems if index is None else (sems[0].at[index], sems[1].at[index])
        copy = remote(src, dst, send_sem, recv_sem, device)
        copy.start()
        self.sent.append(copy)
        return copy

    def far_first(self, steps, make):
        copies = [make(k, steps[k]) for k in reversed(range(len(steps)))]
        return copies[::-1]

    def to_core(self):
        other = self.count * self.size - self.half
        self.core_copy = self.launch(
            self.flat.at[chunk(other, self.count * self.size)], self.core_in,
            self.core_sems, self.spot.other_core(),
        )

    def to_first(self):
        self.core_copy.wait_recv()
        mine = self.flat[chunk(self.half, self.count * self.size), :].astype(F32)
        self.out[...] = (mine + self.core_in[...].astype(F32)).astype(BF16)
        self.first_copies = self.far_first(self.first_steps, lambda k, step: self.launch(
            self.out.at[chunk(self.first_index(step) * self.size, self.size)],
            self.first_in.at[k], self.first_sems, self.first_peer(step), k,
        ))

    def to_second(self):
        total = self.out[chunk(self.own, self.size), :].astype(F32)
        for k, copy in enumerate(self.first_copies):
            copy.wait_recv()
            total = total + self.first_in[k].astype(F32)
        mine = self.second_in.at[self.second_here()]
        mine[...] = total.astype(BF16)
        self.second_copies = self.far_first(self.second_steps, lambda k, step: self.launch(
            mine, mine, self.second_sems, self.second_peer(step), k,
        ))

    def back_to_first(self):
        for copy in self.second_copies:
            copy.wait_recv()
        total = self.second_in[0].astype(F32)
        for i in range(1, len(self.second_steps) + 1):
            total = total + self.second_in[i].astype(F32)
        own = self.full.at[chunk(self.half + self.own, self.size)]
        own[...] = total.astype(BF16)
        self.back_copies = self.far_first(self.first_steps, lambda k, step: self.launch(
            own, own, self.back_sems, self.first_peer(step), k,
        ))

    def back_to_core(self):
        for copy in self.back_copies:
            copy.wait_recv()
        rows = self.full.at[chunk(self.half, self.count * self.size)]
        self.last_copy = self.launch(rows, rows, self.last_sems, self.spot.other_core())

    def finish(self):
        self.last_copy.wait_recv()

    def drain(self):
        for copy in self.sent:
            copy.wait_send()


class PlaneSum(Sum):
    first_steps, second_steps = PLANE, RING

    def first_here(self):
        return self.spot.y * 4 + self.spot.x

    def first_index(self, step):
        y, x = self.spot.plane_spot(*step)
        return y * 4 + x

    def first_peer(self, step):
        return self.spot.plane_peer(*step)

    def second_here(self):
        return self.spot.z

    def second_peer(self, step):
        return self.spot.z_peer(step)


class RingSum(Sum):
    first_steps, second_steps = RING, PLANE

    def first_here(self):
        return self.spot.z

    def first_index(self, step):
        return ring(self.spot.z, step, 8)

    def first_peer(self, step):
        return self.spot.z_peer(step)

    def second_here(self):
        return self.spot.y * 4 + self.spot.x

    def second_peer(self, step):
        return self.spot.plane_peer(*step)


def sum_scratch(kind, size):
    first, second = len(kind.first_steps), len(kind.second_steps)
    sem = pltpu.SemaphoreType.DMA
    return [
        pltpu.VMEM(((first + 1) * size, 128), BF16),
        pltpu.VMEM(((first + 1) * size, 128), BF16),
        pltpu.VMEM((first, size, 128), BF16),
        pltpu.VMEM((second + 1, size, 128), BF16),
        sem((2,)), sem((first,)), sem((first,)), sem((second,)), sem((second,)),
        sem((first,)), sem((first,)), sem((2,)),
    ]


PARTS = ((PlaneSum, 48), (RingSum, 64), (PlaneSum, 32))


def block_kernel(
    x_hbm, ct_hbm, bias_hbm, ga_hbm, wqkv_hbm, wproj_hbm, gm_hbm, wup_hbm, wdown_hbm,
    out_grid, gx_grid, full0, full1, full2,
    x_in, ct_in, bias_in, ga_in, wqkv_in, wproj_in, gm_in, wup_in, wdown_in, load_sem,
    pack, pack_t, place, place_t,
    x_ref, ct_ref, out_ref, gx_ref, bias32, probs, weights, km_s, vm_s, q_s,
    normed_t, nm_t, mixed_t, ct_t, mixed_s, hid_s, hid_grad_s, nm_s, act_s, gpre_s, gqkv_s, gattn_s,
    packed, landed, halo_send, halo_recv, flat0, flat1, flat2, *sum_refs,
):
    spot = Place()
    barrier = pltpu.get_barrier_semaphore()
    devices = spot.everyone()
    for device in devices[:6]:
        pl.semaphore_signal(barrier, inc=1, device_id=device, device_id_type=MESH)
    loads = []
    for i, (src, dst) in enumerate((
        (x_hbm, x_in), (ct_hbm, ct_in), (bias_hbm, bias_in), (ga_hbm, ga_in), (wqkv_hbm, wqkv_in),
        (wproj_hbm, wproj_in), (gm_hbm, gm_in), (wup_hbm, wup_in), (wdown_hbm, wdown_in),
    )):
        loads.append(pltpu.make_async_copy(src, dst, load_sem.at[i]))
        loads[-1].start()
    for device in devices[6:]:
        pl.semaphore_signal(barrier, inc=1, device_id=device, device_id_type=MESH)
    halos = [
        Halo(spot, packed.at[a], landed.at[a], halo_send.at[a], halo_recv.at[a], step)
        for a, step in enumerate((-1, -1, 1, 1))
    ]
    x_halo, ct_halo, out_halo, gx_halo = halos
    sums = []
    for i, (kind, _) in enumerate(PARTS):
        flat, full = ((flat0, full0), (flat1, full1), (flat2, full2))[i]
        count = len(sum_refs) // len(PARTS)
        sums.append(kind(spot, flat, full, sum_refs[i * count:(i + 1) * count]))
    early, late = sums[:2], sums[2]

    pack[...] = table(pack_rows)
    loads[0].wait()
    x_halo.pack(x_in, pack)
    pl.semaphore_wait(barrier, len(devices))
    x_halo.start()
    pack_t[...] = table_t(pack_rows)
    flat1[5 * C:, :] = jnp.zeros((ROWS[1] - 5 * C, 128), BF16)
    flat2[5 * C:, :] = jnp.zeros((ROWS[2] - 5 * C, 128), BF16)
    place[...] = table(place_rows)
    place_t[...] = table_t(place_rows)
    loads[1].wait()
    ct_halo.pack(ct_in, pack)
    ct_halo.start()
    loads[2].wait()
    is_last = spot.lat == lax.axis_size("lat") - 1
    row_half = (lax.broadcasted_iota(jnp.int32, (WTOK, 1), 0) // WLON) % WLAT < WLAT // 2
    col_half = (lax.broadcasted_iota(jnp.int32, (1, WTOK), 1) // WLON) % WLAT < WLAT // 2
    cut = jnp.logical_and(row_half != col_half, is_last)
    penalty = jnp.where(cut, MASKED, 0.0)
    for h in range(HEADS):
        rows = slice(h * WTOK, (h + 1) * WTOK)
        bias32[rows, :] = bias_in[rows, :].astype(F32).T + penalty
    for load in loads[3:]:
        load.wait()
    x_halo.wait()
    x_halo.unpack(place_t, x_ref)

    scale = HEAD ** (-0.5)
    masks = head_masks()
    ga = ga_in[...]
    gm = gm_in[...]

    def forward():
        x = x_ref[...].astype(F32)
        unit, _ = normalize(x)
        normed = (unit * ga).astype(BF16)
        normed_t[...] = normed.T
        qkv = nn(normed, wqkv_in[...]).astype(BF16)
        q_s[...] = qkv[:, :C]
        k = qkv[:, C:2 * C]
        v = qkv[:, 2 * C:]
        for n in range(4):
            rows = slice(n * WTOK, (n + 1) * WTOK)
            km = jnp.concatenate([k[rows] * masks[h] for h in range(HEADS)], axis=0)
            vm = jnp.concatenate([v[rows] * masks[h] for h in range(HEADS)], axis=0)
            km_s[n] = km
            vm_s[n] = vm
            s = (nt(km, q_s[rows, :]) * scale + bias32[...]).reshape(HEADS, WTOK, WTOK)
            e = jnp.exp(s - jnp.max(s, axis=1, keepdims=True))
            p = e * (1.0 / jnp.sum(e, axis=1, keepdims=True))
            probs[n * HEADS:(n + 1) * HEADS] = p
            weights[n] = p.astype(BF16).reshape(HEADS * WTOK, WTOK)
            mixed_s[rows, :] = tn(weights[n], vm).astype(BF16)

    def mlp():
        hidden = (x_ref[...].astype(F32) + nn(mixed_s[...], wproj_in[...])).astype(BF16)
        hid_s[...] = hidden
        unit, inv = normalize(hidden.astype(F32))
        nm_s[...] = (unit * gm).astype(BF16)
        nm_t[...] = nm_s[...].T
        grad_nm = jnp.zeros((TOK, C), F32)
        for f in range(3):
            cols = slice(f * 256, (f + 1) * 256)
            z = nn(nm_s[...], wup_in[:, cols])
            phi = 0.5 * (1.0 + lax.erf(z * (0.5 ** 0.5)))
            act_s[:, cols] = (z * phi).astype(BF16)
            slope = phi + z * (jnp.exp(-0.5 * z * z) * 0.3989422804014327)
            gpre = (nn(ct_ref[...], wdown_in[:, cols]) * slope).astype(BF16)
            gpre_s[:, cols] = gpre
            grad_nm = grad_nm + nt(gpre, wup_in[:, cols])
        grad_hidden = (ct_ref[...].astype(F32) + norm_back(unit, inv, gm, grad_nm)).astype(BF16)
        hid_grad_s[...] = grad_hidden
        gattn_s[...] = nt(grad_hidden, wproj_in[...]).astype(BF16)

    def attention_back(n):
        rows = slice(n * WTOK, (n + 1) * WTOK)
        up = gattn_s[rows, :]
        p = probs[n * HEADS:(n + 1) * HEADS]
        gp = nt(vm_s[n], up).reshape(HEADS, WTOK, WTOK)
        inner = jnp.sum(p * gp, axis=1, keepdims=True)
        gs = (p * (gp - inner) * scale).astype(BF16).reshape(HEADS * WTOK, WTOK)
        gv_all = nn(weights[n], up)
        gk_all = nn(gs, q_s[rows, :])
        gq = tn(gs, km_s[n])
        gk = jnp.zeros((WTOK, C), F32)
        gv = jnp.zeros((WTOK, C), F32)
        for h in range(HEADS):
            gk = jnp.where(masks[h] > 0, gk_all[h * WTOK:(h + 1) * WTOK], gk)
            gv = jnp.where(masks[h] > 0, gv_all[h * WTOK:(h + 1) * WTOK], gv)
        gqkv_s[rows, :] = jnp.concatenate([gq, gk, gv], axis=1).astype(BF16)

    def output():
        out_ref[...] = (hid_s[...].astype(F32) + nt(act_s[...], wdown_in[...])).astype(BF16)

    def input_grad():
        grad_rolled = nt(gqkv_s[...], wqkv_in[...]).astype(BF16).astype(F32)
        unit, inv = normalize(x_ref[...].astype(F32))
        grad_x = norm_back(unit, inv, ga, grad_rolled)
        gx_ref[...] = (hid_grad_s[...].astype(F32) + grad_x).astype(BF16)

    def store_blocks(flat, base, values):
        for t in range(values.shape[1] // 128):
            flat[base + t * C:base + (t + 1) * C, :] = values[:, t * 128:(t + 1) * 128].astype(BF16)

    forward()
    mixed_t[...] = mixed_s[...].T
    ct_halo.wait()
    ct_halo.unpack(place_t, ct_ref)
    ct_t[...] = ct_ref[...].T
    mlp()
    grad_up = nn(nm_t[...], gpre_s[...])
    grad_proj = nn(mixed_t[...], hid_grad_s[...])
    store_blocks(flat1, 0, grad_up[:, :640])
    store_blocks(flat0, 0, nn(ct_t[...], act_s[...]))
    store_blocks(flat0, 6 * C, grad_proj)
    store_blocks(flat0, 7 * C, grad_up[:, 640:])
    for part in early:
        part.to_core()
    attention_back(0)
    attention_back(1)
    for part in early:
        part.to_first()
    attention_back(2)
    attention_back(3)
    grad_qkv = nn(normed_t[...], gqkv_s[...])
    store_blocks(flat2, 0, grad_qkv)
    store_blocks(flat2, 4 * C, jnp.concatenate([grad_qkv[:, 512:], grad_proj[:, 128:]], axis=1))
    late.to_core()
    late.to_first()
    output()
    out_halo.pack(out_ref, place)
    input_grad()
    gx_halo.pack(gx_ref, place)
    for part in sums:
        part.to_second()
    out_halo.start()
    gx_halo.start()
    for part in sums:
        part.back_to_first()
    out_halo.wait()
    out_halo.unpack(pack_t, out_grid)
    for part in sums:
        part.back_to_core()
    gx_halo.wait()
    gx_halo.unpack(pack_t, gx_grid)
    for part in sums:
        part.finish()
    for part in sums:
        part.drain()


def block_call(x, ct, bias, gain_attn, w_qkv, w_proj, gain_mlp, w_up, w_down):
    shape = jax.ShapeDtypeStruct
    args = (x, ct, bias, gain_attn, w_qkv, w_proj, gain_mlp, w_up, w_down)
    sem = pltpu.SemaphoreType.DMA
    return pl.pallas_call(
        block_kernel,
        out_shape=(
            shape((TOK, C), BF16),
            shape((TOK, C), BF16),
            *[shape((rows, 128), BF16) for rows in ROWS],
        ),
        in_specs=[HBM] * 9,
        out_specs=(VMEM,) * 5,
        scratch_shapes=[
            *[pltpu.VMEM(arg.shape, arg.dtype) for arg in args], sem((9,)),
            pltpu.VMEM((PACKED, PAIR), BF16),
            pltpu.VMEM((PAIR, PACKED), BF16),
            pltpu.VMEM((PACKED, PAIR), BF16),
            pltpu.VMEM((PAIR, PACKED), BF16),
            pltpu.VMEM((TOK, C), BF16),
            pltpu.VMEM((TOK, C), BF16),
            pltpu.VMEM((TOK, C), BF16),
            pltpu.VMEM((TOK, C), BF16),
            pltpu.VMEM((HEADS * WTOK, WTOK), F32),
            pltpu.VMEM((4 * HEADS, WTOK, WTOK), F32),
            pltpu.VMEM((4, HEADS * WTOK, WTOK), BF16),
            pltpu.VMEM((4, HEADS * WTOK, C), BF16),
            pltpu.VMEM((4, HEADS * WTOK, C), BF16),
            pltpu.VMEM((TOK, C), BF16),
            *[pltpu.VMEM((C, TOK), BF16)] * 4,
            pltpu.VMEM((TOK, C), BF16),
            pltpu.VMEM((TOK, C), BF16),
            pltpu.VMEM((TOK, C), BF16),
            pltpu.VMEM((TOK, C), BF16),
            pltpu.VMEM((TOK, FF), BF16),
            pltpu.VMEM((TOK, FF), BF16),
            pltpu.VMEM((TOK, 3 * C), BF16),
            pltpu.VMEM((TOK, C), BF16),
            pltpu.VMEM((4, PACKED, 2 * C), BF16),
            pltpu.VMEM((4, PACKED - STAY, 2 * C), BF16),
            sem((4, 3)), sem((4, 3)),
            *[pltpu.VMEM((rows, 128), BF16) for rows in ROWS],
            *[ref for kind, size in PARTS for ref in sum_scratch(kind, size)],
        ],
        compiler_params=pltpu.CompilerParams(
            collective_id=0, has_side_effects=True, vmem_limit_bytes=56 * 2**20
        ),
        name="block",
    )(*args)


def finish_kernel(
    out_in, gx_in, full0_hbm, full1_hbm, full2_hbm, wqkv_hbm, wup_hbm, gain_a_hbm, gain_m_hbm,
    out_hbm, gx_hbm, qkv_hbm, proj_hbm, up_hbm, down_hbm, ga_hbm, gm_hbm,
    full0, full1, full2, wqkv, wup, gain_a, gain_m,
    out_ref, gx_ref, qkv_ref, proj_ref, up_ref, down_ref, ga_ref, gm_ref, in_sem, out_sem,
):
    def read(i, src, dst):
        copy = pltpu.make_async_copy(src, dst, in_sem.at[i])
        copy.start()
        return copy

    written = []

    def write(i, src, dst):
        written.append(pltpu.make_async_copy(src, dst, out_sem.at[i]))
        written[-1].start()

    def block(full, t):
        return full[t * C:(t + 1) * C, :].astype(F32) * FACTOR

    copies = [
        read(i, src, dst) for i, (src, dst) in enumerate((
            (full0_hbm, full0), (full1_hbm, full1), (full2_hbm, full2), (out_in, out_ref),
            (gx_in, gx_ref), (wqkv_hbm, wqkv), (wup_hbm, wup), (gain_a_hbm, gain_a),
            (gain_m_hbm, gain_m),
        ))
    ]
    copies[0].wait()
    for t in range(6):
        down_ref[:, t * 128:(t + 1) * 128] = block(full0, t)
    write(0, down_ref, down_hbm)
    copies[1].wait()
    for t in range(6):
        up_ref[:, t * 128:(t + 1) * 128] = block(full1, t) if t < 5 else block(full0, 7)
    write(1, up_ref, up_hbm)
    copies[2].wait()
    for t in range(4):
        qkv_ref[:, t * 128:(t + 1) * 128] = block(full2, t)
    mixed_tile = block(full2, 4)
    qkv_ref[:, 512:] = mixed_tile[:, :64]
    write(2, qkv_ref, qkv_hbm)
    proj_ref[:, :128] = block(full0, 6)
    proj_ref[:, 128:] = mixed_tile[:, 64:]
    write(3, proj_ref, proj_hbm)
    copies[3].wait()
    write(4, out_ref, out_hbm)
    copies[4].wait()
    write(5, gx_ref, gx_hbm)
    for copy in copies[5:]:
        copy.wait()
    for weight, grad, gain, ref in ((wqkv, qkv_ref, gain_a, ga_ref), (wup, up_ref, gain_m, gm_ref)):
        product = weight[...].astype(F32) * grad[...]
        total = lax.dot_general(
            jnp.ones((8, product.shape[1]), F32), product, (((1,), (1,)), ((), ())),
            precision=lax.Precision.HIGHEST, preferred_element_type=F32,
        )
        ref[...] = total[:1] / gain[...]
    write(6, ga_ref, ga_hbm)
    write(7, gm_ref, gm_hbm)
    for copy in written:
        copy.wait()


def finish_call(out, gx, full, w_qkv, w_up, gain_attn, gain_mlp):
    shape = jax.ShapeDtypeStruct
    results = (
        shape((TOK, C), BF16),
        shape((TOK, C), BF16),
        shape((C, 3 * C), F32),
        shape((C, C), F32),
        shape((C, FF), F32),
        shape((C, FF), F32),
        shape((1, C), F32),
        shape((1, C), F32),
    )
    return pl.pallas_call(
        finish_kernel,
        out_shape=results,
        in_specs=[HBM] * 9,
        out_specs=(HBM,) * 8,
        scratch_shapes=[
            *[pltpu.VMEM((rows, 128), BF16) for rows in ROWS],
            pltpu.VMEM((C, 3 * C), BF16),
            pltpu.VMEM((C, FF), BF16),
            pltpu.VMEM((1, C), F32),
            pltpu.VMEM((1, C), F32),
            *[pltpu.VMEM(result.shape, result.dtype) for result in results],
            pltpu.SemaphoreType.DMA((9,)),
            pltpu.SemaphoreType.DMA((8,)),
        ],
        compiler_params=pltpu.CompilerParams(vmem_limit_bytes=56 * 2**20),
        name="finish",
    )(out, gx, *full, w_qkv, w_up, gain_attn, gain_mlp)


def body(fields, gain_attn, w_qkv, bias, w_proj, gain_mlp, w_up, w_down, cotangent):
    out, gx, *full = block_call(
        fields.reshape(TOK, C), cotangent.reshape(TOK, C), bias.reshape(HEADS * WTOK, WTOK),
        gain_attn.reshape(1, C), w_qkv, w_proj, gain_mlp.reshape(1, C), w_up, w_down.T,
    )
    out, gx, qkv, proj, up, down, ga, gm = finish_call(
        out, gx, full, w_qkv, w_up, gain_attn.reshape(1, C), gain_mlp.reshape(1, C),
    )
    return (
        out.reshape(fields.shape), gx.reshape(fields.shape), qkv, proj, up, down.T,
        ga.reshape(C), gm.reshape(C),
    )


def solution(mesh):
    grid = P(None, "lat", "lon", None)
    in_specs = (grid, P(), P(), P("lat", None, None, None), P(), P(), P(), P(), grid)
    out_specs = (grid, grid, P(), P(), P(), P(), P(), P())
    return jax.shard_map(body, mesh=mesh, in_specs=in_specs, out_specs=out_specs, check_vma=False)
```
